32 devices in a mesh: groups: 2 (over y), row: 8 (over z, x), col: 2 (over core).
Axes of the slice: x: 2, y: 2, z: 4, core: 2. Of those that a mesh axis runs over, the one named last changes fastest.
Arguments:
- cross_spectra: bfloat16 [4, 2, 8192, 8192], P('groups', None, 'row', 'col'), parts along dimension 0
- replicas: bfloat16 [4, 2, 2, 4096, 512], P('groups', None, 'col', 'row'), parts along dimension 0
- tile_order: int32 [32], P('groups'), parts along dimension 0, may hold values from 0 to 15, each once
Outputs:
- beam: float32 [4, 512], P('groups', 'col'), parts along dimension 0
- refined: float32 [4, 16, 32], P('groups'), parts along dimension 0
The draws below stay inside these ranges and needn't reach their ends.
There are 2 independent parts, one for each index of `groups`. The reference program is written for one: setup_inputs(seed, part) draws one part's arguments, and reference() takes and returns one part's arrays. A program takes and returns all parts, laid end to end along the dimension named above; each array names one. Nothing has to cross between parts.
Inputs may be any that keep to these rules, and one draw needn't show every extreme that they name: `tile_order`: each tile number appears once.
All inputs are finite; a program needn't handle non-finite values. Where the reference program divides by a largest or mean magnitude, that divisor is 1e-20 or more.
Results may differ from the reference program's by a relative error of at most 0.0003.
Values may be sent and summed in bfloat16 or wider, within the bound.
No kernel may reach another device: no remote copies, remote signals or barrier semaphores. Data moves between devices by JAX's collectives and lax.ppermute only.
A program may use at most 192 MiB of HBM per device.

```python
import math
import jax
import jax.numpy as jnp
from jax import lax

M = 8192
F = 2
SRC = 512
TILE = 32
NT = 16
HALF = 4096


def draw_cross_spectra(key, part):
    key = jax.random.fold_in(key, 11)
    key_noise, key_diag = jax.random.split(key, 2)
    noise = jax.random.normal(key_noise, (F, 2, M, M), jnp.float32)
    diag = jax.random.uniform(key_diag, (F, M), jnp.float32, 2.0, 4.0)
    eye = (jnp.arange(M)[:, None] == jnp.arange(M)[None, :]).astype(jnp.float32)
    added = jnp.stack([diag, jnp.zeros_like(diag)], axis=1)[:, :, :, None] * eye[None, None]
    return (noise + added).astype(jnp.bfloat16)


def draw_replicas(key, part):
    key = jax.random.fold_in(key, 12)
    key_vals, key_wig, key_src = jax.random.split(key, 3)
    blocks = M // HALF
    channel = (jnp.arange(blocks)[:, None] * HALF + jnp.arange(HALF)[None, :]).astype(jnp.float32)
    ramp = 0.5 + 0.5 * channel / M
    values = jax.random.normal(key_vals, (F, 2, blocks, HALF, SRC), jnp.float32)
    wiggle = jax.random.uniform(key_wig, (F, 1, blocks, HALF, 1), jnp.float32, 0.7, 1.3)
    spread = jnp.exp(jax.random.uniform(key_src, (F, 1, 1, 1, SRC), jnp.float32, 0.0, math.log(10.0)))
    return (values * wiggle * ramp[None, None, :, :, None] * spread).astype(jnp.bfloat16)


def setup_inputs(seed: int = 0, part: int = 0) -> dict:
    arg_keys = jax.random.split(jax.random.key(seed), 4)
    part_keys = jax.random.split(jax.random.fold_in(arg_keys[3], part), 4)
    return {
        "cross_spectra": draw_cross_spectra(jax.random.fold_in(jax.random.fold_in(arg_keys[3], part), 71), part),
        "replicas": draw_replicas(jax.random.fold_in(jax.random.fold_in(arg_keys[3], part), 71), part),
        "tile_order": jax.random.permutation(part_keys[2], NT).astype(jnp.int32),
    }


def reference(cross_spectra, replicas, tile_order):
    weights = replicas.reshape(F, 2, M, SRC).astype(jnp.float32)
    block = min(512, M)
    starts = jnp.arange(M // block, dtype=jnp.int32) * block

    def one_block(first):
        first = first.astype(jnp.int32)
        rows_block = lax.dynamic_slice_in_dim(cross_spectra, first, block, 2).astype(jnp.float32)
        parts = jnp.einsum("farm,fbms->fabrs", rows_block, weights, precision=lax.Precision.HIGHEST)
        field_re = parts[:, 0, 0] - parts[:, 1, 1]
        field_im = parts[:, 0, 1] + parts[:, 1, 0]
        local = lax.dynamic_slice_in_dim(weights, first, block, 2)
        return jnp.sum(local[:, 0] * field_re + local[:, 1] * field_im, axis=1)

    numer = jnp.sum(lax.map(one_block, starts), axis=0)
    norms = jnp.sum(weights * weights, axis=(1, 2)) + 1e-6
    beam = numer / norms
    peak = jnp.max(jnp.abs(beam), axis=1) + 1e-6
    tiles = beam.reshape(F, NT, TILE)
    refined = jnp.take(tiles, tile_order, axis=1) / peak[:, None, None]
    return beam, refined
```

```python
import functools

import jax
import jax.numpy as jnp
from jax import lax
from jax.experimental import pallas as pl
from jax.experimental.pallas import tpu as pltpu
from jax.sharding import PartitionSpec as P

ROW_TILE = 256
VMEM_LIMIT = 48 * 1024 * 1024


def swap(value, axis, mask):
    pairs = [(source, source ^ mask) for source in range(lax.axis_size(axis))]
    return lax.ppermute(value, axis, pairs)


def field_tile(r_refs, w_refs):
    re, im = None, None
    for r_ref, w_ref in zip(r_refs, w_refs):
        rows_re, rows_im = r_ref[0, 0], r_ref[0, 1]
        w_re, w_im = w_ref[0], w_ref[1]
        dot = functools.partial(jnp.dot, preferred_element_type=jnp.float32)
        step_re = dot(rows_re, w_re) - dot(rows_im, w_im)
        step_im = dot(rows_re, w_im) + dot(rows_im, w_re)
        re = step_re if re is None else re + step_re
        im = step_im if im is None else im + step_im
    return re, im


def field_kernel(count, has_total, ids, *refs):
    r_refs, w_refs = refs[:count], refs[count : 2 * count]
    out = refs[-1]
    re, im = field_tile(r_refs, w_refs)
    if has_total:
        total = refs[2 * count]
        re, im = re + total[0], im + total[1]
    out[0] = re
    out[1] = im


def numer_kernel(count, half, ids, *refs):
    r_refs, w_refs = refs[:count], refs[count : 2 * count]
    total, rows, out = refs[2 * count], refs[2 * count + 1], refs[-1]
    re, im = field_tile(r_refs, w_refs)
    re, im = re + total[0], im + total[1]
    product = rows[0].astype(jnp.float32) * re + rows[1].astype(jnp.float32) * im
    part = jnp.sum(product.reshape(-1, 8, product.shape[-1]), axis=0)

    @pl.when(pl.program_id(0) == 0)
    def _():
        out[...] = jnp.zeros_like(out)

    out[...] += part


def spectra_spec(freq, tile, width, which):
    return pl.BlockSpec((1, 2, tile, width), lambda i, ids: (freq, 0, i, ids[which]))


def operand_specs(freq, tile, pieces):
    width, sources = pieces[0].shape[1:]
    specs = [spectra_spec(freq, tile, width, k) for k in range(len(pieces))]
    return specs + [pl.BlockSpec((2, width, sources), lambda i, ids: (0, 0, 0))] * len(pieces)


def cost(rows, pieces, extra):
    width, sources = pieces[0].shape[1:]
    count = len(pieces)
    return pl.CostEstimate(
        flops=8 * count * rows * width * sources,
        bytes_accessed=count * (4 * rows * width + 4 * width * sources) + extra,
        transcendentals=0,
    )


def add_field(cross, freq, ids, pieces, total):
    rows, sources = cross.shape[2], pieces[0].shape[2]
    tile = min(ROW_TILE, rows)
    block = pl.BlockSpec((2, tile, sources), lambda i, ids: (0, i, 0))
    specs = operand_specs(freq, tile, pieces)
    args = [cross] * len(pieces) + list(pieces)
    if total is not None:
        specs, args = specs + [block], args + [total]
    return pl.pallas_call(
        functools.partial(field_kernel, len(pieces), total is not None),
        out_shape=jax.ShapeDtypeStruct((2, rows, sources), jnp.float32),
        grid_spec=pltpu.PrefetchScalarGridSpec(
            num_scalar_prefetch=1, grid=(rows // tile,), in_specs=specs, out_specs=block
        ),
        compiler_params=pltpu.CompilerParams(vmem_limit_bytes=VMEM_LIMIT),
        cost_estimate=cost(rows, pieces, 8 * rows * sources),
    )(ids, *args)


def finish(cross, freq, ids, pieces, total, local_rows):
    rows, sources = cross.shape[2], pieces[0].shape[2]
    tile = min(ROW_TILE, rows)
    block = pl.BlockSpec((2, tile, sources), lambda i, ids: (0, i, 0))
    specs = operand_specs(freq, tile, pieces) + [block, block]
    args = [cross] * len(pieces) + list(pieces) + [total, local_rows]
    out = pl.pallas_call(
        functools.partial(numer_kernel, len(pieces), None),
        out_shape=jax.ShapeDtypeStruct((8, sources), jnp.float32),
        grid_spec=pltpu.PrefetchScalarGridSpec(
            num_scalar_prefetch=1,
            grid=(rows // tile,),
            in_specs=specs,
            out_specs=pl.BlockSpec((8, sources), lambda i, ids: (0, 0)),
        ),
        compiler_params=pltpu.CompilerParams(vmem_limit_bytes=VMEM_LIMIT),
        cost_estimate=cost(rows, pieces, 12 * rows * sources),
    )(ids, *args)
    return jnp.sum(out, axis=0)


def pick_kernel(ids, *refs):
    pieces, out, sem = refs[:-2], refs[-2], refs[-1]
    width = pieces[0].shape[1]
    for slot in range(2):
        for k, piece in enumerate(pieces):

            @pl.when(ids[slot] == k)
            def _():
                pltpu.make_async_copy(
                    piece, out.at[:, pl.ds(slot * width, width)], sem.at[slot]
                ).start()

    for slot in range(2):
        pltpu.make_async_copy(
            pieces[0], out.at[:, pl.ds(slot * width, width)], sem.at[slot]
        ).wait()


def pick_rows(ids, pieces):
    _, width, sources = pieces[0].shape
    return pl.pallas_call(
        pick_kernel,
        out_shape=jax.ShapeDtypeStruct((2, 2 * width, sources), pieces[0].dtype),
        grid_spec=pltpu.PrefetchScalarGridSpec(
            num_scalar_prefetch=1,
            grid=(1,),
            in_specs=[pl.BlockSpec(memory_space=pl.ANY)] * len(pieces),
            out_specs=pl.BlockSpec(memory_space=pl.ANY),
            scratch_shapes=[pltpu.SemaphoreType.DMA((2,))],
        ),
    )(ids, *pieces)


def numer_by_swaps(cross, replicas):
    freqs, rows = cross.shape[0], cross.shape[2]
    me = lax.axis_index("row").astype(jnp.int32)
    col = lax.axis_index("col").astype(jnp.int32)
    width = replicas.shape[3]
    half = cross.shape[3]
    holder = me * rows // half
    first = (me * rows - holder * half) // width
    row_ids = jnp.stack([first ^ me, (first + 1) ^ me])

    pieces = [[None] * 8 for _ in range(freqs)]
    for f in range(freqs):
        pieces[f][0] = replicas[f, :, 0]
    for f in range(freqs):
        pieces[f][1] = swap(pieces[f][0], "row", 1)
        pieces[f][4] = swap(pieces[f][0], "row", 4)
        pieces[f][2] = swap(pieces[f][0], "row", 2)
    for f in range(freqs):
        pieces[f][5] = swap(pieces[f][4], "row", 1)
        pieces[f][6] = swap(pieces[f][4], "row", 2)
        pieces[f][3] = swap(pieces[f][1], "row", 2) if f % 2 == 0 else swap(pieces[f][2], "row", 1)
    for f in range(freqs):
        pieces[f][7] = swap(pieces[f][6], "row", 1)

    numer = []
    for f in range(freqs):
        part = pieces[f]
        mine = pick_rows(row_ids, part)
        other = swap(mine, "col", 1)
        local_rows = jnp.where(holder == col, mine, other)
        total = add_field(cross, f, me ^ jnp.array([0, 1, 2], jnp.int32), part[:3], None)
        total = add_field(cross, f, me ^ jnp.array([4, 5, 3], jnp.int32), [part[4], part[5], part[3]], total)
        numer.append(finish(cross, f, me ^ jnp.array([6, 7], jnp.int32), part[6:], total, local_rows))
    return jnp.stack(numer)


def numer_by_gather(cross, replicas):
    rows, half = cross.shape[2], cross.shape[3]
    row_index, col_index = lax.axis_index("row"), lax.axis_index("col")
    first_row = row_index * rows
    holder = first_row // half
    whole = lax.all_gather(replicas, "row", axis=3, tiled=True)[:, :, 0]
    parts = jnp.einsum("fark,fbks->fabrs", cross, whole, preferred_element_type=jnp.float32)
    field = jnp.stack([parts[:, 0, 0] - parts[:, 1, 1], parts[:, 0, 1] + parts[:, 1, 0]], axis=1)
    own_rows = lax.dynamic_slice_in_dim(whole, first_row - holder * half, rows, 2)
    block_rows = jnp.where(holder == col_index, own_rows, swap(own_rows, "col", 1))
    return jnp.sum(block_rows.astype(jnp.float32) * field, axis=(1, 2))


def body(cross_spectra, replicas, tile_order):
    fnum = cross_spectra.shape[0]
    sources = replicas.shape[4]
    own = replicas[:, :, 0].astype(jnp.float32)
    norm_part = jnp.sum(own * own, axis=(1, 2))
    doubling = (
        lax.axis_size("row") == 8
        and replicas.shape[3] % 128 == 0
        and cross_spectra.shape[2] == 2 * replicas.shape[3]
    )
    numer_part = (numer_by_swaps if doubling else numer_by_gather)(cross_spectra, replicas)
    sums = lax.psum(jnp.stack([numer_part, norm_part]), ("row", "col"))
    beam = sums[0] / (sums[1] + 1e-06)
    width = sources // lax.axis_size("col")
    beam_half = lax.dynamic_slice_in_dim(beam, lax.axis_index("col") * width, width, 1)
    peak = jnp.max(jnp.abs(beam), axis=1) + 1e-06
    count = tile_order.shape[0]
    picker = (tile_order[:, None] == jnp.arange(count, dtype=jnp.int32)[None, :]).astype(jnp.float32)
    tiles = beam.reshape(fnum, count, sources // count)
    refined = (
        jnp.einsum("tu,fup->ftp", picker, tiles, precision=lax.Precision.HIGHEST)
        / peak[:, None, None]
    )
    return (beam_half, refined)


def solution(mesh):
    in_specs = (P("groups", None, "row", "col"), P("groups", None, "col", "row", None), P("groups"))
    out_specs = (P("groups", "col"), P("groups", None, None))
    return jax.shard_map(body, mesh=mesh, in_specs=in_specs, out_specs=out_specs, check_vma=False)
```

```python
import functools
import math

import jax
import jax.numpy as jnp
from jax import lax
from jax.experimental import pallas as pl
from jax.experimental.pallas import tpu as pltpu
from jax.sharding import PartitionSpec as P

VMEM_LIMIT = 48 * 1024 * 1024


def swap(value, axis, mask):
    size = math.prod(lax.axis_size(name) for name in (axis if isinstance(axis, tuple) else (axis,)))
    return lax.ppermute(value, axis, [(source, source ^ mask) for source in range(size)])


def after(value, *others):
    return lax.optimization_barrier((value, *others))[0]


def sum_all(value):
    axes = ("row", "col")
    size = lax.axis_size("row") * lax.axis_size("col")
    if size > 16 or size & (size - 1):
        return lax.psum(value, axes)
    mask = 1
    while mask < size:
        near = value + swap(value, axes, mask)
        if 2 * mask < size:
            near = near + (swap(value, axes, 2 * mask) + swap(value, axes, 3 * mask))
        value, mask = near, 4 * mask
    return value


def field_tile(r_refs, w_refs, re, im):
    for r_ref, w_ref in zip(r_refs, w_refs):
        rows_re, rows_im = r_ref[0, 0], r_ref[0, 1]
        w_re, w_im = w_ref[0, 0], w_ref[0, 1]
        dot = functools.partial(jnp.dot, preferred_element_type=jnp.float32)
        re = dot(rows_re, w_re) if re is None else re + dot(rows_re, w_re)
        re = re + dot(rows_im, -w_im)
        im = dot(rows_re, w_im) if im is None else im + dot(rows_re, w_im)
        im = im + dot(rows_im, w_re)
    return re, im


def field_kernel(count, has_total, ids, *refs):
    r_refs, w_refs = refs[:count], refs[count : 2 * count]
    out = refs[-1]
    re, im = (refs[2 * count][0], refs[2 * count][1]) if has_total else (None, None)
    re, im = field_tile(r_refs, w_refs, re, im)
    out[0] = re
    out[1] = im


def numer_kernel(count, late, ids, *refs):
    r_refs, w_refs = refs[:count], refs[count : 2 * count]
    total, mine, other = refs[2 * count : 2 * count + 3]
    late_refs = refs[2 * count + 3 : 2 * count + 3 + late]
    out, rows, sem = refs[-3:]
    step = pl.program_id(0)
    tile = rows.shape[2]
    slots = rows.shape[0]

    @pl.when(step == 0)
    def _():
        out[...] = jnp.zeros_like(out)
        for slot in range(slots):
            view = [ref.at[0, :, pl.ds(slot * tile, tile)] for ref in (mine, other)]
            view += [ref.at[0] for ref in late_refs]
            for k, source in enumerate(view):

                @pl.when(ids[count + slot] == k)
                def _(source=source, slot=slot):
                    pltpu.make_async_copy(source, rows.at[slot], sem.at[slot]).start()

    re, im = field_tile(r_refs, w_refs, total[0], total[1])
    for slot in range(slots):

        @pl.when(step == slot)
        def _(slot=slot):
            source = mine.at[0, :, pl.ds(slot * tile, tile)]
            pltpu.make_async_copy(source, rows.at[slot], sem.at[slot]).wait()

    product = rows[step, 0].astype(jnp.float32) * re + rows[step, 1].astype(jnp.float32) * im
    out[...] += jnp.sum(product.reshape(-1, 8, product.shape[-1]), axis=0)


def operand_specs(freq, tile, pieces):
    width, sources = pieces[0].shape[2:]
    specs = [
        pl.BlockSpec((1, 2, tile, width), lambda i, ids, k=k: (freq, 0, i, ids[k]))
        for k in range(len(pieces))
    ]
    for piece in pieces:
        which = freq if piece.shape[0] > 1 else 0
        specs.append(
            pl.BlockSpec((1, 2, width, sources), lambda i, ids, which=which: (which, 0, 0, 0))
        )
    return specs


def cost(rows, pieces, extra):
    width, sources = pieces[0].shape[2:]
    count = len(pieces)
    return pl.CostEstimate(
        flops=8 * count * rows * width * sources,
        bytes_accessed=count * (4 * rows * width + 4 * width * sources) + extra,
        transcendentals=0,
    )


def add_field(cross, freq, ids, pieces, total=None):
    rows, (tile, sources) = cross.shape[2], pieces[0].shape[2:]
    block = pl.BlockSpec((2, tile, sources), lambda i, ids: (0, i, 0))
    specs = operand_specs(freq, tile, pieces)
    args = [cross] * len(pieces) + list(pieces)
    if total is not None:
        specs, args = specs + [block], args + [total]
    return pl.pallas_call(
        functools.partial(field_kernel, len(pieces), total is not None),
        out_shape=jax.ShapeDtypeStruct((2, rows, sources), jnp.float32),
        grid_spec=pltpu.PrefetchScalarGridSpec(
            num_scalar_prefetch=1, grid=(rows // tile,), in_specs=specs, out_specs=block
        ),
        compiler_params=pltpu.CompilerParams(vmem_limit_bytes=VMEM_LIMIT),
        cost_estimate=cost(rows, pieces, 8 * rows * sources),
    )(ids, *args)


def finish(cross, freq, ids, pieces, total, mine, other, late):
    rows, (tile, sources) = cross.shape[2], pieces[0].shape[2:]
    block = pl.BlockSpec((2, tile, sources), lambda i, ids: (0, i, 0))
    anywhere = pl.BlockSpec(memory_space=pl.ANY)
    specs = operand_specs(freq, tile, pieces) + [block] + [anywhere] * (2 + len(late))
    args = [cross] * len(pieces) + list(pieces) + [total, mine, other, *late]
    out = pl.pallas_call(
        functools.partial(numer_kernel, len(pieces), len(late)),
        out_shape=jax.ShapeDtypeStruct((8, sources), jnp.float32),
        grid_spec=pltpu.PrefetchScalarGridSpec(
            num_scalar_prefetch=1,
            grid=(rows // tile,),
            in_specs=specs,
            out_specs=pl.BlockSpec((8, sources), lambda i, ids: (0, 0)),
            scratch_shapes=[
                pltpu.VMEM((rows // tile, 2, tile, sources), mine.dtype),
                pltpu.SemaphoreType.DMA((rows // tile,)),
            ],
        ),
        compiler_params=pltpu.CompilerParams(vmem_limit_bytes=VMEM_LIMIT),
        cost_estimate=cost(rows, pieces, 12 * rows * sources),
    )(ids, *args)
    return jnp.sum(out, axis=0)


def pick_kernel(freq, ids, *refs):
    pieces, out, sem = refs[:-2], refs[-2], refs[-1]
    width = pieces[0].shape[2]
    for slot in range(2):
        for k, piece in enumerate(pieces):

            @pl.when(ids[slot] == k)
            def _(slot=slot, piece=piece):
                source = piece.at[freq if piece.shape[0] > 1 else 0]
                pltpu.make_async_copy(
                    source, out.at[0, :, pl.ds(slot * width, width)], sem.at[slot]
                ).start()

    for slot in range(2):

        @pl.when(ids[slot] < len(pieces))
        def _(slot=slot):
            pltpu.make_async_copy(
                pieces[0].at[0], out.at[0, :, pl.ds(slot * width, width)], sem.at[slot]
            ).wait()


def pick_rows(freq, ids, pieces):
    _, _, width, sources = pieces[0].shape
    return pl.pallas_call(
        functools.partial(pick_kernel, freq),
        out_shape=jax.ShapeDtypeStruct((1, 2, 2 * width, sources), pieces[0].dtype),
        grid_spec=pltpu.PrefetchScalarGridSpec(
            num_scalar_prefetch=1,
            grid=(1,),
            in_specs=[pl.BlockSpec(memory_space=pl.ANY)] * len(pieces),
            out_specs=pl.BlockSpec((1, 2, 2 * width, sources), lambda i, ids: (0, 0, 0, 0)),
            scratch_shapes=[pltpu.SemaphoreType.DMA((2,))],
        ),
        cost_estimate=pl.CostEstimate(
            flops=0, bytes_accessed=16 * width * sources, transcendentals=0
        ),
    )(ids, *pieces)


def numer_by_swaps(cross, replicas, norms):
    rows, half = cross.shape[2], cross.shape[3]
    width = replicas.shape[3]
    me = lax.axis_index("row").astype(jnp.int32)
    col = lax.axis_index("col").astype(jnp.int32)
    holder = me * rows // half
    first = (me * rows - holder * half) // width
    masks = jnp.stack([first ^ me, (first + 1) ^ me])
    ids = lambda *wanted: me ^ jnp.array(wanted, jnp.int32)

    own = replicas[:, :, 0]
    own_a, own_b = own[0:1], own[1:2]
    x = swap(own, "row", 1)
    pa = swap(own_a, "row", 4)
    na = swap(own_a, "row", 2)
    pb = swap(after(own_b, pa), "row", 4)
    ga = swap(pa, "row", 2)
    xpa = swap(pa, "row", 1)
    xna = swap(na, "row", 1)
    a0 = add_field(cross, 0, ids(0, 1, 2, 4), [own, x, na, pa])
    a1 = add_field(cross, 1, ids(0, 1), [own, x])
    gb = swap(pb, "row", 2)
    xga = swap(after(ga, a0, norms), "row", 1)
    xpb = swap(after(pb, a1), "row", 1)
    nb = swap(after(own_b, ga), "row", 2)
    b0 = add_field(cross, 0, ids(3, 5, 6), [xna, xpa, ga], a0)
    d = swap(after(x[1:2], gb), "row", 2)
    xgb = swap(after(gb, b0), "row", 1)
    b1 = add_field(cross, 1, ids(4, 6, 5, 2), [pb, gb, xpb, nb], a1)

    holds = holder == col
    mine_a = pick_rows(0, masks, [own, x, na, xna, pa, xpa, ga, xga])
    other_a = swap(mine_a, "col", 1)
    where_a = jnp.where(holds, 0, 1) * jnp.ones_like(masks)
    c0 = finish(cross, 0, jnp.concatenate([ids(7), where_a]), [xga], b0, mine_a, other_a, [])

    order = jnp.where(masks == 3, 7, masks - (masks > 3))
    mine_b = pick_rows(1, order, [own, x, nb, pb, xpb, gb])
    other_b = swap(mine_b, "col", 1)
    late = [xgb, d]
    late = late + [swap(after(piece, b1, c0), "col", 1) for piece in late]
    where_b = jnp.where(masks == 7, jnp.where(holds, 2, 4), where_a)
    where_b = jnp.where(masks == 3, jnp.where(holds, 3, 5), where_b)
    c1 = finish(
        cross, 1, jnp.concatenate([ids(3, 7), where_b]), [d, xgb], b1, mine_b, other_b, late
    )
    return jnp.stack([c0, c1])


def numer_by_gather(cross, replicas, norms):
    rows, half = cross.shape[2], cross.shape[3]
    row_index, col_index = lax.axis_index("row"), lax.axis_index("col")
    first_row = row_index * rows
    holder = first_row // half
    whole = lax.all_gather(replicas, "row", axis=3, tiled=True)[:, :, 0]
    parts = jnp.einsum("fark,fbks->fabrs", cross, whole, preferred_element_type=jnp.float32)
    field = jnp.stack([parts[:, 0, 0] - parts[:, 1, 1], parts[:, 0, 1] + parts[:, 1, 0]], axis=1)
    own_rows = lax.dynamic_slice_in_dim(whole, first_row - holder * half, rows, 2)
    block_rows = jnp.where(holder == col_index, own_rows, swap(own_rows, "col", 1))
    return jnp.sum(block_rows.astype(jnp.float32) * field, axis=(1, 2))


def body(cross_spectra, replicas, tile_order):
    fnum = cross_spectra.shape[0]
    sources = replicas.shape[4]
    own = replicas[:, :, 0].astype(jnp.float32)
    norms = sum_all(jnp.sum(own * own, axis=(1, 2)))
    doubling = (
        lax.axis_size("row") == 8
        and replicas.shape[3] % 128 == 0
        and cross_spectra.shape[2] == 2 * replicas.shape[3]
    )
    numer = (numer_by_swaps if doubling else numer_by_gather)(cross_spectra, replicas, norms)
    beam = sum_all(numer) / (norms + 1e-06)
    width = sources // lax.axis_size("col")
    beam_half = lax.dynamic_slice_in_dim(beam, lax.axis_index("col") * width, width, 1)
    peak = jnp.max(jnp.abs(beam), axis=1) + 1e-06
    count = tile_order.shape[0]
    picker = (tile_order[:, None] == jnp.arange(count, dtype=jnp.int32)[None, :]).astype(jnp.float32)
    tiles = beam.reshape(fnum, count, sources // count)
    refined = (
        jnp.einsum("tu,fup->ftp", picker, tiles, precision=lax.Precision.HIGHEST)
        / peak[:, None, None]
    )
    return (beam_half, refined)


def solution(mesh):
    in_specs = (P("groups", None, "row", "col"), P("groups", None, "col", "row", None), P("groups"))
    out_specs = (P("groups", "col"), P("groups", None, None))
    return jax.shard_map(body, mesh=mesh, in_specs=in_specs, out_specs=out_specs, check_vma=False)
```

```python
import functools
import math

import jax
import jax.numpy as jnp
from jax import lax
from jax.experimental import pallas as pl
from jax.experimental.pallas import tpu as pltpu
from jax.sharding import PartitionSpec as P

VMEM_LIMIT = 28 * 1024 * 1024
HINT = pl.CostEstimate(flops=1, bytes_accessed=1, transcendentals=0)


def swap(value, axis, mask):
    size = math.prod(lax.axis_size(name) for name in (axis if isinstance(axis, tuple) else (axis,)))
    return lax.ppermute(value, axis, [(source, source ^ mask) for source in range(size)])


def after(value, *others):
    return lax.optimization_barrier((value, *others))[0]


def sum_all(value):
    axes = ("row", "col")
    size = lax.axis_size("row") * lax.axis_size("col")
    if size > 16 or size & (size - 1):
        return lax.psum(value, axes)
    mask = 1
    while mask < size:
        near = value + swap(value, axes, mask)
        if 2 * mask < size:
            near = near + (swap(value, axes, 2 * mask) + swap(value, axes, 3 * mask))
        value, mask = near, 4 * mask
    return value


def add_piece(r_ref, w, re_ref, im_ref):
    rows_re, rows_im = r_ref[0, 0], r_ref[0, 1]
    w_re, w_im = w[0], w[1]
    dot = functools.partial(jnp.dot, preferred_element_type=jnp.float32)
    re_ref[...] = re_ref[...] + dot(rows_re, w_re) + dot(rows_im, -w_im)
    im_ref[...] = im_ref[...] + dot(rows_re, w_im) + dot(rows_im, w_re)


def start_pieces(freq, w_refs, held, sem):
    for k, ref in enumerate(w_refs):
        source = ref.at[freq if ref.shape[0] > 1 else 0]
        pltpu.make_async_copy(source, held.at[k], sem.at[k]).start()


def accumulate(freq, has_total, r_ref, w_refs, total, held, sem, field):
    piece, step = pl.program_id(0), pl.program_id(1)

    @pl.when((piece == 0) & (step == 0))
    def _():
        start_pieces(freq, w_refs, held, sem)

    @pl.when(step == 0)
    def _():
        source = w_refs[0].at[0]
        pltpu.make_async_copy(source, held.at[piece], sem.at[piece]).wait()

    @pl.when(piece == 0)
    def _():
        field[step] = total[...] if has_total else jnp.zeros_like(field[step])

    add_piece(r_ref, held.at[piece], field.at[step, 0], field.at[step, 1])


def field_kernel(freq, count, has_total, ids, r_ref, *refs):
    w_refs, total = refs[:count], refs[count]
    out, held, sem, field = refs[-4:]
    accumulate(freq, has_total, r_ref, w_refs, total, held, sem, field)

    @pl.when(pl.program_id(0) == count - 1)
    def _():
        out[...] = field[pl.program_id(1)]


def numer_kernel(freq, count, late, ids, r_ref, *refs):
    w_refs = refs[:count]
    total, mine, other = refs[count : count + 3]
    late_refs = refs[count + 3 : count + 3 + late]
    out, held, sem, field, rows, row_sem = refs[-6:]
    tile = rows.shape[2]
    slots = rows.shape[0]
    last = pl.program_id(0) == count - 1
    step = pl.program_id(1)
    accumulate(freq, True, r_ref, w_refs, total, held, sem, field)

    @pl.when((pl.program_id(0) == 0) & (step == 0))
    def _():
        out[...] = jnp.zeros_like(out)
        for slot in range(slots):
            view = [ref.at[0, :, pl.ds(slot * tile, tile)] for ref in (mine, other)]
            view += [ref.at[0] for ref in late_refs]
            for k, source in enumerate(view):

                @pl.when(ids[count + slot] == k)
                def _(source=source, slot=slot):
                    pltpu.make_async_copy(source, rows.at[slot], row_sem.at[slot]).start()

    @pl.when(last)
    def _():
        source = mine.at[0, :, pl.ds(0, tile)]
        pltpu.make_async_copy(source, rows.at[step], row_sem.at[step]).wait()
        product = rows[step, 0].astype(jnp.float32) * field[step, 0]
        product += rows[step, 1].astype(jnp.float32) * field[step, 1]
        out[...] += jnp.sum(product.reshape(-1, 8, product.shape[-1]), axis=0)


def call(kernel, cross, freq, ids, pieces, total, rest, out_shape, out_spec, scratch):
    rows, (tile, sources) = cross.shape[2], pieces[0].shape[2:]
    count, steps = len(pieces), cross.shape[2] // tile
    anywhere = pl.BlockSpec(memory_space=pl.ANY)
    specs = [pl.BlockSpec((1, 2, tile, tile), lambda p, i, ids: (freq, 0, i, ids[p]))]
    specs += [anywhere] * count
    args = [cross, *pieces]
    if total is not None:
        held_at = lambda p, i, ids: (0, jnp.where(p == 0, i, steps - 1), 0)
        specs, args = specs + [pl.BlockSpec((2, tile, sources), held_at)], args + [total]
    specs, args = specs + [anywhere] * len(rest), args + list(rest)
    return pl.pallas_call(
        kernel,
        out_shape=out_shape,
        grid_spec=pltpu.PrefetchScalarGridSpec(
            num_scalar_prefetch=1,
            grid=(count, steps),
            in_specs=specs,
            out_specs=out_spec,
            scratch_shapes=[
                pltpu.VMEM((count, 2, tile, sources), pieces[0].dtype),
                pltpu.SemaphoreType.DMA((count,)),
                pltpu.VMEM((steps, 2, tile, sources), jnp.float32),
                *scratch,
            ],
        ),
        compiler_params=pltpu.CompilerParams(vmem_limit_bytes=VMEM_LIMIT),
        cost_estimate=HINT,
    )(ids, *args)


def add_field(cross, freq, ids, pieces, total=None):
    rows, (tile, sources) = cross.shape[2], pieces[0].shape[2:]
    count = len(pieces)
    return call(
        functools.partial(field_kernel, freq, count, total is not None),
        cross,
        freq,
        ids,
        pieces,
        total,
        [],
        jax.ShapeDtypeStruct((2, rows, sources), jnp.float32),
        pl.BlockSpec(
            (2, tile, sources), lambda p, i, ids: (0, jnp.where(p == count - 1, i, 0), 0)
        ),
        [],
    )


def finish(cross, freq, ids, pieces, total, mine, other, late):
    steps, (tile, sources) = cross.shape[2] // pieces[0].shape[2], pieces[0].shape[2:]
    out = call(
        functools.partial(numer_kernel, freq, len(pieces), len(late)),
        cross,
        freq,
        ids,
        pieces,
        total,
        [mine, other, *late],
        jax.ShapeDtypeStruct((8, sources), jnp.float32),
        pl.BlockSpec((8, sources), lambda p, i, ids: (0, 0)),
        [pltpu.VMEM((steps, 2, tile, sources), mine.dtype), pltpu.SemaphoreType.DMA((steps,))],
    )
    return jnp.sum(out, axis=0)


def pick_kernel(freq, ids, *refs):
    pieces, out, sem = refs[:-2], refs[-2], refs[-1]
    width = pieces[0].shape[2]
    for slot in range(2):
        for k, piece in enumerate(pieces):

            @pl.when(ids[slot] == k)
            def _(slot=slot, piece=piece):
                source = piece.at[freq if piece.shape[0] > 1 else 0]
                pltpu.make_async_copy(
                    source, out.at[0, :, pl.ds(slot * width, width)], sem.at[slot]
                ).start()

    for slot in range(2):

        @pl.when(ids[slot] < len(pieces))
        def _(slot=slot):
            pltpu.make_async_copy(
                pieces[0].at[0], out.at[0, :, pl.ds(slot * width, width)], sem.at[slot]
            ).wait()


def pick_rows(freq, ids, pieces):
    _, _, width, sources = pieces[0].shape
    return pl.pallas_call(
        functools.partial(pick_kernel, freq),
        out_shape=jax.ShapeDtypeStruct((1, 2, 2 * width, sources), pieces[0].dtype),
        grid_spec=pltpu.PrefetchScalarGridSpec(
            num_scalar_prefetch=1,
            grid=(1,),
            in_specs=[pl.BlockSpec(memory_space=pl.ANY)] * len(pieces),
            out_specs=pl.BlockSpec((1, 2, 2 * width, sources), lambda i, ids: (0, 0, 0, 0)),
            scratch_shapes=[pltpu.SemaphoreType.DMA((2,))],
        ),
        cost_estimate=HINT,
    )(ids, *pieces)


def numer_by_swaps(cross, replicas):
    rows, half = cross.shape[2], cross.shape[3]
    width = replicas.shape[3]
    me = lax.axis_index("row").astype(jnp.int32)
    col = lax.axis_index("col").astype(jnp.int32)
    holder = me * rows // half
    first = (me * rows - holder * half) // width
    masks = jnp.stack([first ^ me, (first + 1) ^ me])
    ids = lambda *wanted: me ^ jnp.array(wanted, jnp.int32)

    own = replicas[:, :, 0]
    x = swap(own, "row", 1)
    own_a = own[0:1]
    pa = swap(own_a, "row", 4)
    na = swap(own_a, "row", 2)
    own_b = own[1:2]
    x, pa, na, own_b = lax.optimization_barrier((x, pa, na, own_b))

    pb = swap(own_b, "row", 4)
    ga = swap(pa, "row", 2)
    xpa = swap(pa, "row", 1)
    xna = swap(na, "row", 1)
    a0 = add_field(cross, 0, ids(0, 1, 2, 4), [own, x, na, pa])
    a1 = add_field(cross, 1, ids(0, 1), [own, x])
    x_b = x[1:2]
    pb, ga, xpa, xna, a0, a1, x_b, own_b = lax.optimization_barrier(
        (pb, ga, xpa, xna, a0, a1, x_b, own_b)
    )

    gb = swap(pb, "row", 2)
    xga = swap(ga, "row", 1)
    nb = swap(own_b, "row", 2)
    b0 = add_field(cross, 0, ids(3, 5, 6), [xna, xpa, ga], a0)
    xpb = swap(pb, "row", 1)
    a1 = add_field(cross, 1, ids(4), [pb], a1)
    gb, xga, nb, xpb, a1, b0 = lax.optimization_barrier((gb, xga, nb, xpb, a1, b0))

    d = swap(x_b, "row", 2)
    xgb = swap(gb, "row", 1)
    b1 = add_field(cross, 1, ids(6, 5, 2), [gb, xpb, nb], a1)

    holds = holder == col
    mine_a = pick_rows(0, masks, [own, x, na, xna, pa, xpa, ga, xga])
    other_a = swap(mine_a, "col", 1)
    where_a = jnp.where(holds, 0, 1) * jnp.ones_like(masks)
    c0 = finish(cross, 0, jnp.concatenate([ids(7), where_a]), [xga], b0, mine_a, other_a, [])

    order = jnp.where(masks == 3, 7, masks - (masks > 3))
    mine_b = pick_rows(1, order, [own, x, nb, pb, xpb, gb])
    other_b = swap(mine_b, "col", 1)
    late = [xgb, d]
    late = late + [swap(after(piece, b1, c0), "col", 1) for piece in late]
    where_b = jnp.where(masks == 7, jnp.where(holds, 2, 4), where_a)
    where_b = jnp.where(masks == 3, jnp.where(holds, 3, 5), where_b)
    c1 = finish(
        cross, 1, jnp.concatenate([ids(3, 7), where_b]), [d, xgb], b1, mine_b, other_b, late
    )
    return jnp.stack([c0, c1])


def numer_by_gather(cross, replicas):
    rows, half = cross.shape[2], cross.shape[3]
    row_index, col_index = lax.axis_index("row"), lax.axis_index("col")
    first_row = row_index * rows
    holder = first_row // half
    whole = lax.all_gather(replicas, "row", axis=3, tiled=True)[:, :, 0]
    parts = jnp.einsum("fark,fbks->fabrs", cross, whole, preferred_element_type=jnp.float32)
    field = jnp.stack([parts[:, 0, 0] - parts[:, 1, 1], parts[:, 0, 1] + parts[:, 1, 0]], axis=1)
    own_rows = lax.dynamic_slice_in_dim(whole, first_row - holder * half, rows, 2)
    block_rows = jnp.where(holder == col_index, own_rows, swap(own_rows, "col", 1))
    return jnp.sum(block_rows.astype(jnp.float32) * field, axis=(1, 2))


def body(cross_spectra, replicas, tile_order):
    fnum = cross_spectra.shape[0]
    sources = replicas.shape[4]
    own = replicas[:, :, 0].astype(jnp.float32)
    norms = jnp.sum(own * own, axis=(1, 2))
    doubling = (
        lax.axis_size("row") == 8
        and replicas.shape[3] % 128 == 0
        and cross_spectra.shape[2] == 2 * replicas.shape[3]
    )
    numer = (numer_by_swaps if doubling else numer_by_gather)(cross_spectra, replicas)
    numer, norms = sum_all(jnp.stack([numer, norms]))
    beam = numer / (norms + 1e-06)
    width = sources // lax.axis_size("col")
    beam_half = lax.dynamic_slice_in_dim(beam, lax.axis_index("col") * width, width, 1)
    peak = jnp.max(jnp.abs(beam), axis=1) + 1e-06
    count = tile_order.shape[0]
    picker = (tile_order[:, None] == jnp.arange(count, dtype=jnp.int32)[None, :]).astype(jnp.float32)
    tiles = beam.reshape(fnum, count, sources // count)
    refined = (
        jnp.einsum("tu,fup->ftp", picker, tiles, precision=lax.Precision.HIGHEST)
        / peak[:, None, None]
    )
    return (beam_half, refined)


def solution(mesh):
    in_specs = (P("groups", None, "row", "col"), P("groups", None, "col", "row", None), P("groups"))
    out_specs = (P("groups", "col"), P("groups", None, None))
    return jax.shard_map(body, mesh=mesh, in_specs=in_specs, out_specs=out_specs, check_vma=False)
```

```python
import functools
import math

import jax
import jax.numpy as jnp
from jax import lax
from jax.experimental import pallas as pl
from jax.experimental.pallas import tpu as pltpu
from jax.sharding import PartitionSpec as P

VMEM_LIMIT = 60 * 1024 * 1024
HINT = pl.CostEstimate(flops=1, bytes_accessed=1, transcendentals=0)


def swap(value, axis, mask):
    size = math.prod(lax.axis_size(name) for name in (axis if isinstance(axis, tuple) else (axis,)))
    return lax.ppermute(value, axis, [(source, source ^ mask) for source in range(size)])


def after(value, *others):
    return lax.optimization_barrier((value, *others))[0]


def sum_all(value):
    axes = ("row", "col")
    size = lax.axis_size("row") * lax.axis_size("col")
    if size > 16 or size & (size - 1):
        return lax.psum(value, axes)
    mask = 1
    while mask < size:
        near = value + swap(value, axes, mask)
        if 2 * mask < size:
            near = near + (swap(value, axes, 2 * mask) + swap(value, axes, 3 * mask))
        value, mask = near, 4 * mask
    return value


def add_piece(r_ref, w, re_ref, im_ref):
    rows_re, rows_im = r_ref[0, 0], r_ref[0, 1]
    w_re, w_im = w[0], w[1]
    dot = functools.partial(jnp.dot, preferred_element_type=jnp.float32)
    re_ref[...] = re_ref[...] + dot(rows_re, w_re) + dot(rows_im, -w_im)
    im_ref[...] = im_ref[...] + dot(rows_re, w_im) + dot(rows_im, w_re)


def start_pieces(freq, w_refs, held, sem):
    for k, ref in enumerate(w_refs):
        source = ref.at[freq if ref.shape[0] > 1 else 0]
        pltpu.make_async_copy(source, held.at[k], sem.at[k]).start()


def accumulate(freq, has_total, r_ref, w_refs, total, held, sem, field):
    piece, step = pl.program_id(0), pl.program_id(1)

    @pl.when((piece == 0) & (step == 0))
    def _():
        start_pieces(freq, w_refs, held, sem)

    @pl.when(step == 0)
    def _():
        source = w_refs[0].at[0]
        pltpu.make_async_copy(source, held.at[piece], sem.at[piece]).wait()

    @pl.when(piece == 0)
    def _():
        field[step] = total[...] if has_total else jnp.zeros_like(field[step])

    add_piece(r_ref, held.at[piece], field.at[step, 0], field.at[step, 1])


def field_kernel(freq, count, has_total, ids, r_ref, *refs):
    w_refs, total = refs[:count], refs[count]
    out, held, sem, field = refs[-4:]
    accumulate(freq, has_total, r_ref, w_refs, total, held, sem, field)

    @pl.when(pl.program_id(0) == count - 1)
    def _():
        out[...] = field[pl.program_id(1)]


def numer_kernel(freq, count, late, ids, r_ref, *refs):
    w_refs = refs[:count]
    total, mine, other = refs[count : count + 3]
    late_refs = refs[count + 3 : count + 3 + late]
    out, held, sem, field, rows, row_sem = refs[-6:]
    tile = rows.shape[2]
    slots = rows.shape[0]
    last = pl.program_id(0) == count - 1
    step = pl.program_id(1)
    accumulate(freq, True, r_ref, w_refs, total, held, sem, field)

    @pl.when((pl.program_id(0) == 0) & (step == 0))
    def _():
        out[...] = jnp.zeros_like(out)
        for slot in range(slots):
            view = [ref.at[0, :, pl.ds(slot * tile, tile)] for ref in (mine, other)]
            view += [ref.at[0] for ref in late_refs]
            for k, source in enumerate(view):

                @pl.when(ids[count + slot] == k)
                def _(source=source, slot=slot):
                    pltpu.make_async_copy(source, rows.at[slot], row_sem.at[slot]).start()

    @pl.when(last)
    def _():
        source = mine.at[0, :, pl.ds(0, tile)]
        pltpu.make_async_copy(source, rows.at[step], row_sem.at[step]).wait()
        product = rows[step, 0].astype(jnp.float32) * field[step, 0]
        product += rows[step, 1].astype(jnp.float32) * field[step, 1]
        out[...] += jnp.sum(product.reshape(-1, 8, product.shape[-1]), axis=0)


def call(kernel, cross, freq, ids, pieces, total, rest, out_shape, out_spec, scratch):
    rows, (tile, sources) = cross.shape[2], pieces[0].shape[2:]
    count, steps = len(pieces), cross.shape[2] // tile
    anywhere = pl.BlockSpec(memory_space=pl.ANY)
    specs = [pl.BlockSpec((1, 2, tile, tile), lambda p, i, ids: (freq, 0, i, ids[p]))]
    specs += [anywhere] * count
    args = [cross, *pieces]
    if total is not None:
        held_at = lambda p, i, ids: (0, jnp.where(p == 0, i, steps - 1), 0)
        specs, args = specs + [pl.BlockSpec((2, tile, sources), held_at)], args + [total]
    specs, args = specs + [anywhere] * len(rest), args + list(rest)
    return pl.pallas_call(
        kernel,
        out_shape=out_shape,
        grid_spec=pltpu.PrefetchScalarGridSpec(
            num_scalar_prefetch=1,
            grid=(count, steps),
            in_specs=specs,
            out_specs=out_spec,
            scratch_shapes=[
                pltpu.VMEM((count, 2, tile, sources), pieces[0].dtype),
                pltpu.SemaphoreType.DMA((count,)),
                pltpu.VMEM((steps, 2, tile, sources), jnp.float32),
                *scratch,
            ],
        ),
        compiler_params=pltpu.CompilerParams(vmem_limit_bytes=VMEM_LIMIT),
        cost_estimate=HINT,
    )(ids, *args)


def add_field(cross, freq, ids, pieces, total=None):
    rows, (tile, sources) = cross.shape[2], pieces[0].shape[2:]
    count = len(pieces)
    return call(
        functools.partial(field_kernel, freq, count, total is not None),
        cross,
        freq,
        ids,
        pieces,
        total,
        [],
        jax.ShapeDtypeStruct((2, rows, sources), jnp.float32),
        pl.BlockSpec(
            (2, tile, sources), lambda p, i, ids: (0, jnp.where(p == count - 1, i, 0), 0)
        ),
        [],
    )


def finish(cross, freq, ids, pieces, total, mine, other, late):
    steps, (tile, sources) = cross.shape[2] // pieces[0].shape[2], pieces[0].shape[2:]
    out = call(
        functools.partial(numer_kernel, freq, len(pieces), len(late)),
        cross,
        freq,
        ids,
        pieces,
        total,
        [mine, other, *late],
        jax.ShapeDtypeStruct((8, sources), jnp.float32),
        pl.BlockSpec((8, sources), lambda p, i, ids: (0, 0)),
        [pltpu.VMEM((steps, 2, tile, sources), mine.dtype), pltpu.SemaphoreType.DMA((steps,))],
    )
    return jnp.sum(out, axis=0)


def pick_kernel(freq, ids, *refs):
    pieces, out, sem = refs[:-2], refs[-2], refs[-1]
    width = pieces[0].shape[2]
    for slot in range(2):
        for k, piece in enumerate(pieces):

            @pl.when(ids[slot] == k)
            def _(slot=slot, piece=piece):
                source = piece.at[freq if piece.shape[0] > 1 else 0]
                pltpu.make_async_copy(
                    source, out.at[0, :, pl.ds(slot * width, width)], sem.at[slot]
                ).start()

    for slot in range(2):

        @pl.when(ids[slot] < len(pieces))
        def _(slot=slot):
            pltpu.make_async_copy(
                pieces[0].at[0], out.at[0, :, pl.ds(slot * width, width)], sem.at[slot]
            ).wait()


def pick_rows(freq, ids, pieces):
    _, _, width, sources = pieces[0].shape
    return pl.pallas_call(
        functools.partial(pick_kernel, freq),
        out_shape=jax.ShapeDtypeStruct((1, 2, 2 * width, sources), pieces[0].dtype),
        grid_spec=pltpu.PrefetchScalarGridSpec(
            num_scalar_prefetch=1,
            grid=(1,),
            in_specs=[pl.BlockSpec(memory_space=pl.ANY)] * len(pieces),
            out_specs=pl.BlockSpec((1, 2, 2 * width, sources), lambda i, ids: (0, 0, 0, 0)),
            scratch_shapes=[pltpu.SemaphoreType.DMA((2,))],
        ),
        cost_estimate=HINT,
    )(ids, *pieces)


def numer_by_swaps(cross, replicas):
    rows, half = cross.shape[2], cross.shape[3]
    width = replicas.shape[3]
    me = lax.axis_index("row").astype(jnp.int32)
    col = lax.axis_index("col").astype(jnp.int32)
    holder = me * rows // half
    first = (me * rows - holder * half) // width
    masks = jnp.stack([first ^ me, (first + 1) ^ me])
    ids = lambda *wanted: me ^ jnp.array(wanted, jnp.int32)

    own = replicas[:, :, 0]
    holds = holder == col
    where_a = jnp.where(holds, 0, 1) * jnp.ones_like(masks)

    own_a = own[0:1]
    x = swap(after(own, own_a), "row", 1)
    pa = swap(own_a, "row", 4)
    na = swap(own_a, "row", 2)
    a0 = add_field(cross, 0, ids(0), [own])
    a1 = add_field(cross, 1, ids(0), [own])
    own_b = after(own, a0)[1:2]
    x, pa, na, own_b, a0, a1 = lax.optimization_barrier((x, pa, na, own_b, a0, a1))

    pb = swap(own_b, "row", 4)
    ga = swap(pa, "row", 2)
    xpa = swap(pa, "row", 1)
    xna = swap(na, "row", 1)
    a0 = add_field(cross, 0, ids(1, 2, 4), [x, na, pa], a0)
    a1 = add_field(cross, 1, ids(1), [x], a1)
    x_b = x[1:2]
    pb, ga, xpa, xna, a0, a1, x_b, own_b = lax.optimization_barrier(
        (pb, ga, xpa, xna, a0, a1, x_b, own_b)
    )

    gb = swap(pb, "row", 2)
    xga = swap(ga, "row", 1)
    b0 = add_field(cross, 0, ids(3, 5, 6), [xna, xpa, ga], a0)
    xpb = swap(pb, "row", 1)
    nb = swap(own_b, "row", 2)
    a1 = add_field(cross, 1, ids(4), [pb], a1)
    d = swap(after(x_b, gb), "row", 2)
    xgb = swap(gb, "row", 1)
    gb, nb, xga, xpb, b0, a1 = lax.optimization_barrier((gb, nb, xga, xpb, b0, a1))

    b1 = add_field(cross, 1, ids(6, 5, 2), [gb, xpb, nb], a1)
    mine_a = pick_rows(0, after(masks, b1), [own, x, na, xna, pa, xpa, ga, xga])
    other_a = swap(mine_a, "col", 1)
    c0 = finish(cross, 0, jnp.concatenate([ids(7), where_a]), [xga], b0, mine_a, other_a, [])

    order = jnp.where(masks == 3, 7, masks - (masks > 3))
    mine_b = pick_rows(1, order, [own, x, nb, pb, xpb, gb])
    other_b = swap(mine_b, "col", 1)
    late = [xgb, d]
    late = late + [swap(after(piece, b1, mine_b), "col", 1) for piece in late]
    where_b = jnp.where(masks == 7, jnp.where(holds, 2, 4), where_a)
    where_b = jnp.where(masks == 3, jnp.where(holds, 3, 5), where_b)
    c1 = finish(
        cross, 1, jnp.concatenate([ids(3, 7), where_b]), [d, xgb], b1, mine_b, other_b, late
    )
    return jnp.stack([c0, c1])


def numer_by_gather(cross, replicas):
    rows, half = cross.shape[2], cross.shape[3]
    row_index, col_index = lax.axis_index("row"), lax.axis_index("col")
    first_row = row_index * rows
    holder = first_row // half
    whole = lax.all_gather(replicas, "row", axis=3, tiled=True)[:, :, 0]
    parts = jnp.einsum("fark,fbks->fabrs", cross, whole, preferred_element_type=jnp.float32)
    field = jnp.stack([parts[:, 0, 0] - parts[:, 1, 1], parts[:, 0, 1] + parts[:, 1, 0]], axis=1)
    own_rows = lax.dynamic_slice_in_dim(whole, first_row - holder * half, rows, 2)
    block_rows = jnp.where(holder == col_index, own_rows, swap(own_rows, "col", 1))
    return jnp.sum(block_rows.astype(jnp.float32) * field, axis=(1, 2))


def body(cross_spectra, replicas, tile_order):
    fnum = cross_spectra.shape[0]
    sources = replicas.shape[4]
    own = replicas[:, :, 0].astype(jnp.float32)
    norms = jnp.sum(own * own, axis=(1, 2))
    doubling = (
        lax.axis_size("row") == 8
        and replicas.shape[3] % 128 == 0
        and cross_spectra.shape[2] == 2 * replicas.shape[3]
    )
    numer = (numer_by_swaps if doubling else numer_by_gather)(cross_spectra, replicas)
    sums = sum_all(jnp.concatenate([numer, norms]))
    numer, norms = sums[:fnum], sums[fnum:]
    beam = numer / (norms + 1e-06)
    width = sources // lax.axis_size("col")
    beam_half = lax.dynamic_slice_in_dim(beam, lax.axis_index("col") * width, width, 1)
    peak = jnp.max(jnp.abs(beam), axis=1) + 1e-06
    count = tile_order.shape[0]
    picker = (tile_order[:, None] == jnp.arange(count, dtype=jnp.int32)[None, :]).astype(jnp.float32)
    tiles = beam.reshape(fnum, count, sources // count)
    refined = (
        jnp.einsum("tu,fup->ftp", picker, tiles, precision=lax.Precision.HIGHEST)
        / peak[:, None, None]
    )
    return (beam_half, refined)


def solution(mesh):
    in_specs = (P("groups", None, "row", "col"), P("groups", None, "col", "row", None), P("groups"))
    out_specs = (P("groups", "col"), P("groups", None, None))
    return jax.shard_map(body, mesh=mesh, in_specs=in_specs, out_specs=out_specs, check_vma=False)
```

```python
import functools
import math

import jax
import jax.numpy as jnp
from jax import lax
from jax.experimental import pallas as pl
from jax.experimental.pallas import tpu as pltpu
from jax.sharding import PartitionSpec as P

LANES = 256
VMEM_LIMIT = 60 * 1024 * 1024
HINT = pl.CostEstimate(flops=1, bytes_accessed=1, transcendentals=0)


def swap(value, axis, mask):
    size = math.prod(lax.axis_size(name) for name in (axis if isinstance(axis, tuple) else (axis,)))
    return lax.ppermute(value, axis, [(source, source ^ mask) for source in range(size)])


def after(value, *others):
    return lax.optimization_barrier((value, *others))[0]


def sum_all(value):
    axes = ("row", "col")
    size = lax.axis_size("row") * lax.axis_size("col")
    if size > 16 or size & (size - 1):
        return lax.psum(value, axes)
    mask = 1
    while mask < size:
        near = value + swap(value, axes, mask)
        if 2 * mask < size:
            near = near + (swap(value, axes, 2 * mask) + swap(value, axes, 3 * mask))
        value, mask = near, 4 * mask
    return value


def accumulate(freq, first, r_ref, w_refs, total, held, sem, field, tot, tot_sem):
    piece, step = pl.program_id(0), pl.program_id(1)
    lanes = field.shape[3]

    @pl.when((piece == 0) & (step == 0))
    def _():
        for k, ref in enumerate(w_refs):
            source = ref.at[freq if ref.shape[0] > 1 else 0]
            pltpu.make_async_copy(source, held.at[k], sem.at[k]).start()
        if total is not None:
            pltpu.make_async_copy(total, tot, tot_sem.at[0]).start()
        first()

    @pl.when(step == 0)
    def _():
        pltpu.make_async_copy(w_refs[0].at[0], held.at[piece], sem.at[piece]).wait()

    here = pl.ds(pl.multiple_of(step * lanes, lanes), lanes)
    rows_re, rows_im = r_ref[0, 0], r_ref[0, 1]
    w_re, w_im = held[piece, 0, :, here], held[piece, 1, :, here]
    dot = functools.partial(jnp.dot, preferred_element_type=jnp.float32)

    @pl.when(piece == 0)
    def _():
        field[step, 0] = dot(rows_re, w_re) + dot(rows_im, -w_im)
        field[step, 1] = dot(rows_re, w_im) + dot(rows_im, w_re)

    @pl.when(piece > 0)
    def _():
        field[step, 0] += dot(rows_re, w_re) + dot(rows_im, -w_im)
        field[step, 1] += dot(rows_re, w_im) + dot(rows_im, w_re)

    if total is not None:

        @pl.when((piece == len(w_refs) - 1) & (step == 0))
        def _():
            pltpu.make_async_copy(total, tot, tot_sem.at[0]).wait()


def field_kernel(freq, count, ids, r_ref, *refs):
    w_refs, (total, out, held, sem, field, tot, tot_sem) = refs[:count], refs[count:]
    accumulate(freq, lambda: None, r_ref, w_refs, total, held, sem, field, tot, tot_sem)
    step = pl.program_id(1)

    @pl.when(pl.program_id(0) == count - 1)
    def _():
        out[0] = field[step] + tot[step]


def first_kernel(freq, count, ids, r_ref, *refs):
    w_refs, (out, held, sem, field) = refs[:count], refs[count:]
    accumulate(freq, lambda: None, r_ref, w_refs, None, held, sem, field, None, None)

    @pl.when(pl.program_id(0) == count - 1)
    def _():
        out[0] = field[pl.program_id(1)]


def start_rows(freq, ids, base, whole, singles, rows, sem):
    width = rows.shape[1] // 2
    for slot in range(2):
        here = pl.ds(slot * width, width)
        views = [ref.at[freq, :, here] for ref in whole] + [ref.at[0] for ref in singles]
        for k, source in enumerate(views):

            @pl.when(ids[base + slot] == k)
            def _(source=source, slot=slot, here=here):
                pltpu.make_async_copy(source, rows.at[:, here], sem.at[slot]).start()


def wait_rows(slot, singles, rows, sem):
    width = rows.shape[1] // 2
    here = pl.ds(slot * width, width)
    pltpu.make_async_copy(singles[0].at[0], rows.at[:, here], sem.at[slot]).wait()


def fold(rows_re, rows_im, re, im):
    product = rows_re.astype(jnp.float32) * re + rows_im.astype(jnp.float32) * im
    return jnp.sum(product.reshape(-1, 8, product.shape[-1]), axis=0)


def numer_kernel(freq, count, ids, r_ref, *refs):
    w_refs, total, whole = refs[:count], refs[count], refs[count + 1 : count + 3]
    singles = refs[count + 3 : -8]
    out, held, sem, field, tot, tot_sem, rows, row_sem = refs[-8:]
    begin = lambda: start_rows(freq, ids, count, whole, singles, rows, row_sem)
    accumulate(freq, begin, r_ref, w_refs, total, held, sem, field, tot, tot_sem)
    step = pl.program_id(1)
    lanes = field.shape[3]
    last = pl.program_id(0) == count - 1

    @pl.when(last & (step == 0))
    def _():
        for slot in range(2):
            wait_rows(slot, singles, rows, row_sem)

    @pl.when(last)
    def _():
        here = pl.ds(pl.multiple_of(step * lanes, lanes), lanes)
        re, im = field[step, 0] + tot[step, 0], field[step, 1] + tot[step, 1]
        out[...] = fold(rows[0, :, here], rows[1, :, here], re, im)


def dot_kernel(freq, ids, field, *refs):
    whole, singles, (out, rows, sem) = refs[:2], refs[2:-3], refs[-3:]
    step = pl.program_id(0)
    lanes = field.shape[3]

    @pl.when(step == 0)
    def _():
        start_rows(freq, ids, 0, whole, singles, rows, sem)
        for slot in range(2):
            wait_rows(slot, singles, rows, sem)

    here = pl.ds(pl.multiple_of(step * lanes, lanes), lanes)
    out[...] = fold(rows[0, :, here], rows[1, :, here], field[0, 0], field[0, 1])


ANYWHERE = pl.BlockSpec(memory_space=pl.ANY)


def call(kernel, cross, freq, ids, pieces, rest, out_shape, out_spec, has_total, scratch):
    rows, (width, sources) = cross.shape[2], pieces[0].shape[2:]
    count, steps = len(pieces), sources // LANES
    total = [pltpu.VMEM((steps, 2, rows, LANES), jnp.float32), pltpu.SemaphoreType.DMA((1,))]
    return pl.pallas_call(
        functools.partial(kernel, freq, count),
        out_shape=out_shape,
        grid_spec=pltpu.PrefetchScalarGridSpec(
            num_scalar_prefetch=1,
            grid=(count, steps),
            in_specs=[pl.BlockSpec((1, 2, rows, width), lambda p, n, ids: (freq, 0, 0, ids[p]))]
            + [ANYWHERE] * (count + len(rest)),
            out_specs=out_spec,
            scratch_shapes=[
                pltpu.VMEM((count, 2, width, sources), pieces[0].dtype),
                pltpu.SemaphoreType.DMA((count,)),
                pltpu.VMEM((steps, 2, rows, LANES), jnp.float32),
                *(total if has_total else []),
                *scratch,
            ],
        ),
        compiler_params=pltpu.CompilerParams(vmem_limit_bytes=VMEM_LIMIT),
        cost_estimate=HINT,
    )(ids, cross, *pieces, *rest)


def add_field(cross, freq, ids, pieces, total=None):
    rows, sources = cross.shape[2], pieces[0].shape[3]
    count = len(pieces)
    return call(
        first_kernel if total is None else field_kernel,
        cross,
        freq,
        ids,
        pieces,
        [] if total is None else [total],
        jax.ShapeDtypeStruct((sources // LANES, 2, rows, LANES), jnp.float32),
        pl.BlockSpec(
            (1, 2, rows, LANES), lambda p, n, ids: (jnp.where(p == count - 1, n, 0), 0, 0, 0)
        ),
        total is not None,
        [],
    )


def row_scratch(rows, sources, dtype):
    return [pltpu.VMEM((2, rows, sources), dtype), pltpu.SemaphoreType.DMA((2,))]


def finish(cross, freq, ids, pieces, total, whole, singles):
    rows, sources = cross.shape[2], pieces[0].shape[3]
    count = len(pieces)
    out = call(
        numer_kernel,
        cross,
        freq,
        ids,
        pieces,
        [total, *whole, *singles],
        jax.ShapeDtypeStruct((8, sources), jnp.float32),
        pl.BlockSpec((8, LANES), lambda p, n, ids: (0, jnp.where(p == count - 1, n, 0))),
        True,
        row_scratch(rows, sources, pieces[0].dtype),
    )
    return jnp.sum(out, axis=0)


def dot_rows(freq, ids, field, whole, singles):
    steps, _, rows, lanes = field.shape
    sources = steps * lanes
    out = pl.pallas_call(
        functools.partial(dot_kernel, freq),
        out_shape=jax.ShapeDtypeStruct((8, sources), jnp.float32),
        grid_spec=pltpu.PrefetchScalarGridSpec(
            num_scalar_prefetch=1,
            grid=(steps,),
            in_specs=[pl.BlockSpec((1, 2, rows, lanes), lambda n, ids: (n, 0, 0, 0))]
            + [ANYWHERE] * (2 + len(singles)),
            out_specs=pl.BlockSpec((8, lanes), lambda n, ids: (0, n)),
            scratch_shapes=row_scratch(rows, sources, whole[0].dtype),
        ),
        compiler_params=pltpu.CompilerParams(vmem_limit_bytes=VMEM_LIMIT),
        cost_estimate=HINT,
    )(ids, field, *whole, *singles)
    return jnp.sum(out, axis=0)


def pick_kernel(plan, ids, *refs):
    pieces, out, sem = refs[:-2], refs[-2], refs[-1]
    width = pieces[0].shape[2]
    for wait in (False, True):
        for place, (freq, slots, choices) in enumerate(plan):
            for slot in range(2):
                for mask, k in choices:

                    @pl.when(ids[slot] == mask)
                    def _(place=place, freq=freq, slots=slots, slot=slot, k=k):
                        piece = pieces[k]
                        source = piece.at[freq if piece.shape[0] > 1 else 0]
                        start = slot * width if slots == 2 else 0
                        copy = pltpu.make_async_copy(
                            source, out.at[place, :, pl.ds(start, width)], sem.at[place, slot]
                        )
                        copy.wait() if wait else copy.start()


def pick_rows(ids, plan, pieces):
    _, _, width, sources = pieces[0].shape
    shape = (len(plan), 2, plan[0][1] * width, sources)
    return pl.pallas_call(
        functools.partial(pick_kernel, plan),
        out_shape=jax.ShapeDtypeStruct(shape, pieces[0].dtype),
        grid_spec=pltpu.PrefetchScalarGridSpec(
            num_scalar_prefetch=1,
            grid=(1,),
            in_specs=[ANYWHERE] * len(pieces),
            out_specs=pl.BlockSpec(shape, lambda i, ids: (0, 0, 0, 0)),
            scratch_shapes=[pltpu.SemaphoreType.DMA((len(plan), 2))],
        ),
        compiler_params=pltpu.CompilerParams(vmem_limit_bytes=VMEM_LIMIT),
        cost_estimate=HINT,
    )(ids, *pieces)


def numer_by_swaps(cross, replicas):
    rows, half = cross.shape[2], cross.shape[3]
    width = replicas.shape[3]
    me = lax.axis_index("row").astype(jnp.int32)
    col = lax.axis_index("col").astype(jnp.int32)
    holder = me * rows // half
    first = (me * rows - holder * half) // width
    masks = jnp.stack([first ^ me, (first + 1) ^ me])
    holds = holder == col
    ids = lambda *wanted: me ^ jnp.array(wanted, jnp.int32)
    barrier = lambda *values: lax.optimization_barrier(values)
    own = replicas[:, :, 0]

    own_a = own[0:1]
    x = swap(after(own, own_a), "row", 1)
    pa = swap(own_a, "row", 4)
    na = swap(own_a, "row", 2)
    a0 = add_field(cross, 0, ids(0), [own])
    a1 = add_field(cross, 1, ids(0), [own])
    own_b = after(own, a0)[1:2]
    x, pa, na, own_b, a0, a1 = barrier(x, pa, na, own_b, a0, a1)

    pb = swap(own_b, "row", 4)
    ga = swap(pa, "row", 2)
    xpa = swap(pa, "row", 1)
    xna = swap(na, "row", 1)
    a0 = add_field(cross, 0, ids(1, 2, 4), [x, na, pa], a0)
    a1 = add_field(cross, 1, ids(1), [x], a1)
    x_b = x[1:2]
    pb, ga, xpa, xna, a0, a1, x_b, own_b = barrier(pb, ga, xpa, xna, a0, a1, x_b, own_b)

    gb = swap(pb, "row", 2)
    xga = swap(ga, "row", 1)
    xpb = swap(pb, "row", 1)
    nb = swap(own_b, "row", 2)
    b0 = add_field(cross, 0, ids(3, 5, 6), [xna, xpa, ga], a0)
    a1 = add_field(cross, 1, ids(4), [pb], a1)
    plan = [
        (0, 2, [(0, 0), (1, 1), (2, 2), (3, 3), (4, 4), (5, 5), (6, 6)]),
        (1, 2, [(0, 0), (1, 1), (4, 7)]),
    ]
    mine = pick_rows(after(masks, b0), plan, [own, x, na, xna, pa, xpa, ga, pb])
    gb, nb, xga, xpb, b0, a1, x_b, mine = barrier(gb, nb, xga, xpb, b0, a1, x_b, mine)

    other = swap(mine, "col", 1)
    other_xga = swap(xga, "col", 1)
    d = swap(x_b, "row", 2)
    xgb = swap(gb, "row", 1)
    b1 = add_field(cross, 1, ids(6, 5, 2), [gb, xpb, nb], a1)
    plan = [(0, 1, [(6, 0), (5, 1), (2, 2)])]
    mine_b = pick_rows(after(masks, b1), plan, [gb, xpb, nb])
    whole = jnp.where(holds, 0, 1)
    where = jnp.where(masks == 7, jnp.where(holds, 2, 3), whole)
    c0 = finish(
        cross, 0, jnp.concatenate([ids(7), where]), [xga], b0, [mine, other], [xga, other_xga]
    )
    d, xgb, b1, mine_b, c0 = barrier(d, xgb, b1, mine_b, c0)

    other_b, other_d, other_xgb = (swap(piece, "col", 1) for piece in (mine_b, d, xgb))
    field = add_field(cross, 1, ids(3, 7), [d, xgb], b1)
    where = jnp.full_like(masks, whole)
    for k, mask in enumerate((6, 5, 2)):
        where = jnp.where(masks == mask, jnp.where(holds, 2 + k, 5), where)
    where = jnp.where(masks == 3, jnp.where(holds, 6, 7), where)
    where = jnp.where(masks == 7, jnp.where(holds, 8, 9), where)
    singles = [gb, xpb, nb, other_b, d, other_d, xgb, other_xgb]
    c1 = dot_rows(1, where, field, [mine, other], singles)
    return jnp.stack([c0, c1])


def numer_by_gather(cross, replicas):
    rows, half = cross.shape[2], cross.shape[3]
    row_index, col_index = lax.axis_index("row"), lax.axis_index("col")
    first_row = row_index * rows
    holder = first_row // half
    whole = lax.all_gather(replicas, "row", axis=3, tiled=True)[:, :, 0]
    parts = jnp.einsum("fark,fbks->fabrs", cross, whole, preferred_element_type=jnp.float32)
    field = jnp.stack([parts[:, 0, 0] - parts[:, 1, 1], parts[:, 0, 1] + parts[:, 1, 0]], axis=1)
    own_rows = lax.dynamic_slice_in_dim(whole, first_row - holder * half, rows, 2)
    block_rows = jnp.where(holder == col_index, own_rows, swap(own_rows, "col", 1))
    return jnp.sum(block_rows.astype(jnp.float32) * field, axis=(1, 2))


def body(cross_spectra, replicas, tile_order):
    fnum = cross_spectra.shape[0]
    sources = replicas.shape[4]
    own = replicas[:, :, 0].astype(jnp.float32)
    norms = jnp.sum(own * own, axis=(1, 2))
    doubling = (
        lax.axis_size("row") == 8
        and replicas.shape[3] % 128 == 0
        and cross_spectra.shape[2] == 2 * replicas.shape[3]
    )
    numer = (numer_by_swaps if doubling else numer_by_gather)(cross_spectra, replicas)
    sums = sum_all(jnp.concatenate([numer, norms]))
    numer, norms = sums[:fnum], sums[fnum:]
    beam = numer / (norms + 1e-06)
    width = sources // lax.axis_size("col")
    beam_half = lax.dynamic_slice_in_dim(beam, lax.axis_index("col") * width, width, 1)
    peak = jnp.max(jnp.abs(beam), axis=1) + 1e-06
    count = tile_order.shape[0]
    picker = (tile_order[:, None] == jnp.arange(count, dtype=jnp.int32)[None, :]).astype(jnp.float32)
    tiles = beam.reshape(fnum, count, sources // count)
    refined = (
        jnp.einsum("tu,fup->ftp", picker, tiles, precision=lax.Precision.HIGHEST)
        / peak[:, None, None]
    )
    return (beam_half, refined)


def solution(mesh):
    in_specs = (P("groups", None, "row", "col"), P("groups", None, "col", "row", None), P("groups"))
    out_specs = (P("groups", "col"), P("groups", None, None))
    return jax.shard_map(body, mesh=mesh, in_specs=in_specs, out_specs=out_specs, check_vma=False)
```

```python
import functools
import math

import jax
import jax.numpy as jnp
from jax import lax
from jax.experimental import pallas as pl
from jax.experimental.pallas import tpu as pltpu
from jax.sharding import PartitionSpec as P

VMEM_LIMIT = 60 * 1024 * 1024
HINT = pl.CostEstimate(flops=1, bytes_accessed=1, transcendentals=0)


def swap(value, axis, mask):
    size = math.prod(lax.axis_size(name) for name in (axis if isinstance(axis, tuple) else (axis,)))
    return lax.ppermute(value, axis, [(source, source ^ mask) for source in range(size)])


def after(value, *others):
    return lax.optimization_barrier((value, *others))[0]


def sum_all(value):
    axes = ("row", "col")
    size = lax.axis_size("row") * lax.axis_size("col")
    if size > 16 or size & (size - 1):
        return lax.psum(value, axes)
    mask = 1
    while mask < size:
        near = value + swap(value, axes, mask)
        if 2 * mask < size:
            near = near + (swap(value, axes, 2 * mask) + swap(value, axes, 3 * mask))
        value, mask = near, 4 * mask
    return value


def piece_copies(freq, ids, cross, ref, k, left, right, sem):
    width = ref.shape[2]
    columns = pl.ds(pl.multiple_of(ids[k] * width, width), width)
    which = freq if ref.shape[0] > 1 else 0
    low, high = pl.ds(0, width), pl.ds(width, width)
    return [
        pltpu.make_async_copy(ref.at[which, 0], right.at[k, 0, low], sem.at[k, 0]),
        pltpu.make_async_copy(ref.at[which, 1], right.at[k, 1, low], sem.at[k, 1]),
        pltpu.make_async_copy(ref.at[which, 0], right.at[k, 1, high], sem.at[k, 2]),
        pltpu.make_async_copy(cross.at[freq, 0, :, columns], left.at[k, :, low], sem.at[k, 3]),
        pltpu.make_async_copy(cross.at[freq, 1, :, columns], left.at[k, :, high], sem.at[k, 4]),
    ]


def accumulate(freq, ids, first, cross, w_refs, total, left, right, sem, field, tot, tot_sem):
    piece, part = pl.program_id(0), pl.program_id(1)
    copies = [
        piece_copies(freq, ids, cross, ref, k, left, right, sem) for k, ref in enumerate(w_refs)
    ]

    @pl.when((piece == 0) & (part == 0))
    def _():
        for group in copies:
            for copy in group:
                copy.start()
        if total is not None:
            pltpu.make_async_copy(total, tot, tot_sem.at[0]).start()
        first()

    for k, group in enumerate(copies):

        @pl.when((piece == k) & (part == 0))
        def _(k=k, group=group):
            for copy in group:
                copy.wait()
            width = right.shape[2] // 2
            right[k, 0, width:] = -right[k, 1, :width]

    dot = functools.partial(jnp.dot, preferred_element_type=jnp.float32)

    @pl.when(piece == 0)
    def _():
        field[part] = dot(left[piece], right[piece, part])

    @pl.when(piece > 0)
    def _():
        field[part] += dot(left[piece], right[piece, part])

    if total is not None:

        @pl.when((piece == len(w_refs) - 1) & (part == 0))
        def _():
            pltpu.make_async_copy(total, tot, tot_sem.at[0]).wait()


def field_kernel(freq, count, ids, cross, *refs):
    w_refs, (total, out, left, right, sem, field, tot, tot_sem) = refs[:count], refs[count:]
    accumulate(
        freq, ids, lambda: None, cross, w_refs, total, left, right, sem, field, tot, tot_sem
    )
    part = pl.program_id(1)

    @pl.when(pl.program_id(0) == count - 1)
    def _():
        out[0] = field[part] + tot[part]


def first_kernel(freq, count, ids, cross, *refs):
    w_refs, (out, left, right, sem, field) = refs[:count], refs[count:]
    accumulate(freq, ids, lambda: None, cross, w_refs, None, left, right, sem, field, None, None)

    @pl.when(pl.program_id(0) == count - 1)
    def _():
        out[0] = field[pl.program_id(1)]


def start_rows(freq, ids, base, whole, singles, rows, sem):
    width = rows.shape[1] // 2
    for slot in range(2):
        here = pl.ds(slot * width, width)
        views = [ref.at[freq, :, here] for ref in whole] + [ref.at[0] for ref in singles]
        for k, source in enumerate(views):

            @pl.when(ids[base + slot] == k)
            def _(source=source, slot=slot, here=here):
                pltpu.make_async_copy(source, rows.at[:, here], sem.at[slot]).start()


def wait_rows(slot, singles, rows, sem):
    width = rows.shape[1] // 2
    here = pl.ds(slot * width, width)
    pltpu.make_async_copy(singles[0].at[0], rows.at[:, here], sem.at[slot]).wait()


def fold(rows, field):
    product = rows.astype(jnp.float32) * field
    return jnp.sum(product.reshape(-1, 8, product.shape[-1]), axis=0)


def numer_kernel(freq, count, ids, cross, *refs):
    w_refs, total, whole = refs[:count], refs[count], refs[count + 1 : count + 3]
    singles = refs[count + 3 : -9]
    out, left, right, sem, field, tot, tot_sem, rows, row_sem = refs[-9:]
    begin = lambda: start_rows(freq, ids, count, whole, singles, rows, row_sem)
    accumulate(freq, ids, begin, cross, w_refs, total, left, right, sem, field, tot, tot_sem)
    part = pl.program_id(1)
    last = pl.program_id(0) == count - 1

    @pl.when(last & (part == 0))
    def _():
        out[...] = jnp.zeros_like(out)
        for slot in range(2):
            wait_rows(slot, singles, rows, row_sem)

    @pl.when(last)
    def _():
        out[...] += fold(rows[part], field[part] + tot[part])


def dot_kernel(freq, ids, field, *refs):
    whole, singles, (out, rows, sem) = refs[:2], refs[2:-3], refs[-3:]
    slot, part = pl.program_id(0), pl.program_id(1)
    width = field.shape[1]

    @pl.when((slot == 0) & (part == 0))
    def _():
        out[...] = jnp.zeros_like(out)
        start_rows(freq, ids, 0, whole, singles, rows, sem)

    for k in range(2):

        @pl.when((slot == k) & (part == 0))
        def _(k=k):
            wait_rows(k, singles, rows, sem)

    here = pl.ds(pl.multiple_of(slot * width, width), width)
    out[...] += fold(rows[part, here], field[0])


ANYWHERE = pl.BlockSpec(memory_space=pl.ANY)


def call(kernel, cross, freq, ids, pieces, rest, out_shape, out_spec, has_total, scratch):
    rows, (width, sources) = cross.shape[2], pieces[0].shape[2:]
    count, dtype = len(pieces), pieces[0].dtype
    total = [pltpu.VMEM((2, rows, sources), jnp.float32), pltpu.SemaphoreType.DMA((1,))]
    return pl.pallas_call(
        functools.partial(kernel, freq, count),
        out_shape=out_shape,
        grid_spec=pltpu.PrefetchScalarGridSpec(
            num_scalar_prefetch=1,
            grid=(count, 2),
            in_specs=[ANYWHERE] * (1 + count + len(rest)),
            out_specs=out_spec,
            scratch_shapes=[
                pltpu.VMEM((count, rows, 2 * width), dtype),
                pltpu.VMEM((count, 2, 2 * width, sources), dtype),
                pltpu.SemaphoreType.DMA((count, 5)),
                pltpu.VMEM((2, rows, sources), jnp.float32),
                *(total if has_total else []),
                *scratch,
            ],
        ),
        compiler_params=pltpu.CompilerParams(vmem_limit_bytes=VMEM_LIMIT),
        cost_estimate=HINT,
    )(ids, cross, *pieces, *rest)


def add_field(cross, freq, ids, pieces, total=None):
    rows, sources = cross.shape[2], pieces[0].shape[3]
    count = len(pieces)
    return call(
        first_kernel if total is None else field_kernel,
        cross,
        freq,
        ids,
        pieces,
        [] if total is None else [total],
        jax.ShapeDtypeStruct((2, rows, sources), jnp.float32),
        pl.BlockSpec(
            (1, rows, sources), lambda p, part, ids: (jnp.where(p == count - 1, part, 0), 0, 0)
        ),
        total is not None,
        [],
    )


def row_scratch(rows, sources, dtype):
    return [pltpu.VMEM((2, rows, sources), dtype), pltpu.SemaphoreType.DMA((2,))]


def finish(cross, freq, ids, pieces, total, whole, singles):
    rows, sources = cross.shape[2], pieces[0].shape[3]
    out = call(
        numer_kernel,
        cross,
        freq,
        ids,
        pieces,
        [total, *whole, *singles],
        jax.ShapeDtypeStruct((8, sources), jnp.float32),
        pl.BlockSpec((8, sources), lambda p, part, ids: (0, 0)),
        True,
        row_scratch(rows, sources, pieces[0].dtype),
    )
    return jnp.sum(out, axis=0)


def dot_rows(freq, ids, field, whole, singles):
    _, rows, sources = field.shape
    out = pl.pallas_call(
        functools.partial(dot_kernel, freq),
        out_shape=jax.ShapeDtypeStruct((8, sources), jnp.float32),
        grid_spec=pltpu.PrefetchScalarGridSpec(
            num_scalar_prefetch=1,
            grid=(2, 2),
            in_specs=[
                pl.BlockSpec((1, rows // 2, sources), lambda slot, part, ids: (part, slot, 0))
            ]
            + [ANYWHERE] * (2 + len(singles)),
            out_specs=pl.BlockSpec((8, sources), lambda slot, part, ids: (0, 0)),
            scratch_shapes=row_scratch(rows, sources, whole[0].dtype),
        ),
        compiler_params=pltpu.CompilerParams(vmem_limit_bytes=VMEM_LIMIT),
        cost_estimate=HINT,
    )(ids, field, *whole, *singles)
    return jnp.sum(out, axis=0)


def pick_kernel(plan, ids, *refs):
    pieces, out, sem = refs[:-2], refs[-2], refs[-1]
    width = pieces[0].shape[2]
    for wait in (False, True):
        for place, (freq, slots, choices) in enumerate(plan):
            for slot in range(2):
                for mask, k in choices:

                    @pl.when(ids[slot] == mask)
                    def _(place=place, freq=freq, slots=slots, slot=slot, k=k):
                        piece = pieces[k]
                        source = piece.at[freq if piece.shape[0] > 1 else 0]
                        start = slot * width if slots == 2 else 0
                        copy = pltpu.make_async_copy(
                            source, out.at[place, :, pl.ds(start, width)], sem.at[place, slot]
                        )
                        copy.wait() if wait else copy.start()


def pick_rows(ids, plan, pieces):
    _, _, width, sources = pieces[0].shape
    shape = (len(plan), 2, plan[0][1] * width, sources)
    return pl.pallas_call(
        functools.partial(pick_kernel, plan),
        out_shape=jax.ShapeDtypeStruct(shape, pieces[0].dtype),
        grid_spec=pltpu.PrefetchScalarGridSpec(
            num_scalar_prefetch=1,
            grid=(1,),
            in_specs=[ANYWHERE] * len(pieces),
            out_specs=pl.BlockSpec(shape, lambda i, ids: (0, 0, 0, 0)),
            scratch_shapes=[pltpu.SemaphoreType.DMA((len(plan), 2))],
        ),
        compiler_params=pltpu.CompilerParams(vmem_limit_bytes=VMEM_LIMIT),
        cost_estimate=HINT,
    )(ids, *pieces)


def numer_by_swaps(cross, replicas):
    rows, half = cross.shape[2], cross.shape[3]
    width = replicas.shape[3]
    me = lax.axis_index("row").astype(jnp.int32)
    col = lax.axis_index("col").astype(jnp.int32)
    holder = me * rows // half
    first = (me * rows - holder * half) // width
    masks = jnp.stack([first ^ me, (first + 1) ^ me])
    holds = holder == col
    ids = lambda *wanted: me ^ jnp.array(wanted, jnp.int32)
    barrier = lambda *values: lax.optimization_barrier(values)
    own = replicas[:, :, 0]

    own_a = own[0:1]
    x = swap(after(own, own_a), "row", 1)
    pa = swap(own_a, "row", 4)
    na = swap(own_a, "row", 2)
    a0 = add_field(cross, 0, ids(0), [own])
    a1 = add_field(cross, 1, ids(0), [own])
    own_b = after(own, a0)[1:2]
    x, pa, na, own_b, a0, a1 = barrier(x, pa, na, own_b, a0, a1)

    pb = swap(own_b, "row", 4)
    ga = swap(pa, "row", 2)
    xpa = swap(pa, "row", 1)
    xna = swap(na, "row", 1)
    a0 = add_field(cross, 0, ids(1, 2, 4), [x, na, pa], a0)
    a1 = add_field(cross, 1, ids(1), [x], a1)
    x_b = x[1:2]
    pb, ga, xpa, xna, a0, a1, x_b, own_b = barrier(pb, ga, xpa, xna, a0, a1, x_b, own_b)

    gb = swap(pb, "row", 2)
    xga = swap(ga, "row", 1)
    xpb = swap(pb, "row", 1)
    nb = swap(own_b, "row", 2)
    b0 = add_field(cross, 0, ids(3, 5, 6), [xna, xpa, ga], a0)
    a1 = add_field(cross, 1, ids(4), [pb], a1)
    plan = [
        (0, 2, [(0, 0), (1, 1), (2, 2), (3, 3), (4, 4), (5, 5), (6, 6)]),
        (1, 2, [(0, 0), (1, 1), (4, 7)]),
    ]
    mine = pick_rows(after(masks, b0), plan, [own, x, na, xna, pa, xpa, ga, pb])
    gb, nb, xga, xpb, b0, a1, x_b, mine = barrier(gb, nb, xga, xpb, b0, a1, x_b, mine)

    other = swap(mine, "col", 1)
    other_xga = swap(xga, "col", 1)
    d = swap(x_b, "row", 2)
    xgb = swap(gb, "row", 1)
    b1 = add_field(cross, 1, ids(6, 5, 2), [gb, xpb, nb], a1)
    plan = [(0, 1, [(6, 0), (5, 1), (2, 2)])]
    mine_b = pick_rows(after(masks, b1), plan, [gb, xpb, nb])
    whole = jnp.where(holds, 0, 1)
    where = jnp.where(masks == 7, jnp.where(holds, 2, 3), whole)
    c0 = finish(
        cross, 0, jnp.concatenate([ids(7), where]), [xga], b0, [mine, other], [xga, other_xga]
    )
    d, xgb, b1, mine_b, c0 = barrier(d, xgb, b1, mine_b, c0)

    other_b, other_d, other_xgb = (swap(piece, "col", 1) for piece in (mine_b, d, xgb))
    field = add_field(cross, 1, ids(3, 7), [d, xgb], b1)
    where = jnp.full_like(masks, whole)
    for k, mask in enumerate((6, 5, 2)):
        where = jnp.where(masks == mask, jnp.where(holds, 2 + k, 5), where)
    where = jnp.where(masks == 3, jnp.where(holds, 6, 7), where)
    where = jnp.where(masks == 7, jnp.where(holds, 8, 9), where)
    singles = [gb, xpb, nb, other_b, d, other_d, xgb, other_xgb]
    c1 = dot_rows(1, where, field, [mine, other], singles)
    return jnp.stack([c0, c1])


def numer_by_gather(cross, replicas):
    rows, half = cross.shape[2], cross.shape[3]
    row_index, col_index = lax.axis_index("row"), lax.axis_index("col")
    first_row = row_index * rows
    holder = first_row // half
    whole = lax.all_gather(replicas, "row", axis=3, tiled=True)[:, :, 0]
    parts = jnp.einsum("fark,fbks->fabrs", cross, whole, preferred_element_type=jnp.float32)
    field = jnp.stack([parts[:, 0, 0] - parts[:, 1, 1], parts[:, 0, 1] + parts[:, 1, 0]], axis=1)
    own_rows = lax.dynamic_slice_in_dim(whole, first_row - holder * half, rows, 2)
    block_rows = jnp.where(holder == col_index, own_rows, swap(own_rows, "col", 1))
    return jnp.sum(block_rows.astype(jnp.float32) * field, axis=(1, 2))


def body(cross_spectra, replicas, tile_order):
    fnum = cross_spectra.shape[0]
    sources = replicas.shape[4]
    own = replicas[:, :, 0].astype(jnp.float32)
    norms = jnp.sum(own * own, axis=(1, 2))
    doubling = (
        lax.axis_size("row") == 8
        and replicas.shape[3] % 128 == 0
        and cross_spectra.shape[2] == 2 * replicas.shape[3]
    )
    numer = (numer_by_swaps if doubling else numer_by_gather)(cross_spectra, replicas)
    sums = sum_all(jnp.concatenate([numer, norms]))
    numer, norms = sums[:fnum], sums[fnum:]
    beam = numer / (norms + 1e-06)
    width = sources // lax.axis_size("col")
    beam_half = lax.dynamic_slice_in_dim(beam, lax.axis_index("col") * width, width, 1)
    peak = jnp.max(jnp.abs(beam), axis=1) + 1e-06
    count = tile_order.shape[0]
    picker = (tile_order[:, None] == jnp.arange(count, dtype=jnp.int32)[None, :]).astype(jnp.float32)
    tiles = beam.reshape(fnum, count, sources // count)
    refined = (
        jnp.einsum("tu,fup->ftp", picker, tiles, precision=lax.Precision.HIGHEST)
        / peak[:, None, None]
    )
    return (beam_half, refined)


def solution(mesh):
    in_specs = (P("groups", None, "row", "col"), P("groups", None, "col", "row", None), P("groups"))
    out_specs = (P("groups", "col"), P("groups", None, None))
    return jax.shard_map(body, mesh=mesh, in_specs=in_specs, out_specs=out_specs, check_vma=False)
```

```python
import functools
import math

import jax
import jax.numpy as jnp
from jax import lax
from jax.experimental import pallas as pl
from jax.experimental.pallas import tpu as pltpu
from jax.sharding import PartitionSpec as P

VMEM_LIMIT = 63 * 1024 * 1024
HINT = pl.CostEstimate(flops=1, bytes_accessed=1, transcendentals=0)


def swap(value, axis, mask):
    size = math.prod(lax.axis_size(name) for name in (axis if isinstance(axis, tuple) else (axis,)))
    return lax.ppermute(value, axis, [(source, source ^ mask) for source in range(size)])


def after(value, *others):
    return lax.optimization_barrier((value, *others))[0]


def sum_all(value):
    axes = ("row", "col")
    size = lax.axis_size("row") * lax.axis_size("col")
    if size > 16 or size & (size - 1):
        return lax.psum(value, axes)
    mask = 1
    while mask < size:
        near = value + swap(value, axes, mask)
        if 2 * mask < size:
            near = near + (swap(value, axes, 2 * mask) + swap(value, axes, 3 * mask))
        value, mask = near, 4 * mask
    return value


def piece_copies(freq, ids, cross, ref, k, left, right, sem):
    width = ref.shape[2]
    columns = pl.ds(pl.multiple_of(ids[k] * width, width), width)
    which = freq if ref.shape[0] > 1 else 0
    low, high = pl.ds(0, width), pl.ds(width, width)
    return [
        pltpu.make_async_copy(ref.at[which, 0], right.at[k, 0, low], sem.at[k, 0]),
        pltpu.make_async_copy(ref.at[which, 1], right.at[k, 1, low], sem.at[k, 1]),
        pltpu.make_async_copy(cross.at[freq, 0, :, columns], left.at[k, :, low], sem.at[k, 2]),
        pltpu.make_async_copy(cross.at[freq, 1, :, columns], left.at[k, :, high], sem.at[k, 3]),
    ]


def accumulate(freq, ids, first, cross, w_refs, total, left, right, sem, field, tot, tot_sem):
    piece, part = pl.program_id(0), pl.program_id(1)
    copies = [
        piece_copies(freq, ids, cross, ref, k, left, right, sem) for k, ref in enumerate(w_refs)
    ]

    for k, group in enumerate(copies):

        @pl.when((piece == k) & (part == 0))
        def _(k=k, group=group):
            if k == 0:
                for copy in group:
                    copy.start()
            for copy in group:
                copy.wait()
            if k + 1 < len(copies):
                for copy in copies[k + 1]:
                    copy.start()
            if k == 0:
                if total is not None:
                    pltpu.make_async_copy(total, tot, tot_sem.at[0]).start()
                first()
            width = right.shape[2] // 2
            right[k, 0, width:] = -right[k, 1, :width]
            right[k, 1, width:] = right[k, 0, :width]

    dot = functools.partial(jnp.dot, preferred_element_type=jnp.float32)

    @pl.when(piece == 0)
    def _():
        field[part] = dot(left[piece], right[piece, part])

    @pl.when(piece > 0)
    def _():
        field[part] += dot(left[piece], right[piece, part])

    if total is not None:

        @pl.when((piece == len(w_refs) - 1) & (part == 0))
        def _():
            pltpu.make_async_copy(total, tot, tot_sem.at[0]).wait()


def field_kernel(freq, count, ids, cross, *refs):
    w_refs, (total, out, left, right, sem, field, tot, tot_sem) = refs[:count], refs[count:]
    accumulate(
        freq, ids, lambda: None, cross, w_refs, total, left, right, sem, field, tot, tot_sem
    )
    part = pl.program_id(1)

    @pl.when(pl.program_id(0) == count - 1)
    def _():
        out[0] = field[part] + tot[part]


def first_kernel(freq, count, ids, cross, *refs):
    w_refs, (out, left, right, sem, field) = refs[:count], refs[count:]
    accumulate(freq, ids, lambda: None, cross, w_refs, None, left, right, sem, field, None, None)

    @pl.when(pl.program_id(0) == count - 1)
    def _():
        out[0] = field[pl.program_id(1)]


def start_rows(freq, ids, base, whole, singles, rows, sem):
    width = rows.shape[1] // 2
    for slot in range(2):
        here = pl.ds(slot * width, width)
        views = [ref.at[freq, :, here] for ref in whole] + [ref.at[0] for ref in singles]
        for k, source in enumerate(views):

            @pl.when(ids[base + slot] == k)
            def _(source=source, slot=slot, here=here):
                pltpu.make_async_copy(source, rows.at[:, here], sem.at[slot]).start()


def wait_rows(slot, singles, rows, sem):
    width = rows.shape[1] // 2
    here = pl.ds(slot * width, width)
    pltpu.make_async_copy(singles[0].at[0], rows.at[:, here], sem.at[slot]).wait()


def fold(rows, field):
    product = rows.astype(jnp.float32) * field
    return jnp.sum(product.reshape(-1, 8, product.shape[-1]), axis=0)


def numer_kernel(freq, count, ids, cross, *refs):
    w_refs, total, whole = refs[:count], refs[count], refs[count + 1 : count + 3]
    singles = refs[count + 3 : -9]
    out, left, right, sem, field, tot, tot_sem, rows, row_sem = refs[-9:]
    begin = lambda: start_rows(freq, ids, count, whole, singles, rows, row_sem)
    accumulate(freq, ids, begin, cross, w_refs, total, left, right, sem, field, tot, tot_sem)
    part = pl.program_id(1)
    last = pl.program_id(0) == count - 1

    @pl.when(last & (part == 0))
    def _():
        out[...] = jnp.zeros_like(out)
        for slot in range(2):
            wait_rows(slot, singles, rows, row_sem)

    @pl.when(last)
    def _():
        out[...] += fold(rows[part], field[part] + tot[part])


def dot_kernel(freq, ids, field, before, norms, *refs):
    whole, singles, (out, rows, sem, sums) = refs[:2], refs[2:-4], refs[-4:]
    slot, part = pl.program_id(0), pl.program_id(1)
    width = field.shape[1]

    @pl.when((slot == 0) & (part == 0))
    def _():
        sums[...] = jnp.zeros_like(sums)
        start_rows(freq, ids, 0, whole, singles, rows, sem)

    for k in range(2):

        @pl.when((slot == k) & (part == 0))
        def _(k=k):
            wait_rows(k, singles, rows, sem)

    here = pl.ds(pl.multiple_of(slot * width, width), width)
    sums[...] += fold(rows[part, here], field[0])

    @pl.when((slot == 1) & (part == 1))
    def _():
        out[0:1] = jnp.sum(before[...], axis=0, keepdims=True)
        out[1:2] = jnp.sum(sums[...], axis=0, keepdims=True)
        out[2:4] = norms[...]


ANYWHERE = pl.BlockSpec(memory_space=pl.ANY)


def call(kernel, cross, freq, ids, pieces, rest, out_shape, out_spec, has_total, scratch):
    rows, (width, sources) = cross.shape[2], pieces[0].shape[2:]
    count, dtype = len(pieces), pieces[0].dtype
    total = [pltpu.VMEM((2, rows, sources), jnp.float32), pltpu.SemaphoreType.DMA((1,))]
    return pl.pallas_call(
        functools.partial(kernel, freq, count),
        out_shape=out_shape,
        grid_spec=pltpu.PrefetchScalarGridSpec(
            num_scalar_prefetch=1,
            grid=(count, 2),
            in_specs=[ANYWHERE] * (1 + count + len(rest)),
            out_specs=out_spec,
            scratch_shapes=[
                pltpu.VMEM((count, rows, 2 * width), dtype),
                pltpu.VMEM((count, 2, 2 * width, sources), dtype),
                pltpu.SemaphoreType.DMA((count, 4)),
                pltpu.VMEM((2, rows, sources), jnp.float32),
                *(total if has_total else []),
                *scratch,
            ],
        ),
        compiler_params=pltpu.CompilerParams(vmem_limit_bytes=VMEM_LIMIT),
        cost_estimate=HINT,
    )(ids, cross, *pieces, *rest)


def add_field(cross, freq, ids, pieces, total=None):
    rows, sources = cross.shape[2], pieces[0].shape[3]
    count = len(pieces)
    return call(
        first_kernel if total is None else field_kernel,
        cross,
        freq,
        ids,
        pieces,
        [] if total is None else [total],
        jax.ShapeDtypeStruct((2, rows, sources), jnp.float32),
        pl.BlockSpec(
            (1, rows, sources), lambda p, part, ids: (jnp.where(p == count - 1, part, 0), 0, 0)
        ),
        total is not None,
        [],
    )


def row_scratch(rows, sources, dtype):
    return [pltpu.VMEM((2, rows, sources), dtype), pltpu.SemaphoreType.DMA((2,))]


def finish(cross, freq, ids, pieces, total, whole, singles):
    rows, sources = cross.shape[2], pieces[0].shape[3]
    return call(
        numer_kernel,
        cross,
        freq,
        ids,
        pieces,
        [total, *whole, *singles],
        jax.ShapeDtypeStruct((8, sources), jnp.float32),
        pl.BlockSpec((8, sources), lambda p, part, ids: (0, 0)),
        True,
        row_scratch(rows, sources, pieces[0].dtype),
    )


def dot_rows(freq, ids, field, before, norms, whole, singles):
    _, rows, sources = field.shape
    return pl.pallas_call(
        functools.partial(dot_kernel, freq),
        out_shape=jax.ShapeDtypeStruct((4, sources), jnp.float32),
        grid_spec=pltpu.PrefetchScalarGridSpec(
            num_scalar_prefetch=1,
            grid=(2, 2),
            in_specs=[
                pl.BlockSpec((1, rows // 2, sources), lambda slot, part, ids: (part, slot, 0)),
                pl.BlockSpec((8, sources), lambda slot, part, ids: (0, 0)),
                pl.BlockSpec((2, sources), lambda slot, part, ids: (0, 0)),
            ]
            + [ANYWHERE] * (2 + len(singles)),
            out_specs=pl.BlockSpec((4, sources), lambda slot, part, ids: (0, 0)),
            scratch_shapes=[
                *row_scratch(rows, sources, whole[0].dtype),
                pltpu.VMEM((8, sources), jnp.float32),
            ],
        ),
        compiler_params=pltpu.CompilerParams(vmem_limit_bytes=VMEM_LIMIT),
        cost_estimate=HINT,
    )(ids, field, before, norms, *whole, *singles)


def pick_kernel(plan, ids, *refs):
    pieces, out, sem = refs[:-2], refs[-2], refs[-1]
    width = pieces[0].shape[2]
    for wait in (False, True):
        for place, (freq, slots, choices) in enumerate(plan):
            for slot in range(2):
                for mask, k in choices:

                    @pl.when(ids[slot] == mask)
                    def _(place=place, freq=freq, slots=slots, slot=slot, k=k):
                        piece = pieces[k]
                        source = piece.at[freq if piece.shape[0] > 1 else 0]
                        start = slot * width if slots == 2 else 0
                        copy = pltpu.make_async_copy(
                            source, out.at[place, :, pl.ds(start, width)], sem.at[place, slot]
                        )
                        copy.wait() if wait else copy.start()


def pick_rows(ids, plan, pieces):
    _, _, width, sources = pieces[0].shape
    shape = (len(plan), 2, plan[0][1] * width, sources)
    return pl.pallas_call(
        functools.partial(pick_kernel, plan),
        out_shape=jax.ShapeDtypeStruct(shape, pieces[0].dtype),
        grid_spec=pltpu.PrefetchScalarGridSpec(
            num_scalar_prefetch=1,
            grid=(1,),
            in_specs=[ANYWHERE] * len(pieces),
            out_specs=pl.BlockSpec(shape, lambda i, ids: (0, 0, 0, 0)),
            scratch_shapes=[pltpu.SemaphoreType.DMA((len(plan), 2))],
        ),
        compiler_params=pltpu.CompilerParams(vmem_limit_bytes=VMEM_LIMIT),
        cost_estimate=HINT,
    )(ids, *pieces)


def sums_by_swaps(cross, replicas, norms):
    rows, half = cross.shape[2], cross.shape[3]
    width = replicas.shape[3]
    me = lax.axis_index("row").astype(jnp.int32)
    col = lax.axis_index("col").astype(jnp.int32)
    holder = me * rows // half
    first = (me * rows - holder * half) // width
    masks = jnp.stack([first ^ me, (first + 1) ^ me])
    holds = holder == col
    ids = lambda *wanted: me ^ jnp.array(wanted, jnp.int32)
    barrier = lambda *values: lax.optimization_barrier(values)
    own = replicas[:, :, 0]
    numbers = [ids(0), ids(1, 2, 4), ids(1), ids(3, 5, 6), ids(4), ids(6, 5, 2), ids(3, 7)]

    whole = jnp.where(holds, 0, 1)
    where_a = jnp.where(masks == 7, jnp.where(holds, 2, 3), whole)
    where_b = jnp.full_like(masks, whole)
    for k, mask in enumerate((6, 5, 2)):
        where_b = jnp.where(masks == mask, jnp.where(holds, 2 + k, 5), where_b)
    where_b = jnp.where(masks == 3, jnp.where(holds, 6, 7), where_b)
    where_b = jnp.where(masks == 7, jnp.where(holds, 8, 9), where_b)
    numbers += [jnp.concatenate([ids(7), where_a]), where_b, masks]

    own_a = own[0:1]
    x = swap(after(own, own_a), "row", 1)
    pa = swap(own_a, "row", 4)
    na = swap(own_a, "row", 2)
    a0 = add_field(cross, 0, numbers[0], [own])
    a1 = add_field(cross, 1, numbers[0], [own])
    own_b = after(own, a0)[1:2]
    pb = swap(after(own_b, pa), "row", 4)
    x, pa, na, own_b, a0, a1, norms, *numbers = barrier(
        x, pa, na, own_b, a0, a1, norms, *numbers
    )
    _, ids_a0, ids_a1, ids_b0, ids_b1, ids_c1, ids_d1, ids_c0, where_b, masks = numbers

    ga = swap(pa, "row", 2)
    xpa = swap(pa, "row", 1)
    xna = swap(na, "row", 1)
    a0 = add_field(cross, 0, ids_a0, [x, na, pa], a0)
    a1 = add_field(cross, 1, ids_a1, [x], a1)
    x_b = x[1:2]
    pb, ga, xpa, xna, a0, a1, x_b, own_b = barrier(pb, ga, xpa, xna, a0, a1, x_b, own_b)

    gb = swap(pb, "row", 2)
    xga = swap(ga, "row", 1)
    xpb = swap(pb, "row", 1)
    nb = swap(own_b, "row", 2)
    b0 = add_field(cross, 0, ids_b0, [xna, xpa, ga], a0)
    a1 = add_field(cross, 1, ids_b1, [pb], a1)
    plan = [
        (0, 2, [(0, 0), (1, 1), (2, 2), (3, 3), (4, 4), (5, 5), (6, 6)]),
        (1, 2, [(0, 0), (1, 1), (4, 7)]),
    ]
    mine = pick_rows(after(masks, b0), plan, [own, x, na, xna, pa, xpa, ga, pb])
    gb, nb, xga, xpb, b0, a1, x_b, mine = barrier(gb, nb, xga, xpb, b0, a1, x_b, mine)

    other = swap(mine, "col", 1)
    other_xga = swap(xga, "col", 1)
    d = swap(x_b, "row", 2)
    xgb = swap(gb, "row", 1)
    b1 = add_field(cross, 1, ids_c1, [gb, xpb, nb], a1)
    plan = [(0, 1, [(6, 0), (5, 1), (2, 2)])]
    mine_b = pick_rows(after(masks, b1), plan, [gb, xpb, nb])
    c0 = finish(cross, 0, ids_c0, [xga], b0, [mine, other], [xga, other_xga])
    d, xgb, b1, mine_b, c0 = barrier(d, xgb, b1, mine_b, c0)

    other_b, other_d, other_xgb = (swap(piece, "col", 1) for piece in (mine_b, d, xgb))
    field = add_field(cross, 1, ids_d1, [d, xgb], b1)
    singles = [gb, xpb, nb, other_b, d, other_d, xgb, other_xgb]
    return dot_rows(1, where_b, field, c0, norms, [mine, other], singles)


def sums_by_gather(cross, replicas, norms):
    rows, half = cross.shape[2], cross.shape[3]
    row_index, col_index = lax.axis_index("row"), lax.axis_index("col")
    first_row = row_index * rows
    holder = first_row // half
    whole = lax.all_gather(replicas, "row", axis=3, tiled=True)[:, :, 0]
    parts = jnp.einsum("fark,fbks->fabrs", cross, whole, preferred_element_type=jnp.float32)
    field = jnp.stack([parts[:, 0, 0] - parts[:, 1, 1], parts[:, 0, 1] + parts[:, 1, 0]], axis=1)
    own_rows = lax.dynamic_slice_in_dim(whole, first_row - holder * half, rows, 2)
    block_rows = jnp.where(holder == col_index, own_rows, swap(own_rows, "col", 1))
    numer = jnp.sum(block_rows.astype(jnp.float32) * field, axis=(1, 2))
    return jnp.concatenate([numer, norms])


def body(cross_spectra, replicas, tile_order):
    fnum = cross_spectra.shape[0]
    sources = replicas.shape[4]
    own = replicas[:, :, 0].astype(jnp.float32)
    norms = jnp.sum(own * own, axis=(1, 2))
    doubling = (
        lax.axis_size("row") == 8
        and fnum == 2
        and replicas.shape[3] % 128 == 0
        and cross_spectra.shape[2] == 2 * replicas.shape[3]
    )
    sums = (sums_by_swaps if doubling else sums_by_gather)(cross_spectra, replicas, norms)
    sums = sum_all(sums)
    numer, norms = sums[:fnum], sums[fnum:]
    beam = numer / (norms + 1e-06)
    width = sources // lax.axis_size("col")
    beam_half = lax.dynamic_slice_in_dim(beam, lax.axis_index("col") * width, width, 1)
    peak = jnp.max(jnp.abs(beam), axis=1) + 1e-06
    count = tile_order.shape[0]
    picker = (tile_order[:, None] == jnp.arange(count, dtype=jnp.int32)[None, :]).astype(jnp.float32)
    tiles = beam.reshape(fnum, count, sources // count)
    refined = (
        jnp.einsum("tu,fup->ftp", picker, tiles, precision=lax.Precision.HIGHEST)
        / peak[:, None, None]
    )
    return (beam_half, refined)


def solution(mesh):
    in_specs = (P("groups", None, "row", "col"), P("groups", None, "col", "row", None), P("groups"))
    out_specs = (P("groups", "col"), P("groups", None, None))
    return jax.shard_map(body, mesh=mesh, in_specs=in_specs, out_specs=out_specs, check_vma=False)
```

```python
import functools
import math

import jax
import jax.numpy as jnp
from jax import lax
from jax.experimental import pallas as pl
from jax.experimental.pallas import tpu as pltpu
from jax.sharding import PartitionSpec as P

VMEM_LIMIT = 63 * 1024 * 1024
HINT = pl.CostEstimate(flops=1, bytes_accessed=1, transcendentals=0)
ANYWHERE = pl.BlockSpec(memory_space=pl.ANY)


def swap(value, axis, mask):
    size = math.prod(lax.axis_size(name) for name in (axis if isinstance(axis, tuple) else (axis,)))
    return lax.ppermute(value, axis, [(source, source ^ mask) for source in range(size)])


def swap_some(value, mask, wanted):
    size = lax.axis_size("row")
    return lax.ppermute(value, "row", [(k, k ^ mask) for k in range(size) if wanted(k)])


def middle(index):
    return (index // 2) % 4 in (1, 2)


def end(index):
    return not middle(index)


def after(value, *others):
    return lax.optimization_barrier((value, *others))[0]


def sum_all(value):
    axes = ("row", "col")
    size = lax.axis_size("row") * lax.axis_size("col")
    if size > 16 or size & (size - 1):
        return lax.psum(value, axes)
    mask = 1
    while mask < size:
        near = value + swap(value, axes, mask)
        if 2 * mask < size:
            near = near + (swap(value, axes, 2 * mask) + swap(value, axes, 3 * mask))
        value, mask = near, 4 * mask
    return value


def dot(a, b):
    return jnp.dot(a, b, preferred_element_type=jnp.float32)


def at_freq(ref, freq):
    return ref.at[freq if ref.shape[0] > 1 else 0]


def weight_copies(freq, ref, right, sem):
    low = pl.ds(0, ref.shape[2])
    source = at_freq(ref, freq)
    return [
        pltpu.make_async_copy(source.at[0], right.at[0, low], sem.at[0]),
        pltpu.make_async_copy(source.at[1], right.at[1, low], sem.at[1]),
    ]


def spread(right):
    width = right.shape[1] // 2
    right[0, width:] = -right[1, :width]
    right[1, width:] = right[0, :width]


def spectra_copies(freq, column, cross, left, sem):
    width = left.shape[1] // 2
    columns = pl.ds(pl.multiple_of(column * width, width), width)
    return [
        pltpu.make_async_copy(
            cross.at[freq, part, :, columns], left.at[:, pl.ds(part * width, width)], sem.at[part]
        )
        for part in range(2)
    ]


def field_kernel(freq, count, has_total, ids, cross, *refs):
    w_refs, refs = refs[:count], refs[count:]
    total, refs = (refs[0], refs[1:]) if has_total else (None, refs)
    out, left, right, l_sem, w_sem, field, tot, tot_sem = refs
    piece, part = pl.program_id(0), pl.program_id(1)
    copies = [
        weight_copies(freq, ref, right.at[k], w_sem.at[k])
        + spectra_copies(freq, ids[k], cross, left.at[k], l_sem.at[k])
        for k, ref in enumerate(w_refs)
    ]
    for k, group in enumerate(copies):

        @pl.when((piece == k) & (part == 0))
        def _(k=k, group=group):
            if k == 0:
                for copy in group:
                    copy.start()
            for copy in group:
                copy.wait()
            if k + 1 < count:
                for copy in copies[k + 1]:
                    copy.start()
            if k == 0 and has_total:
                pltpu.make_async_copy(total, tot, tot_sem.at[0]).start()
            spread(right.at[k])

    last = piece == count - 1
    if count > 1:

        @pl.when(piece == 0)
        def _():
            field[part] = dot(left[piece], right[piece, part])

        @pl.when((piece > 0) & (piece < count - 1))
        def _():
            field[part] += dot(left[piece], right[piece, part])

    @pl.when(last)
    def _():
        value = dot(left[piece], right[piece, part])
        if count > 1:
            value += field[part]
        if has_total:

            @pl.when(part == 0)
            def _():
                pltpu.make_async_copy(total, tot, tot_sem.at[0]).wait()

            value += tot[part]
        out[0] = value


def add_field(cross, freq, ids, pieces, total=None):
    rows, (width, sources) = cross.shape[2], pieces[0].shape[2:]
    count, dtype = len(pieces), pieces[0].dtype
    has_total = total is not None
    return pl.pallas_call(
        functools.partial(field_kernel, freq, count, has_total),
        out_shape=jax.ShapeDtypeStruct((2, rows, sources), jnp.float32),
        grid_spec=pltpu.PrefetchScalarGridSpec(
            num_scalar_prefetch=1,
            grid=(count, 2),
            in_specs=[ANYWHERE] * (1 + count + has_total),
            out_specs=pl.BlockSpec(
                (1, rows, sources), lambda p, part, ids: (jnp.where(p == count - 1, part, 0), 0, 0)
            ),
            scratch_shapes=[
                pltpu.VMEM((count, rows, 2 * width), dtype),
                pltpu.VMEM((count, 2, 2 * width, sources), dtype),
                pltpu.SemaphoreType.DMA((count, 2)),
                pltpu.SemaphoreType.DMA((count, 2)),
                pltpu.VMEM((2, rows, sources), jnp.float32),
                pltpu.VMEM((2, rows, sources), jnp.float32),
                pltpu.SemaphoreType.DMA((1,)),
            ],
        ),
        compiler_params=pltpu.CompilerParams(vmem_limit_bytes=VMEM_LIMIT),
        cost_estimate=HINT,
    )(ids, cross, *pieces, *([total] if has_total else []))


def start_rows(freq, ids, base, refs, rows, sem):
    width = rows.shape[1] // 2
    views = []
    for picked, *pieces in (refs[:4], refs[4:]):
        views += [picked.at[freq, :, pl.ds(slot * width, width)] for slot in range(2)]
        views += [at_freq(ref, freq) for ref in pieces]
    for slot in range(2):
        here = pl.ds(slot * width, width)
        for k, source in enumerate(views):

            @pl.when(ids[base + slot] == k)
            def _(source=source, slot=slot, here=here):
                pltpu.make_async_copy(source, rows.at[:, here], sem.at[slot]).start()


def wait_rows(freq, slot, refs, rows, sem):
    width = rows.shape[1] // 2
    source = refs[0].at[freq, :, pl.ds(0, width)]
    here = rows.at[:, pl.ds(slot * width, width)]
    pltpu.make_async_copy(source, here, sem.at[slot]).wait()


def fold(rows, field):
    product = rows.astype(jnp.float32) * field
    return jnp.sum(product.reshape(-1, 8, product.shape[-1]), axis=0)


def late_kernel(freq, ids, cross, w5, w6, w7, block_re, block_im, total, *refs):
    row_refs, refs = refs[:8], refs[8:]
    sums, field_out, left, right, l_sem, w_sem, field, tot, sem, rows, row_sem = refs
    step, part = pl.program_id(0), pl.program_id(1)
    width = w5.shape[2]
    first = weight_copies(freq, w5, right.at[0], w_sem.at[0]) + spectra_copies(
        freq, ids[0], cross, left.at[0], l_sem.at[0]
    )
    six = weight_copies(freq, w6, right.at[1], w_sem.at[1])
    seven = weight_copies(freq, w7, right.at[1], w_sem.at[1])
    second = spectra_copies(freq, ids[1], cross, left.at[1], l_sem.at[1])
    third = [
        pltpu.make_async_copy(
            ref.at[0, min(k, ref.shape[1] - 1)],
            left.at[2, :, pl.ds(k * width, width)],
            l_sem.at[2, k],
        )
        for k, ref in enumerate((block_re, block_im))
    ]
    total_copy = pltpu.make_async_copy(total, tot, sem.at[0])
    out_copies = [
        pltpu.make_async_copy(field.at[k], field_out.at[k], sem.at[1 + k]) for k in range(2)
    ]

    @pl.when((step == 0) & (part == 0))
    def _():
        sums[...] = jnp.zeros_like(sums)
        for copy in first:
            copy.start()
        for copy in first:
            copy.wait()
        for copy in second:
            copy.start()

        @pl.when(ids[2] == 1)
        def _():
            for copy in seven:
                copy.start()

        @pl.when(ids[2] == 0)
        def _():
            for copy in six:
                copy.start()

        total_copy.start()
        spread(right.at[0])

    @pl.when((step == 1) & (part == 0))
    def _():
        for copy in second + six:
            copy.wait()
        for copy in third:
            copy.start()
        start_rows(freq, ids, 5, row_refs, rows, row_sem)
        total_copy.wait()
        spread(right.at[1])

    @pl.when((step == 2) & (part == 0))
    def _():
        for copy in third:
            copy.wait()
        for slot in range(2):
            wait_rows(freq, slot, row_refs, rows, row_sem)

    @pl.when(step == 0)
    def _():
        field[part] = dot(left[0], right[0, part])

    for k in range(2):

        @pl.when((step == 1) & (part == k))
        def _(k=k):
            field[k] = field[k] + tot[k] + dot(left[1], right[1, k])
            out_copies[k].start()

    @pl.when(step == 2)
    def _():
        sums[...] += fold(rows[part], dot(left[2], right[0, part]))

    @pl.when((step == 2) & (part == 1))
    def _():
        for copy in out_copies:
            copy.wait()


def add_late(cross, freq, ids, pieces, blocks, total, row_refs):
    rows, (width, sources) = cross.shape[2], pieces[0].shape[2:]
    dtype = pieces[0].dtype
    return pl.pallas_call(
        functools.partial(late_kernel, freq),
        out_shape=(
            jax.ShapeDtypeStruct((8, sources), jnp.float32),
            jax.ShapeDtypeStruct(total.shape, total.dtype),
        ),
        grid_spec=pltpu.PrefetchScalarGridSpec(
            num_scalar_prefetch=1,
            grid=(3, 2),
            in_specs=[ANYWHERE] * (7 + len(row_refs)),
            out_specs=(pl.BlockSpec((8, sources), lambda step, part, ids: (0, 0)), ANYWHERE),
            scratch_shapes=[
                pltpu.VMEM((3, rows, 2 * width), dtype),
                pltpu.VMEM((2, 2, 2 * width, sources), dtype),
                pltpu.SemaphoreType.DMA((3, 2)),
                pltpu.SemaphoreType.DMA((2, 2)),
                pltpu.VMEM((2, rows, sources), jnp.float32),
                pltpu.VMEM((2, rows, sources), jnp.float32),
                pltpu.SemaphoreType.DMA((3,)),
                pltpu.VMEM((2, rows, sources), dtype),
                pltpu.SemaphoreType.DMA((2,)),
            ],
        ),
        compiler_params=pltpu.CompilerParams(vmem_limit_bytes=VMEM_LIMIT),
        cost_estimate=HINT,
    )(ids, cross, *pieces, *blocks, total, *row_refs)


def dot_kernel(ids, norms, *refs):
    groups, (out, rows, row_sem, field, sem) = (refs[:10], refs[10:20]), refs[20:]
    width = rows.shape[2] // 2
    pairs = [(slot, part) for slot in range(2) for part in range(2)]
    copies = {}
    for freq, (field_ref, _, *row_refs) in enumerate(groups):
        start_rows(freq, ids, 3, row_refs, rows.at[freq], row_sem.at[freq])
        for slot, part in pairs:
            here = pl.ds(slot * width, width)
            copies[freq, slot, part] = pltpu.make_async_copy(
                field_ref.at[part, here], field.at[freq, part, here], sem.at[freq, 2 * slot + part]
            )
            copies[freq, slot, part].start()
    for freq, (_, sums_ref, *row_refs) in enumerate(groups):
        sums = sums_ref[...]
        for slot, part in pairs:
            if part == 0:
                wait_rows(freq, slot, row_refs, rows.at[freq], row_sem.at[freq])
            copies[freq, slot, part].wait()
            here = slice(slot * width, (slot + 1) * width)
            sums += fold(rows[freq, part, here], field[freq, part, here])
        out[freq : freq + 1] = jnp.sum(sums, axis=0, keepdims=True)
    out[2:4] = norms[...]


def dot_rows(ids, norms, groups):
    _, rows, sources = groups[0][0].shape
    whole = lambda shape: pl.BlockSpec(shape, lambda i, ids: (0, 0))
    return pl.pallas_call(
        dot_kernel,
        out_shape=jax.ShapeDtypeStruct((4, sources), jnp.float32),
        grid_spec=pltpu.PrefetchScalarGridSpec(
            num_scalar_prefetch=1,
            grid=(1,),
            in_specs=[whole((2, sources))] + [ANYWHERE, whole((8, sources)), *[ANYWHERE] * 8] * 2,
            out_specs=whole((4, sources)),
            scratch_shapes=[
                pltpu.VMEM((2, 2, rows, sources), groups[0][2].dtype),
                pltpu.SemaphoreType.DMA((2, 2)),
                pltpu.VMEM((2, 2, rows, sources), jnp.float32),
                pltpu.SemaphoreType.DMA((2, 4)),
            ],
        ),
        compiler_params=pltpu.CompilerParams(vmem_limit_bytes=VMEM_LIMIT),
        cost_estimate=HINT,
    )(ids, norms, *groups[0], *groups[1])


def copy_call(kernel, ids, shape, dtype, args, copies):
    return pl.pallas_call(
        kernel,
        out_shape=jax.ShapeDtypeStruct(shape, dtype),
        grid_spec=pltpu.PrefetchScalarGridSpec(
            num_scalar_prefetch=1,
            grid=(1,),
            in_specs=[ANYWHERE] * len(args),
            out_specs=pl.BlockSpec(shape, lambda i, ids: (0,) * len(shape)),
            scratch_shapes=[pltpu.SemaphoreType.DMA((copies,))],
        ),
        compiler_params=pltpu.CompilerParams(vmem_limit_bytes=VMEM_LIMIT),
        cost_estimate=HINT,
    )(ids, *args)


def block_kernel(freq, first, ids, cross, out, sem):
    width = out.shape[3]
    columns = pl.ds(pl.multiple_of(ids[0] * width, width), width)
    copies = [
        pltpu.make_async_copy(cross.at[freq, first + k, :, columns], out.at[0, k], sem.at[k])
        for k in range(out.shape[1])
    ]
    for copy in copies:
        copy.start()
    for copy in copies:
        copy.wait()


def take_block(cross, freq, parts, ids, width):
    shape = (1, len(parts), cross.shape[2], width)
    kernel = functools.partial(block_kernel, freq, parts[0])
    return copy_call(kernel, ids, shape, cross.dtype, [cross], len(parts))


def pair_kernel(ids, own, x, n, m, out, sem):
    width = own.shape[2]
    for pair in (0, 1):
        copies = [
            pltpu.make_async_copy(
                ref.at[freq], out.at[freq, :, pl.ds(slot * width, width)], sem.at[2 * freq + slot]
            )
            for freq in range(out.shape[0])
            for slot, ref in enumerate(((own, x), (n, m))[pair])
        ]

        @pl.when(ids[0] == pair)
        def _(copies=copies):
            for copy in copies:
                copy.start()
            for copy in copies:
                copy.wait()


def take_pair(ids, own, x, n, m):
    freqs, _, width, sources = own.shape
    shape = (freqs, 2, 2 * width, sources)
    return copy_call(pair_kernel, ids, shape, own.dtype, [own, x, n, m], 2 * freqs)


def either_kernel(freqs, ids, first, second, out, sem):
    for k, ref in enumerate((first, second)):

        @pl.when(ids[0] == k)
        def _(ref=ref):
            copies = [
                pltpu.make_async_copy(at_freq(ref, freq), out.at[slot], sem.at[slot])
                for slot, freq in enumerate(freqs)
            ]
            for copy in copies:
                copy.start()
            for copy in copies:
                copy.wait()


def take_either(freqs, ids, first, second):
    shape = (len(freqs), *first.shape[1:])
    kernel = functools.partial(either_kernel, freqs)
    return copy_call(kernel, ids, shape, first.dtype, [first, second], len(freqs))


def sums_by_swaps(cross, replicas, norms):
    rows, half = cross.shape[2], cross.shape[3]
    width = replicas.shape[3]
    me = lax.axis_index("row").astype(jnp.int32)
    col = lax.axis_index("col").astype(jnp.int32)
    holds = me * rows // half == col
    mid = ((me // 2) % 4 == 1) | ((me // 2) % 4 == 2)
    flag = lambda value: jnp.where(value, 1, 0).astype(jnp.int32).reshape(1)
    ids = lambda *wanted: me ^ jnp.array(wanted, jnp.int32)
    barrier = lambda *values: lax.optimization_barrier(values)

    slots = jnp.arange(2, dtype=jnp.int32)
    per_half = half // width
    own_masks = (2 * me % per_half + slots) ^ me
    next_masks = ((2 * (me ^ 2) % per_half + slots) ^ me) & 3
    table = lambda masks: sum(
        jnp.where(masks == mask, place, 0)
        for mask, place in enumerate((0, 1, 0, 2, 2, 4, 1, 3))
    ) + jnp.where(holds, 0, 5)
    late_ids = jnp.concatenate(
        [
            ids(5),
            jnp.where(mid, ids(7), ids(6)),
            flag(mid),
            table(own_masks),
            table(next_masks),
        ]
    ).astype(jnp.int32)
    pair = flag(((me >> 1) ^ me) & 1 != 0)
    numbers = [ids(1, 2, 6), ids(3, 4), ids(7), late_ids, pair, flag(mid)]

    own = replicas[:, :, 0]
    x = swap(own, "row", 1)
    n = swap(own, "row", 2)
    m = swap_some(own, 6, middle)
    a0 = add_field(cross, 0, ids(0), [own])
    a1 = add_field(cross, 1, ids(0), [own])
    block_a = take_block(cross, 0, (0, 1), ids(7), width)
    x, n, m, a0, a1, block_a, norms, *numbers = barrier(x, n, m, a0, a1, block_a, norms, *numbers)
    ids_a, ids_b, ids_7, late_ids, pair, is_mid = numbers

    g = swap_some(m, 2, middle)
    m2 = swap_some(n, 6, middle)
    xn = swap(n, "row", 1)
    block_a = swap_some(block_a, 2, end)
    a0 = add_field(cross, 0, ids_a, [x, n, m], a0)
    a1 = add_field(cross, 1, ids_a, [x, n, m], a1)
    block_re = take_block(cross, 1, (0,), ids_7, width)
    block_im = take_block(cross, 1, (1,), ids_7, width)
    mine = take_pair(pair, own, x, n, m)
    x_a, x_b = x[0:1], x[1:2]
    g, m2, xn, block_a, a0, a1, block_re, block_im, mine, x_a, x_b = barrier(
        g, m2, xn, block_a, a0, a1, block_re, block_im, mine, x_a, x_b
    )

    w4_a = take_either((0,), is_mid, g, m2)
    x5_a = swap(w4_a, "row", 1)
    w6_a = swap_some(w4_a, 2, middle)
    w7_a = swap_some(x_a, 6, middle)
    block_re = swap_some(block_re, 2, end)
    other = swap(mine, "col", 1)
    b0 = add_field(cross, 0, ids_b, [xn, w4_a], a0)
    w4_b = take_either((1,), after(is_mid, b0), g, m2)
    later = take_either((0, 1), after(pair, b0), m2, xn)
    b1 = add_field(cross, 1, ids_b, [xn, w4_b], a1)
    x5_a, w6_a, w7_a, block_re, other, b0, w4_b, later, x_b, block_im = barrier(
        x5_a, w6_a, w7_a, block_re, other, b0, w4_b, later, x_b, block_im
    )

    x5_b = swap(w4_b, "row", 1)
    w6_b = swap_some(w4_b, 2, middle)
    w7_b = swap_some(x_b, 6, middle)
    block_im = swap_some(block_im, 2, end)
    other_later = swap(later, "col", 1)
    early = [mine, later, later, later, other, other_later, other_later, other_later]
    sums_a, field_a = add_late(
        cross, 0, late_ids, [x5_a, w6_a, w7_a], [block_a, block_a], b0, early
    )
    late_a = take_either((0,), pair, x5_a, w7_a)
    x5_b, w6_b, w7_b, block_im, sums_a, field_a, b1, late_a, other_later = barrier(
        x5_b, w6_b, w7_b, block_im, sums_a, field_a, b1, late_a, other_later
    )

    other_late_a = swap(late_a, "col", 1)
    other_w7_b = swap(w7_b, "col", 1)
    other_x5_b = swap(x5_b, "col", 1)
    early[5:] = [other_later] * 3
    sums_b, field_b = add_late(
        cross, 1, late_ids, [x5_b, w6_b, w7_b], [block_re, block_im], b1, early
    )
    rows_a = [mine, later, late_a, late_a, other, other_later, other_late_a, other_late_a]
    rows_b = [mine, later, w7_b, x5_b, other, other_later, other_w7_b, other_x5_b]
    groups = [(field_a, sums_a, *rows_a), (field_b, sums_b, *rows_b)]
    return dot_rows(late_ids, norms, groups)


def sums_by_gather(cross, replicas, norms):
    rows, half = cross.shape[2], cross.shape[3]
    row_index, col_index = lax.axis_index("row"), lax.axis_index("col")
    first_row = row_index * rows
    holder = first_row // half
    whole = lax.all_gather(replicas, "row", axis=3, tiled=True)[:, :, 0]
    parts = jnp.einsum("fark,fbks->fabrs", cross, whole, preferred_element_type=jnp.float32)
    field = jnp.stack([parts[:, 0, 0] - parts[:, 1, 1], parts[:, 0, 1] + parts[:, 1, 0]], axis=1)
    own_rows = lax.dynamic_slice_in_dim(whole, first_row - holder * half, rows, 2)
    block_rows = jnp.where(holder == col_index, own_rows, swap(own_rows, "col", 1))
    numer = jnp.sum(block_rows.astype(jnp.float32) * field, axis=(1, 2))
    return jnp.concatenate([numer, norms])


def body(cross_spectra, replicas, tile_order):
    fnum = cross_spectra.shape[0]
    sources = replicas.shape[4]
    own = replicas[:, :, 0].astype(jnp.float32)
    norms = jnp.sum(own * own, axis=(1, 2))
    doubling = (
        lax.axis_size("row") == 8
        and fnum == 2
        and replicas.shape[3] % 128 == 0
        and cross_spectra.shape[2] == 2 * replicas.shape[3]
    )
    sums = (sums_by_swaps if doubling else sums_by_gather)(cross_spectra, replicas, norms)
    sums = sum_all(sums)
    numer, norms = sums[:fnum], sums[fnum:]
    beam = numer / (norms + 1e-06)
    width = sources // lax.axis_size("col")
    beam_half = lax.dynamic_slice_in_dim(beam, lax.axis_index("col") * width, width, 1)
    peak = jnp.max(jnp.abs(beam), axis=1) + 1e-06
    count = tile_order.shape[0]
    picker = (tile_order[:, None] == jnp.arange(count, dtype=jnp.int32)[None, :]).astype(jnp.float32)
    tiles = beam.reshape(fnum, count, sources // count)
    refined = (
        jnp.einsum("tu,fup->ftp", picker, tiles, precision=lax.Precision.HIGHEST)
        / peak[:, None, None]
    )
    return (beam_half, refined)


def solution(mesh):
    in_specs = (P("groups", None, "row", "col"), P("groups", None, "col", "row", None), P("groups"))
    out_specs = (P("groups", "col"), P("groups", None, None))
    return jax.shard_map(body, mesh=mesh, in_specs=in_specs, out_specs=out_specs, check_vma=False)
```

```python
import functools
import math

import jax
import jax.numpy as jnp
from jax import lax
from jax.experimental import pallas as pl
from jax.experimental.pallas import tpu as pltpu
from jax.sharding import PartitionSpec as P

VMEM_LIMIT = 63 * 1024 * 1024
HINT = pl.CostEstimate(flops=1, bytes_accessed=1, transcendentals=0)
ANYWHERE = pl.BlockSpec(memory_space=pl.ANY)


def swap(value, axis, mask):
    size = math.prod(lax.axis_size(name) for name in (axis if isinstance(axis, tuple) else (axis,)))
    return lax.ppermute(value, axis, [(source, source ^ mask) for source in range(size)])


def swap_middle(value):
    axes = ("row", "col")
    size = lax.axis_size("row") * lax.axis_size("col")
    target = lambda k: k ^ 12 if (k // 4) % 4 in (1, 2) else k ^ 1
    return lax.ppermute(value, axes, [(k, target(k)) for k in range(size)])


def after(value, *others):
    return lax.optimization_barrier((value, *others))[0]


def sum_all(value):
    axes = ("row", "col")
    size = lax.axis_size("row") * lax.axis_size("col")
    if size > 16 or size & (size - 1):
        return lax.psum(value, axes)
    mask = 1
    while mask < size:
        near = value + swap(value, axes, mask)
        if 2 * mask < size:
            near = near + (swap(value, axes, 2 * mask) + swap(value, axes, 3 * mask))
        value, mask = near, 4 * mask
    return value


def dot(a, b):
    return jnp.dot(a, b, preferred_element_type=jnp.float32)


def at_freq(ref, freq):
    return ref.at[freq if ref.shape[0] > 1 else 0]


def weight_copies(freq, ref, right, sem):
    low = pl.ds(0, ref.shape[2])
    source = at_freq(ref, freq)
    return [
        pltpu.make_async_copy(source.at[0], right.at[0, low], sem.at[0]),
        pltpu.make_async_copy(source.at[1], right.at[1, low], sem.at[1]),
    ]


def spread(right):
    width = right.shape[1] // 2
    right[0, width:] = -right[1, :width]
    right[1, width:] = right[0, :width]


def spectra_copies(freq, column, cross, left, sem):
    width = left.shape[1] // 2
    columns = pl.ds(pl.multiple_of(column * width, width), width)
    return [
        pltpu.make_async_copy(
            cross.at[freq, part, :, columns], left.at[:, pl.ds(part * width, width)], sem.at[part]
        )
        for part in range(2)
    ]


def field_kernel(freq, count, has_total, gated, ids, cross, *refs):
    w_refs, refs = refs[:count], refs[count:]
    total, refs = (refs[0], refs[1:]) if has_total else (None, refs)
    out, left, right, l_sem, w_sem, field, tot, tot_sem = refs
    piece, part = pl.program_id(0), pl.program_id(1)
    copies = [
        weight_copies(freq, ref, right.at[k], w_sem.at[k])
        + spectra_copies(freq, ids[k], cross, left.at[k], l_sem.at[k])
        for k, ref in enumerate(w_refs)
    ]
    for k, group in enumerate(copies):

        @pl.when((piece == k) & (part == 0))
        def _(k=k, group=group):
            if k == 0:
                for copy in group:
                    copy.start()
            for copy in group:
                copy.wait()
            if k + 1 < count:
                for copy in copies[k + 1]:
                    copy.start()
            if k == 0 and has_total:
                pltpu.make_async_copy(total, tot, tot_sem.at[0]).start()
            spread(right.at[k])

    last = piece == count - 1
    if count > 1:

        @pl.when(piece == 0)
        def _():
            field[part] = dot(left[piece], right[piece, part])

        @pl.when((piece > 0) & (piece < count - 1))
        def _():
            field[part] += dot(left[piece], right[piece, part])

    @pl.when(last)
    def _():
        value = dot(left[piece], right[piece, part])
        if gated:
            value = jnp.where(ids[count] == 1, value, 0.0)
        if count > 1:
            value += field[part]
        if has_total:

            @pl.when(part == 0)
            def _():
                pltpu.make_async_copy(total, tot, tot_sem.at[0]).wait()

            value += tot[part]
        out[0] = value


def add_field(cross, freq, ids, pieces, total=None, gated=False):
    rows, (width, sources) = cross.shape[2], pieces[0].shape[2:]
    count, dtype = len(pieces), pieces[0].dtype
    has_total = total is not None
    return pl.pallas_call(
        functools.partial(field_kernel, freq, count, has_total, gated),
        out_shape=jax.ShapeDtypeStruct((2, rows, sources), jnp.float32),
        grid_spec=pltpu.PrefetchScalarGridSpec(
            num_scalar_prefetch=1,
            grid=(count, 2),
            in_specs=[ANYWHERE] * (1 + count + has_total),
            out_specs=pl.BlockSpec(
                (1, rows, sources), lambda p, part, ids: (jnp.where(p == count - 1, part, 0), 0, 0)
            ),
            scratch_shapes=[
                pltpu.VMEM((count, rows, 2 * width), dtype),
                pltpu.VMEM((count, 2, 2 * width, sources), dtype),
                pltpu.SemaphoreType.DMA((count, 2)),
                pltpu.SemaphoreType.DMA((count, 2)),
                pltpu.VMEM((2, rows, sources), jnp.float32),
                pltpu.VMEM((2, rows, sources), jnp.float32),
                pltpu.SemaphoreType.DMA((1,)),
            ],
        ),
        compiler_params=pltpu.CompilerParams(vmem_limit_bytes=VMEM_LIMIT),
        cost_estimate=HINT,
    )(ids, cross, *pieces, *([total] if has_total else []))


def start_rows(freq, ids, base, refs, rows, sem):
    width = rows.shape[1] // 2
    views = []
    for picked, *pieces in (refs[:5], refs[5:]):
        views += [picked.at[freq, :, pl.ds(slot * width, width)] for slot in range(2)]
        views += [at_freq(ref, freq) for ref in pieces]
    for slot in range(2):
        here = pl.ds(slot * width, width)
        for k, source in enumerate(views):

            @pl.when(ids[base + slot] == k)
            def _(source=source, slot=slot, here=here):
                pltpu.make_async_copy(source, rows.at[:, here], sem.at[slot]).start()


def wait_rows(freq, slot, refs, rows, sem):
    width = rows.shape[1] // 2
    source = refs[0].at[freq, :, pl.ds(0, width)]
    here = rows.at[:, pl.ds(slot * width, width)]
    pltpu.make_async_copy(source, here, sem.at[slot]).wait()


def fold(rows, field):
    product = rows.astype(jnp.float32) * field
    return jnp.sum(product.reshape(-1, 8, product.shape[-1]), axis=0)


def late_kernel(freq, ids, cross, w5, w6, w7, block_re, block_im, total, *refs):
    row_refs, refs = refs[:10], refs[10:]
    sums, field_out, left, right, l_sem, w_sem, field, tot, sem, rows, row_sem = refs
    step, part = pl.program_id(0), pl.program_id(1)
    width = w5.shape[2]
    first = weight_copies(freq, w5, right.at[0], w_sem.at[0]) + spectra_copies(
        freq, ids[0], cross, left.at[0], l_sem.at[0]
    )
    six = weight_copies(freq, w6, right.at[1], w_sem.at[1])
    seven = weight_copies(freq, w7, right.at[1], w_sem.at[1])
    second = spectra_copies(freq, ids[1], cross, left.at[1], l_sem.at[1])
    third = [
        pltpu.make_async_copy(
            ref.at[min(k, ref.shape[0] - 1), half],
            left.at[2, pl.ds(half * width, width), pl.ds(k * width, width)],
            l_sem.at[2 + half, k],
        )
        for k, ref in enumerate((block_re, block_im))
        for half in range(2)
    ]
    total_copy = pltpu.make_async_copy(total, tot, sem.at[0])
    out_copies = [
        pltpu.make_async_copy(field.at[k], field_out.at[k], sem.at[1 + k]) for k in range(2)
    ]

    @pl.when((step == 0) & (part == 0))
    def _():
        sums[...] = jnp.zeros_like(sums)
        for copy in first:
            copy.start()
        for copy in first:
            copy.wait()
        for copy in second:
            copy.start()

        @pl.when(ids[2] == 1)
        def _():
            for copy in seven:
                copy.start()

        @pl.when(ids[2] == 0)
        def _():
            for copy in six:
                copy.start()

        total_copy.start()
        spread(right.at[0])

    @pl.when((step == 1) & (part == 0))
    def _():
        for copy in second + six:
            copy.wait()
        for copy in third:
            copy.start()
        start_rows(freq, ids, 5, row_refs, rows, row_sem)
        total_copy.wait()
        spread(right.at[1])

    @pl.when((step == 2) & (part == 0))
    def _():
        for copy in third:
            copy.wait()
        for slot in range(2):
            wait_rows(freq, slot, row_refs, rows, row_sem)

    @pl.when(step == 0)
    def _():
        field[part] = dot(left[0], right[0, part])

    for k in range(2):

        @pl.when((step == 1) & (part == k))
        def _(k=k):
            field[k] = field[k] + tot[k] + dot(left[1], right[1, k])
            out_copies[k].start()

    @pl.when((step == 2) & (ids[2] == 1))
    def _():
        sums[...] += fold(rows[part], dot(left[2], right[0, part]))

    @pl.when((step == 2) & (part == 1))
    def _():
        for copy in out_copies:
            copy.wait()


def add_late(cross, freq, ids, pieces, blocks, total, row_refs):
    rows, (width, sources) = cross.shape[2], pieces[0].shape[2:]
    dtype = pieces[0].dtype
    return pl.pallas_call(
        functools.partial(late_kernel, freq),
        out_shape=(
            jax.ShapeDtypeStruct((8, sources), jnp.float32),
            jax.ShapeDtypeStruct(total.shape, total.dtype),
        ),
        grid_spec=pltpu.PrefetchScalarGridSpec(
            num_scalar_prefetch=1,
            grid=(3, 2),
            in_specs=[ANYWHERE] * (7 + len(row_refs)),
            out_specs=(pl.BlockSpec((8, sources), lambda step, part, ids: (0, 0)), ANYWHERE),
            scratch_shapes=[
                pltpu.VMEM((3, rows, 2 * width), dtype),
                pltpu.VMEM((2, 2, 2 * width, sources), dtype),
                pltpu.SemaphoreType.DMA((4, 2)),
                pltpu.SemaphoreType.DMA((2, 2)),
                pltpu.VMEM((2, rows, sources), jnp.float32),
                pltpu.VMEM((2, rows, sources), jnp.float32),
                pltpu.SemaphoreType.DMA((3,)),
                pltpu.VMEM((2, rows, sources), dtype),
                pltpu.SemaphoreType.DMA((2,)),
            ],
        ),
        compiler_params=pltpu.CompilerParams(vmem_limit_bytes=VMEM_LIMIT),
        cost_estimate=HINT,
    )(ids, cross, *pieces, *blocks, total, *row_refs)


def dot_kernel(ids, norms, *refs):
    groups, (out, rows, row_sem, field, sem) = (refs[:12], refs[12:24]), refs[24:]
    width = rows.shape[2] // 2
    pairs = [(slot, part) for slot in range(2) for part in range(2)]
    copies = {}
    for freq, (field_ref, _, *row_refs) in enumerate(groups):
        start_rows(freq, ids, 3, row_refs, rows.at[freq], row_sem.at[freq])
        for slot, part in pairs:
            here = pl.ds(slot * width, width)
            copies[freq, slot, part] = pltpu.make_async_copy(
                field_ref.at[part, here], field.at[freq, part, here], sem.at[freq, 2 * slot + part]
            )
            copies[freq, slot, part].start()
    for freq, (_, sums_ref, *row_refs) in enumerate(groups):
        sums = sums_ref[...]
        for slot, part in pairs:
            if part == 0:
                wait_rows(freq, slot, row_refs, rows.at[freq], row_sem.at[freq])
            copies[freq, slot, part].wait()
            here = slice(slot * width, (slot + 1) * width)
            sums += fold(rows[freq, part, here], field[freq, part, here])
        out[freq : freq + 1] = jnp.sum(sums, axis=0, keepdims=True)
    out[2:4] = norms[...]


def dot_rows(ids, norms, groups):
    _, rows, sources = groups[0][0].shape
    whole = lambda shape: pl.BlockSpec(shape, lambda i, ids: (0, 0))
    return pl.pallas_call(
        dot_kernel,
        out_shape=jax.ShapeDtypeStruct((4, sources), jnp.float32),
        grid_spec=pltpu.PrefetchScalarGridSpec(
            num_scalar_prefetch=1,
            grid=(1,),
            in_specs=[whole((2, sources))] + [ANYWHERE, whole((8, sources)), *[ANYWHERE] * 10] * 2,
            out_specs=whole((4, sources)),
            scratch_shapes=[
                pltpu.VMEM((2, 2, rows, sources), groups[0][2].dtype),
                pltpu.SemaphoreType.DMA((2, 2)),
                pltpu.VMEM((2, 2, rows, sources), jnp.float32),
                pltpu.SemaphoreType.DMA((2, 4)),
            ],
        ),
        compiler_params=pltpu.CompilerParams(vmem_limit_bytes=VMEM_LIMIT),
        cost_estimate=HINT,
    )(ids, norms, *groups[0], *groups[1])


def copy_kernel(inputs, jobs, ids, *refs):
    refs, (stage, in_sem, out_sem) = refs[:-3], refs[-3:]
    sources, targets = refs[:inputs], refs[inputs:]
    writes = [
        pltpu.make_async_copy(stage.at[k], target(targets), out_sem.at[k])
        for k, (_, target) in enumerate(jobs)
    ]

    def each(act):
        for k, (options, _) in enumerate(jobs):
            for value, source in options:

                @pl.when(ids[0] == value)
                def _(k=k, source=source):
                    act(k, pltpu.make_async_copy(source(sources, ids), stage.at[k], in_sem.at[k]))

    def pass_on(k, copy):
        copy.wait()
        writes[k].start()

    def finish(k, copy):
        writes[k].wait()

    each(lambda k, copy: copy.start())
    each(pass_on)
    each(finish)


def copies(ids, args, jobs, shapes, unit, dtype, alias=None):
    return pl.pallas_call(
        functools.partial(copy_kernel, len(args), jobs),
        out_shape=[jax.ShapeDtypeStruct(shape, dtype) for shape in shapes],
        grid_spec=pltpu.PrefetchScalarGridSpec(
            num_scalar_prefetch=1,
            grid=(1,),
            in_specs=[ANYWHERE] * len(args),
            out_specs=[ANYWHERE] * len(shapes),
            scratch_shapes=[
                pltpu.VMEM((len(jobs), *unit), dtype),
                pltpu.SemaphoreType.DMA((len(jobs),)),
                pltpu.SemaphoreType.DMA((len(jobs),)),
            ],
        ),
        input_output_aliases={} if alias is None else {1 + alias: 0},
        compiler_params=pltpu.CompilerParams(vmem_limit_bytes=VMEM_LIMIT),
        cost_estimate=HINT,
    )(ids, *args)


def block_source(at, freq, part, half, width):
    def source(refs, ids):
        columns = pl.ds(pl.multiple_of(ids[1] * width, width), width)
        return refs[at].at[freq, part, pl.ds(half * width, width), columns]

    return source


def entry(at, *index):
    return lambda refs, ids=None: refs[at].at[index]


def fill_block(ids, piece, cross):
    _, _, width, sources = piece.shape
    jobs = [
        ([(0, block_source(1, 0, part, half, width))], entry(0, part, half))
        for part in range(2)
        for half in range(2)
    ]
    return copies(ids, [piece, cross], jobs, [piece.shape], (width, sources), piece.dtype, 0)[0]


def take_pair(ids, own, x, n, m):
    freqs, _, width, sources = own.shape
    jobs = [
        (
            [(0, entry(slot, freq, part)), (1, entry(2 + slot, freq, part))],
            entry(0, freq, part, pl.ds(slot * width, width)),
        )
        for freq in range(freqs)
        for part in range(2)
        for slot in range(2)
    ]
    shape = (freqs, 2, 2 * width, sources)
    return copies(ids, [own, x, n, m], jobs, [shape], (width, sources), own.dtype)[0]


def take_next(freq, ids, ends, middles, cross):
    _, _, width, sources = ends.shape
    jobs = []
    for part in range(2):
        block = block_source(2, 1, freq, part, width)
        jobs.append(([(0, block), (1, entry(1, freq, part))], entry(1, 0, part)))
        jobs.append(([(0, entry(0, freq, part)), (1, entry(1, freq, part))], entry(0, 0, part)))
    shape = (1, 2, width, sources)
    args = [ends, middles, cross]
    return copies(ids, args, jobs, [shape, shape], (width, sources), ends.dtype)


def sums_by_swaps(cross, replicas, norms):
    rows, half = cross.shape[2], cross.shape[3]
    width = replicas.shape[3]
    me = lax.axis_index("row").astype(jnp.int32)
    col = lax.axis_index("col").astype(jnp.int32)
    holds = me * rows // half == col
    mid = ((me // 2) % 4 == 1) | ((me // 2) % 4 == 2)
    flag = lambda value: jnp.where(value, 1, 0).astype(jnp.int32).reshape(1)
    ids = lambda *wanted: me ^ jnp.array(wanted, jnp.int32)
    barrier = lambda *values: lax.optimization_barrier(values)

    slots = jnp.arange(2, dtype=jnp.int32)
    per_half = half // width
    own_masks = (2 * me % per_half + slots) ^ me
    next_masks = ((2 * (me ^ 2) % per_half + slots) ^ me) & 3
    table = lambda masks: sum(
        jnp.where(masks == mask, place, 0)
        for mask, place in enumerate((0, 1, 0, 2, 3, 5, 1, 4))
    ) + jnp.where(holds, 0, 6)
    late_ids = jnp.concatenate(
        [
            ids(5),
            jnp.where(mid, ids(7), ids(6)),
            flag(mid),
            table(own_masks),
            table(next_masks),
        ]
    ).astype(jnp.int32)
    pair = flag(((me >> 1) ^ me) & 1 != 0)
    ids_a = jnp.concatenate([ids(1, 2, 6), flag(mid)])
    ids_z = jnp.concatenate([flag(mid), ids(7)])
    numbers = [ids_a, ids(3, 4), ids_z, late_ids, pair]

    own = replicas[:, :, 0]
    x = swap(own, "row", 1)
    n = swap(own, "row", 2)
    m = swap_middle(own)
    a0 = add_field(cross, 0, ids(0), [own])
    a1 = add_field(cross, 1, ids(0), [own])
    x, n, m, a0, a1, norms, *numbers = barrier(x, n, m, a0, a1, norms, *numbers)
    ids_a, ids_b, ids_z, late_ids, pair = numbers

    m = fill_block(ids_z, m, cross)
    z = swap(m, "row", 2)
    m2 = swap_middle(n)
    xn = swap(n, "row", 1)
    a0 = add_field(cross, 0, ids_a, [x, n, m], a0, gated=True)
    a1 = add_field(cross, 1, ids_a, [x, n, m], a1, gated=True)
    mine = take_pair(pair, own, x, n, m)
    x_a, x_b = x[0:1], x[1:2]
    z, m2, xn, a0, a1, mine, x_a, x_b = barrier(z, m2, xn, a0, a1, mine, x_a, x_b)

    w4_a, send_a = take_next(0, ids_z, z, m2, cross)
    x5_a = swap(w4_a, "row", 1)
    z_a = swap(send_a, "row", 2)
    w7_a = swap_middle(x_a)
    other = swap(mine, "col", 1)
    b0 = add_field(cross, 0, ids_b, [xn, w4_a], a0)
    w4_b, send_b = take_next(1, after(ids_z, b0), z, m2, cross)
    b1 = add_field(cross, 1, ids_b, [xn, w4_b], a1)
    x5_a, z_a, w7_a, other, b0, w4_b, send_b, x_b, xn, m2 = barrier(
        x5_a, z_a, w7_a, other, b0, w4_b, send_b, x_b, xn, m2
    )

    x5_b = swap(w4_b, "row", 1)
    z_b = swap(send_b, "row", 2)
    w7_b = swap_middle(x_b)
    other_xn = swap(xn, "col", 1)
    other_m2 = swap(m2, "col", 1)
    early = [mine, xn, m2, xn, xn, other, other_xn, other_m2, other_xn, other_xn]
    sums_a, field_a = add_late(cross, 0, late_ids, [x5_a, z_a, w7_a], [z, z], b0, early)
    x5_b, z_b, w7_b, sums_a, field_a, b1, other_xn, other_m2, x5_a, w7_a = barrier(
        x5_b, z_b, w7_b, sums_a, field_a, b1, other_xn, other_m2, x5_a, w7_a
    )

    late = [w7_a, x5_a, w7_b, x5_b]
    others = [swap(piece, "col", 1) for piece in late]
    early = [mine, xn, m2, xn, xn, other, other_xn, other_m2, other_xn, other_xn]
    sums_b, field_b = add_late(cross, 1, late_ids, [x5_b, z_b, w7_b], [z_a, z_b], b1, early)
    here, there = [mine, xn, m2], [other, other_xn, other_m2]
    groups = [
        (field_a, sums_a, *here, *late[:2], *there, *others[:2]),
        (field_b, sums_b, *here, *late[2:], *there, *others[2:]),
    ]
    return dot_rows(late_ids, norms, groups)


def sums_by_gather(cross, replicas, norms):
    rows, half = cross.shape[2], cross.shape[3]
    row_index, col_index = lax.axis_index("row"), lax.axis_index("col")
    first_row = row_index * rows
    holder = first_row // half
    whole = lax.all_gather(replicas, "row", axis=3, tiled=True)[:, :, 0]
    parts = jnp.einsum("fark,fbks->fabrs", cross, whole, preferred_element_type=jnp.float32)
    field = jnp.stack([parts[:, 0, 0] - parts[:, 1, 1], parts[:, 0, 1] + parts[:, 1, 0]], axis=1)
    own_rows = lax.dynamic_slice_in_dim(whole, first_row - holder * half, rows, 2)
    block_rows = jnp.where(holder == col_index, own_rows, swap(own_rows, "col", 1))
    numer = jnp.sum(block_rows.astype(jnp.float32) * field, axis=(1, 2))
    return jnp.concatenate([numer, norms])


def body(cross_spectra, replicas, tile_order):
    fnum = cross_spectra.shape[0]
    sources = replicas.shape[4]
    own = replicas[:, :, 0].astype(jnp.float32)
    norms = jnp.sum(own * own, axis=(1, 2))
    doubling = (
        lax.axis_size("row") == 8
        and fnum == 2
        and replicas.shape[3] % 128 == 0
        and cross_spectra.shape[2] == 2 * replicas.shape[3]
    )
    sums = (sums_by_swaps if doubling else sums_by_gather)(cross_spectra, replicas, norms)
    sums = sum_all(sums)
    numer, norms = sums[:fnum], sums[fnum:]
    beam = numer / (norms + 1e-06)
    width = sources // lax.axis_size("col")
    beam_half = lax.dynamic_slice_in_dim(beam, lax.axis_index("col") * width, width, 1)
    peak = jnp.max(jnp.abs(beam), axis=1) + 1e-06
    count = tile_order.shape[0]
    picker = (tile_order[:, None] == jnp.arange(count, dtype=jnp.int32)[None, :]).astype(jnp.float32)
    tiles = beam.reshape(fnum, count, sources // count)
    refined = (
        jnp.einsum("tu,fup->ftp", picker, tiles, precision=lax.Precision.HIGHEST)
        / peak[:, None, None]
    )
    return (beam_half, refined)


def solution(mesh):
    in_specs = (P("groups", None, "row", "col"), P("groups", None, "col", "row", None), P("groups"))
    out_specs = (P("groups", "col"), P("groups", None, None))
    return jax.shard_map(body, mesh=mesh, in_specs=in_specs, out_specs=out_specs, check_vma=False)
```

```python
import functools
import math

import jax
import jax.numpy as jnp
from jax import lax
from jax.experimental import pallas as pl
from jax.experimental.pallas import tpu as pltpu
from jax.sharding import PartitionSpec as P

VMEM_LIMIT = 63 * 1024 * 1024
HINT = pl.CostEstimate(flops=1, bytes_accessed=1, transcendentals=0)
ANYWHERE = pl.BlockSpec(memory_space=pl.ANY)


def swap(value, axis, mask):
    size = math.prod(lax.axis_size(name) for name in (axis if isinstance(axis, tuple) else (axis,)))
    return lax.ppermute(value, axis, [(source, source ^ mask) for source in range(size)])


def swap_middle(value):
    axes = ("row", "col")
    size = lax.axis_size("row") * lax.axis_size("col")
    target = lambda k: k ^ 12 if (k // 4) % 4 in (1, 2) else k ^ 1
    return lax.ppermute(value, axes, [(k, target(k)) for k in range(size)])


def after(value, *others):
    return lax.optimization_barrier((value, *others))[0]


def sum_all(value):
    axes = ("row", "col")
    size = lax.axis_size("row") * lax.axis_size("col")
    if size > 16 or size & (size - 1):
        return lax.psum(value, axes)
    mask = 1
    while mask < size:
        near = value + swap(value, axes, mask)
        if 2 * mask < size:
            near = near + (swap(value, axes, 2 * mask) + swap(value, axes, 3 * mask))
        value, mask = near, 4 * mask
    return value


def dot(a, b):
    return jnp.dot(a, b, preferred_element_type=jnp.float32)


def at_freq(ref, freq):
    return ref.at[freq if ref.shape[0] > 1 else 0]


def weight_copies(freq, ref, right, sem):
    low = pl.ds(0, ref.shape[2])
    source = at_freq(ref, freq)
    return [
        pltpu.make_async_copy(source.at[0], right.at[0, low], sem.at[0]),
        pltpu.make_async_copy(source.at[1], right.at[1, low], sem.at[1]),
    ]


def spread(right):
    width = right.shape[1] // 2
    right[0, width:] = -right[1, :width]
    right[1, width:] = right[0, :width]


def spectra_copies(freq, column, cross, left, sem):
    width = left.shape[1] // 2
    columns = pl.ds(pl.multiple_of(column * width, width), width)
    return [
        pltpu.make_async_copy(
            cross.at[freq, part, :, columns], left.at[:, pl.ds(part * width, width)], sem.at[part]
        )
        for part in range(2)
    ]


def field_kernel(freq, count, has_total, gated, ids, cross, *refs):
    w_refs, refs = refs[:count], refs[count:]
    total, refs = (refs[0], refs[1:]) if has_total else (None, refs)
    out, left, right, l_sem, w_sem, field, tot, tot_sem = refs
    piece, part = pl.program_id(0), pl.program_id(1)
    copies = [
        weight_copies(freq, ref, right.at[k], w_sem.at[k])
        + spectra_copies(freq, ids[k], cross, left.at[k], l_sem.at[k])
        for k, ref in enumerate(w_refs)
    ]
    for k, group in enumerate(copies):

        @pl.when((piece == k) & (part == 0))
        def _(k=k, group=group):
            if k == 0:
                for copy in group:
                    copy.start()
            for copy in group:
                copy.wait()
            if k + 1 < count:
                for copy in copies[k + 1]:
                    copy.start()
            if k == 0 and has_total:
                pltpu.make_async_copy(total, tot, tot_sem.at[0]).start()
            spread(right.at[k])

    last = piece == count - 1
    if count > 1:

        @pl.when(piece == 0)
        def _():
            field[part] = dot(left[piece], right[piece, part])

        @pl.when((piece > 0) & (piece < count - 1))
        def _():
            field[part] += dot(left[piece], right[piece, part])

    @pl.when(last)
    def _():
        value = dot(left[piece], right[piece, part])
        if gated:
            value = jnp.where(ids[count] == 1, value, 0.0)
        if count > 1:
            value += field[part]
        if has_total:

            @pl.when(part == 0)
            def _():
                pltpu.make_async_copy(total, tot, tot_sem.at[0]).wait()

            value += tot[part]
        out[0] = value


def add_field(cross, freq, ids, pieces, total=None, gated=False):
    rows, (width, sources) = cross.shape[2], pieces[0].shape[2:]
    count, dtype = len(pieces), pieces[0].dtype
    has_total = total is not None
    return pl.pallas_call(
        functools.partial(field_kernel, freq, count, has_total, gated),
        out_shape=jax.ShapeDtypeStruct((2, rows, sources), jnp.float32),
        grid_spec=pltpu.PrefetchScalarGridSpec(
            num_scalar_prefetch=1,
            grid=(count, 2),
            in_specs=[ANYWHERE] * (1 + count + has_total),
            out_specs=pl.BlockSpec(
                (1, rows, sources), lambda p, part, ids: (jnp.where(p == count - 1, part, 0), 0, 0)
            ),
            scratch_shapes=[
                pltpu.VMEM((count, rows, 2 * width), dtype),
                pltpu.VMEM((count, 2, 2 * width, sources), dtype),
                pltpu.SemaphoreType.DMA((count, 2)),
                pltpu.SemaphoreType.DMA((count, 2)),
                pltpu.VMEM((2, rows, sources), jnp.float32),
                pltpu.VMEM((2, rows, sources), jnp.float32),
                pltpu.SemaphoreType.DMA((1,)),
            ],
        ),
        compiler_params=pltpu.CompilerParams(vmem_limit_bytes=VMEM_LIMIT),
        cost_estimate=HINT,
    )(ids, cross, *pieces, *([total] if has_total else []))


def start_rows(freq, ids, base, refs, rows, sem):
    width = rows.shape[1] // 2
    views = []
    for picked, *pieces in (refs[:5], refs[5:]):
        views += [picked.at[freq, :, pl.ds(slot * width, width)] for slot in range(2)]
        views += [at_freq(ref, freq) for ref in pieces]
    for slot in range(2):
        here = pl.ds(slot * width, width)
        for k, source in enumerate(views):

            @pl.when(ids[base + slot] == k)
            def _(source=source, slot=slot, here=here):
                pltpu.make_async_copy(source, rows.at[:, here], sem.at[slot]).start()


def wait_rows(freq, slot, refs, rows, sem):
    width = rows.shape[1] // 2
    source = refs[0].at[freq, :, pl.ds(0, width)]
    here = rows.at[:, pl.ds(slot * width, width)]
    pltpu.make_async_copy(source, here, sem.at[slot]).wait()


def fold(rows, field):
    product = rows.astype(jnp.float32) * field
    return jnp.sum(product.reshape(-1, 8, product.shape[-1]), axis=0)


def late_kernel(freq, ids, cross, w5, w6, w7, block_re, block_im, total, *refs):
    row_refs, refs = refs[:10], refs[10:]
    sums, field_out, left, right, l_sem, w_sem, field, tot, sem, rows, row_sem = refs
    late = ids[7]
    step, part = pl.program_id(0), pl.program_id(1)
    width = w5.shape[2]
    first = weight_copies(freq, w5, right.at[0], w_sem.at[0]) + spectra_copies(
        freq, ids[0], cross, left.at[0], l_sem.at[0]
    )
    six = weight_copies(freq, w6, right.at[1], w_sem.at[1])
    seven = weight_copies(freq, w7, right.at[1], w_sem.at[1])
    second = spectra_copies(freq, ids[1], cross, left.at[1], l_sem.at[1])
    third = [
        pltpu.make_async_copy(
            ref.at[min(k, ref.shape[0] - 1), half],
            left.at[2, pl.ds(half * width, width), pl.ds(k * width, width)],
            l_sem.at[2 + half, k],
        )
        for k, ref in enumerate((block_re, block_im))
        for half in range(2)
    ]
    total_copy = pltpu.make_async_copy(total, tot, sem.at[0])
    late_rows = pl.ds(pl.multiple_of(jnp.minimum(late, 1) * width, width), width)
    out_copies = [
        pltpu.make_async_copy(field.at[k, late_rows], field_out.at[k], sem.at[1 + k])
        for k in range(2)
    ]

    @pl.when((step == 0) & (part == 0))
    def _():
        sums[...] = jnp.zeros_like(sums)
        for copy in first:
            copy.start()
        for copy in first:
            copy.wait()
        for copy in second:
            copy.start()

        @pl.when(ids[2] == 1)
        def _():
            for copy in seven:
                copy.start()

        @pl.when(ids[2] == 0)
        def _():
            for copy in six:
                copy.start()

        total_copy.start()
        start_rows(freq, ids, 3, row_refs, rows.at[0], row_sem.at[0])
        spread(right.at[0])

    @pl.when((step == 1) & (part == 0))
    def _():
        for copy in second + six:
            copy.wait()
        for copy in third:
            copy.start()
        start_rows(freq, ids, 5, row_refs, rows.at[1], row_sem.at[1])
        total_copy.wait()
        for slot in range(2):
            wait_rows(freq, slot, row_refs, rows.at[0], row_sem.at[0])
        spread(right.at[1])

    @pl.when((step == 2) & (part == 0))
    def _():
        for copy in third:
            copy.wait()
        for slot in range(2):
            wait_rows(freq, slot, row_refs, rows.at[1], row_sem.at[1])

    @pl.when(step == 0)
    def _():
        field[part] = dot(left[0], right[0, part])

    for k in range(2):

        @pl.when((step == 1) & (part == k))
        def _(k=k):
            field[k] = field[k] + tot[k] + dot(left[1], right[1, k])
            out_copies[k].start()
            for slot in range(2):

                @pl.when(late != slot)
                def _(slot=slot):
                    here = slice(slot * width, (slot + 1) * width)
                    sums[...] += fold(rows[0, k, here], field[k, here])

    @pl.when((step == 2) & (ids[2] == 1))
    def _():
        sums[...] += fold(rows[1, part], dot(left[2], right[0, part]))

    @pl.when((step == 2) & (part == 1))
    def _():
        for copy in out_copies:
            copy.wait()


def add_late(cross, freq, ids, pieces, blocks, total, row_refs):
    rows, (width, sources) = cross.shape[2], pieces[0].shape[2:]
    dtype = pieces[0].dtype
    return pl.pallas_call(
        functools.partial(late_kernel, freq),
        out_shape=(
            jax.ShapeDtypeStruct((8, sources), jnp.float32),
            jax.ShapeDtypeStruct((2, width, sources), jnp.float32),
        ),
        grid_spec=pltpu.PrefetchScalarGridSpec(
            num_scalar_prefetch=1,
            grid=(3, 2),
            in_specs=[ANYWHERE] * (7 + len(row_refs)),
            out_specs=(pl.BlockSpec((8, sources), lambda step, part, ids: (0, 0)), ANYWHERE),
            scratch_shapes=[
                pltpu.VMEM((3, rows, 2 * width), dtype),
                pltpu.VMEM((2, 2, 2 * width, sources), dtype),
                pltpu.SemaphoreType.DMA((4, 2)),
                pltpu.SemaphoreType.DMA((2, 2)),
                pltpu.VMEM((2, rows, sources), jnp.float32),
                pltpu.VMEM((2, rows, sources), jnp.float32),
                pltpu.SemaphoreType.DMA((3,)),
                pltpu.VMEM((2, 2, rows, sources), dtype),
                pltpu.SemaphoreType.DMA((2, 2)),
            ],
        ),
        compiler_params=pltpu.CompilerParams(vmem_limit_bytes=VMEM_LIMIT),
        cost_estimate=HINT,
    )(ids, cross, *pieces, *blocks, total, *row_refs)


def dot_kernel(ids, norms, *refs):
    groups, (out, rows, field, sem) = (refs[:6], refs[6:12]), refs[12:]
    for freq, (field_ref, _, *sources) in enumerate(groups):

        @pl.when(ids[0] < 4)
        def _(freq=freq, field_ref=field_ref):
            pltpu.make_async_copy(field_ref, field.at[freq], sem.at[0, freq]).start()

        for k, source in enumerate(sources):

            @pl.when(ids[0] == k)
            def _(freq=freq, source=source):
                pltpu.make_async_copy(source.at[0], rows.at[freq], sem.at[1, freq]).start()

    for freq, (field_ref, sums, *sources) in enumerate(groups):
        out[freq : freq + 1] = jnp.sum(sums[...], axis=0, keepdims=True)

        @pl.when(ids[0] < 4)
        def _(freq=freq, field_ref=field_ref, sources=sources):
            pltpu.make_async_copy(field_ref, field.at[freq], sem.at[0, freq]).wait()
            pltpu.make_async_copy(sources[0].at[0], rows.at[freq], sem.at[1, freq]).wait()
            more = sum(fold(rows[freq, part], field[freq, part]) for part in range(2))
            out[freq : freq + 1] += jnp.sum(more, axis=0, keepdims=True)

    out[2:4] = norms[...]


def dot_rows(ids, norms, groups):
    late_shape, dtype = groups[0][0].shape, groups[0][2].dtype
    sources = late_shape[-1]
    whole = lambda shape: pl.BlockSpec(shape, lambda i, ids: (0, 0))
    return pl.pallas_call(
        dot_kernel,
        out_shape=jax.ShapeDtypeStruct((4, sources), jnp.float32),
        grid_spec=pltpu.PrefetchScalarGridSpec(
            num_scalar_prefetch=1,
            grid=(1,),
            in_specs=[whole((2, sources))] + [ANYWHERE, whole((8, sources)), *[ANYWHERE] * 4] * 2,
            out_specs=whole((4, sources)),
            scratch_shapes=[
                pltpu.VMEM((2, *late_shape), dtype),
                pltpu.VMEM((2, *late_shape), jnp.float32),
                pltpu.SemaphoreType.DMA((2, 2)),
            ],
        ),
        compiler_params=pltpu.CompilerParams(vmem_limit_bytes=VMEM_LIMIT),
        cost_estimate=HINT,
    )(ids, norms, *groups[0], *groups[1])


def copy_kernel(inputs, jobs, ids, *refs):
    refs, (stage, in_sem, out_sem) = refs[:-3], refs[-3:]
    sources, targets = refs[:inputs], refs[inputs:]
    writes = [
        pltpu.make_async_copy(stage.at[k], target(targets), out_sem.at[k])
        for k, (_, target) in enumerate(jobs)
    ]

    def each(act):
        for k, (options, _) in enumerate(jobs):
            for value, source in options:

                @pl.when(ids[0] == value)
                def _(k=k, source=source):
                    act(k, pltpu.make_async_copy(source(sources, ids), stage.at[k], in_sem.at[k]))

    def pass_on(k, copy):
        copy.wait()
        writes[k].start()

    def finish(k, copy):
        writes[k].wait()

    each(lambda k, copy: copy.start())
    each(pass_on)
    each(finish)


def copies(ids, args, jobs, shapes, unit, dtype, alias=None):
    return pl.pallas_call(
        functools.partial(copy_kernel, len(args), jobs),
        out_shape=[jax.ShapeDtypeStruct(shape, dtype) for shape in shapes],
        grid_spec=pltpu.PrefetchScalarGridSpec(
            num_scalar_prefetch=1,
            grid=(1,),
            in_specs=[ANYWHERE] * len(args),
            out_specs=[ANYWHERE] * len(shapes),
            scratch_shapes=[
                pltpu.VMEM((len(jobs), *unit), dtype),
                pltpu.SemaphoreType.DMA((len(jobs),)),
                pltpu.SemaphoreType.DMA((len(jobs),)),
            ],
        ),
        input_output_aliases={} if alias is None else {1 + alias: 0},
        compiler_params=pltpu.CompilerParams(vmem_limit_bytes=VMEM_LIMIT),
        cost_estimate=HINT,
    )(ids, *args)


def block_source(at, freq, part, half, width):
    def source(refs, ids):
        columns = pl.ds(pl.multiple_of(ids[1] * width, width), width)
        return refs[at].at[freq, part, pl.ds(half * width, width), columns]

    return source


def entry(at, *index):
    return lambda refs, ids=None: refs[at].at[index]


def fill_block(ids, piece, cross):
    _, _, width, sources = piece.shape
    jobs = [
        ([(0, block_source(1, 0, part, half, width))], entry(0, part, half))
        for part in range(2)
        for half in range(2)
    ]
    return copies(ids, [piece, cross], jobs, [piece.shape], (width, sources), piece.dtype, 0)[0]


def take_pair(ids, own, x, n, m):
    freqs, _, width, sources = own.shape
    jobs = [
        (
            [(0, entry(slot, freq, part)), (1, entry(2 + slot, freq, part))],
            entry(0, freq, part, pl.ds(slot * width, width)),
        )
        for freq in range(freqs)
        for part in range(2)
        for slot in range(2)
    ]
    shape = (freqs, 2, 2 * width, sources)
    return copies(ids, [own, x, n, m], jobs, [shape], (width, sources), own.dtype)[0]


def take_next(freq, ids, ends, middles, cross):
    _, _, width, sources = ends.shape
    jobs = []
    for part in range(2):
        block = block_source(2, 1, freq, part, width)
        jobs.append(([(0, block), (1, entry(1, freq, part))], entry(1, 0, part)))
        jobs.append(([(0, entry(0, freq, part)), (1, entry(1, freq, part))], entry(0, 0, part)))
    shape = (1, 2, width, sources)
    args = [ends, middles, cross]
    return copies(ids, args, jobs, [shape, shape], (width, sources), ends.dtype)


def sums_by_swaps(cross, replicas, norms):
    rows, half = cross.shape[2], cross.shape[3]
    width = replicas.shape[3]
    me = lax.axis_index("row").astype(jnp.int32)
    col = lax.axis_index("col").astype(jnp.int32)
    holds = me * rows // half == col
    mid = ((me // 2) % 4 == 1) | ((me // 2) % 4 == 2)
    flag = lambda value: jnp.where(value, 1, 0).astype(jnp.int32).reshape(1)
    ids = lambda *wanted: me ^ jnp.array(wanted, jnp.int32)
    barrier = lambda *values: lax.optimization_barrier(values)

    slots = jnp.arange(2, dtype=jnp.int32)
    per_half = half // width
    own_masks = (2 * me % per_half + slots) ^ me
    next_masks = ((2 * (me ^ 2) % per_half + slots) ^ me) & 3
    table = lambda masks: sum(
        jnp.where(masks == mask, place, 0)
        for mask, place in enumerate((0, 1, 0, 2, 3, 5, 1, 4))
    ) + jnp.where(holds, 0, 6)
    late_slot = own_masks[0] & 1 ^ 1
    late_source = jnp.where(own_masks[0] & 2 != 0, 0, 1) + jnp.where(holds, 0, 2)
    ids_dot = jnp.where(mid, late_source, 4).astype(jnp.int32).reshape(1)
    late_ids = jnp.concatenate(
        [
            ids(5),
            jnp.where(mid, ids(7), ids(6)),
            flag(mid),
            table(own_masks),
            table(next_masks),
            jnp.where(mid, late_slot, 2).reshape(1),
        ]
    ).astype(jnp.int32)
    pair = flag(((me >> 1) ^ me) & 1 != 0)
    ids_a = jnp.concatenate([ids(1, 2, 6), flag(mid)])
    ids_z = jnp.concatenate([flag(mid), ids(7)])
    numbers = [ids_a, ids(3, 4), ids_z, late_ids, pair, ids_dot]

    own = replicas[:, :, 0]
    x = swap(own, "row", 1)
    n = swap(own, "row", 2)
    m = swap_middle(own)
    a0 = add_field(cross, 0, ids(0), [own])
    a1 = add_field(cross, 1, ids(0), [own])
    m = fill_block(ids_z, m, cross)
    x, n, m, a0, a1, norms, *numbers = barrier(x, n, m, a0, a1, norms, *numbers)
    ids_a, ids_b, ids_z, late_ids, pair, ids_dot = numbers

    z = swap(m, "row", 2)
    m2 = swap_middle(n)
    xn = swap(n, "row", 1)
    a0 = add_field(cross, 0, ids_a, [x, n, m], a0, gated=True)
    a1 = add_field(cross, 1, ids_a, [x, n, m], a1, gated=True)
    mine = take_pair(pair, own, x, n, m)
    x_a, x_b = x[0:1], x[1:2]
    z, m2, xn, a0, a1, mine, x_a, x_b = barrier(z, m2, xn, a0, a1, mine, x_a, x_b)

    w4_a, send_a = take_next(0, ids_z, z, m2, cross)
    x5_a = swap(w4_a, "row", 1)
    z_a = swap(send_a, "row", 2)
    w7_a = swap_middle(x_a)
    other = swap(mine, "col", 1)
    b0 = add_field(cross, 0, ids_b, [xn, w4_a], a0)
    w4_b, send_b = take_next(1, after(ids_z, b0), z, m2, cross)
    b1 = add_field(cross, 1, ids_b, [xn, w4_b], a1)
    x5_a, z_a, w7_a, other, b0, w4_b, send_b, x_b, xn, m2 = barrier(
        x5_a, z_a, w7_a, other, b0, w4_b, send_b, x_b, xn, m2
    )

    x5_b = swap(w4_b, "row", 1)
    z_b = swap(send_b, "row", 2)
    w7_b = swap_middle(x_b)
    other_xn = swap(xn, "col", 1)
    other_m2 = swap(m2, "col", 1)
    early = [mine, xn, m2, xn, xn, other, other_xn, other_m2, other_xn, other_xn]
    sums_a, field_a = add_late(cross, 0, late_ids, [x5_a, z_a, w7_a], [z, z], b0, early)
    x5_b, z_b, w7_b, sums_a, field_a, b1, other_xn, other_m2, x5_a, w7_a = barrier(
        x5_b, z_b, w7_b, sums_a, field_a, b1, other_xn, other_m2, x5_a, w7_a
    )

    late = [w7_a, x5_a, w7_b, x5_b]
    others = [swap(piece, "col", 1) for piece in late]
    early = [mine, xn, m2, xn, xn, other, other_xn, other_m2, other_xn, other_xn]
    sums_b, field_b = add_late(cross, 1, late_ids, [x5_b, z_b, w7_b], [z_a, z_b], b1, early)
    groups = [
        (field_a, sums_a, *late[:2], *others[:2]),
        (field_b, sums_b, *late[2:], *others[2:]),
    ]
    return dot_rows(ids_dot, norms, groups)


def sums_by_gather(cross, replicas, norms):
    rows, half = cross.shape[2], cross.shape[3]
    row_index, col_index = lax.axis_index("row"), lax.axis_index("col")
    first_row = row_index * rows
    holder = first_row // half
    whole = lax.all_gather(replicas, "row", axis=3, tiled=True)[:, :, 0]
    parts = jnp.einsum("fark,fbks->fabrs", cross, whole, preferred_element_type=jnp.float32)
    field = jnp.stack([parts[:, 0, 0] - parts[:, 1, 1], parts[:, 0, 1] + parts[:, 1, 0]], axis=1)
    own_rows = lax.dynamic_slice_in_dim(whole, first_row - holder * half, rows, 2)
    block_rows = jnp.where(holder == col_index, own_rows, swap(own_rows, "col", 1))
    numer = jnp.sum(block_rows.astype(jnp.float32) * field, axis=(1, 2))
    return jnp.concatenate([numer, norms])


def body(cross_spectra, replicas, tile_order):
    fnum = cross_spectra.shape[0]
    sources = replicas.shape[4]
    own = replicas[:, :, 0].astype(jnp.float32)
    norms = jnp.sum(own * own, axis=(1, 2))
    doubling = (
        lax.axis_size("row") == 8
        and fnum == 2
        and replicas.shape[3] % 128 == 0
        and cross_spectra.shape[2] == 2 * replicas.shape[3]
    )
    sums = (sums_by_swaps if doubling else sums_by_gather)(cross_spectra, replicas, norms)
    sums = sum_all(sums)
    numer, norms = sums[:fnum], sums[fnum:]
    beam = numer / (norms + 1e-06)
    width = sources // lax.axis_size("col")
    beam_half = lax.dynamic_slice_in_dim(beam, lax.axis_index("col") * width, width, 1)
    peak = jnp.max(jnp.abs(beam), axis=1) + 1e-06
    count = tile_order.shape[0]
    picker = (tile_order[:, None] == jnp.arange(count, dtype=jnp.int32)[None, :]).astype(jnp.float32)
    tiles = beam.reshape(fnum, count, sources // count)
    refined = (
        jnp.einsum("tu,fup->ftp", picker, tiles, precision=lax.Precision.HIGHEST)
        / peak[:, None, None]
    )
    return (beam_half, refined)


def solution(mesh):
    in_specs = (P("groups", None, "row", "col"), P("groups", None, "col", "row", None), P("groups"))
    out_specs = (P("groups", "col"), P("groups", None, None))
    return jax.shard_map(body, mesh=mesh, in_specs=in_specs, out_specs=out_specs, check_vma=False)
```

```python
import functools
import math

import jax
import jax.numpy as jnp
from jax import lax
from jax.experimental import pallas as pl
from jax.experimental.pallas import tpu as pltpu
from jax.sharding import PartitionSpec as P

VMEM_LIMIT = 63 * 1024 * 1024
HINT = pl.CostEstimate(flops=1, bytes_accessed=1, transcendentals=0)
ANYWHERE = pl.BlockSpec(memory_space=pl.ANY)


def swap(value, axis, mask):
    size = math.prod(lax.axis_size(name) for name in (axis if isinstance(axis, tuple) else (axis,)))
    return lax.ppermute(value, axis, [(source, source ^ mask) for source in range(size)])


def swap_middle(value):
    axes = ("row", "col")
    size = lax.axis_size("row") * lax.axis_size("col")
    target = lambda k: k ^ 12 if (k // 4) % 4 in (1, 2) else k ^ 1
    return lax.ppermute(value, axes, [(k, target(k)) for k in range(size)])


def after(value, *others):
    return lax.optimization_barrier((value, *others))[0]


def sum_all(value):
    axes = ("row", "col")
    size = lax.axis_size("row") * lax.axis_size("col")
    if size > 16:
        return lax.psum(value, axes)
    copies = jnp.broadcast_to(value[None], (size, *value.shape))
    return jnp.sum(lax.all_to_all(copies, axes, 0, 0, tiled=True), axis=0)


def dot(a, b):
    return jnp.dot(a, b, preferred_element_type=jnp.float32)


def at_freq(ref, freq):
    return ref.at[freq if ref.shape[0] > 1 else 0]


def weight_copies(freq, ref, right, sem):
    low = pl.ds(0, ref.shape[2])
    source = at_freq(ref, freq)
    return [
        pltpu.make_async_copy(source.at[0], right.at[0, low], sem.at[0]),
        pltpu.make_async_copy(source.at[1], right.at[1, low], sem.at[1]),
    ]


def spread(right):
    width = right.shape[1] // 2
    right[0, width:] = -right[1, :width]
    right[1, width:] = right[0, :width]


def spectra_copies(freq, column, cross, left, sem):
    width = left.shape[1] // 2
    columns = pl.ds(pl.multiple_of(column * width, width), width)
    return [
        pltpu.make_async_copy(
            cross.at[freq, part, :, columns], left.at[:, pl.ds(part * width, width)], sem.at[part]
        )
        for part in range(2)
    ]


def field_kernel(freq, count, has_total, gated, ids, cross, *refs):
    w_refs, refs = refs[:count], refs[count:]
    total, refs = (refs[0], refs[1:]) if has_total else (None, refs)
    out, left, right, l_sem, w_sem, field, tot, tot_sem = refs
    piece, part = pl.program_id(0), pl.program_id(1)
    copies = [
        weight_copies(freq, ref, right.at[k], w_sem.at[k])
        + spectra_copies(freq, ids[k], cross, left.at[k], l_sem.at[k])
        for k, ref in enumerate(w_refs)
    ]
    for k, group in enumerate(copies):

        @pl.when((piece == k) & (part == 0))
        def _(k=k, group=group):
            if k == 0:
                for copy in group:
                    copy.start()
            for copy in group:
                copy.wait()
            if k + 1 < count:
                for copy in copies[k + 1]:
                    copy.start()
            if k == 0 and has_total:
                pltpu.make_async_copy(total, tot, tot_sem.at[0]).start()
            spread(right.at[k])

    last = piece == count - 1
    if count > 1:

        @pl.when(piece == 0)
        def _():
            field[part] = dot(left[piece], right[piece, part])

        @pl.when((piece > 0) & (piece < count - 1))
        def _():
            field[part] += dot(left[piece], right[piece, part])

    @pl.when(last)
    def _():
        value = dot(left[piece], right[piece, part])
        if gated:
            value = jnp.where(ids[count] == 1, value, 0.0)
        if count > 1:
            value += field[part]
        if has_total:

            @pl.when(part == 0)
            def _():
                pltpu.make_async_copy(total, tot, tot_sem.at[0]).wait()

            value += tot[part]
        out[0] = value


def add_field(cross, freq, ids, pieces, total=None, gated=False):
    rows, (width, sources) = cross.shape[2], pieces[0].shape[2:]
    count, dtype = len(pieces), pieces[0].dtype
    has_total = total is not None
    return pl.pallas_call(
        functools.partial(field_kernel, freq, count, has_total, gated),
        out_shape=jax.ShapeDtypeStruct((2, rows, sources), jnp.float32),
        grid_spec=pltpu.PrefetchScalarGridSpec(
            num_scalar_prefetch=1,
            grid=(count, 2),
            in_specs=[ANYWHERE] * (1 + count + has_total),
            out_specs=pl.BlockSpec(
                (1, rows, sources), lambda p, part, ids: (jnp.where(p == count - 1, part, 0), 0, 0)
            ),
            scratch_shapes=[
                pltpu.VMEM((count, rows, 2 * width), dtype),
                pltpu.VMEM((count, 2, 2 * width, sources), dtype),
                pltpu.SemaphoreType.DMA((count, 2)),
                pltpu.SemaphoreType.DMA((count, 2)),
                pltpu.VMEM((2, rows, sources), jnp.float32),
                pltpu.VMEM((2, rows, sources), jnp.float32),
                pltpu.SemaphoreType.DMA((1,)),
            ],
        ),
        compiler_params=pltpu.CompilerParams(vmem_limit_bytes=VMEM_LIMIT),
        cost_estimate=HINT,
    )(ids, cross, *pieces, *([total] if has_total else []))


def start_rows(freq, ids, base, refs, rows, sem):
    width = rows.shape[1] // 2
    views = []
    for picked, *pieces in (refs[:5], refs[5:]):
        views += [picked.at[freq, :, pl.ds(slot * width, width)] for slot in range(2)]
        views += [at_freq(ref, freq) for ref in pieces]
    for slot in range(2):
        here = pl.ds(slot * width, width)
        for k, source in enumerate(views):

            @pl.when(ids[base + slot] == k)
            def _(source=source, slot=slot, here=here):
                pltpu.make_async_copy(source, rows.at[:, here], sem.at[slot]).start()


def wait_rows(freq, slot, refs, rows, sem):
    width = rows.shape[1] // 2
    source = refs[0].at[freq, :, pl.ds(0, width)]
    here = rows.at[:, pl.ds(slot * width, width)]
    pltpu.make_async_copy(source, here, sem.at[slot]).wait()


def fold(rows, field):
    product = rows.astype(jnp.float32) * field
    return jnp.sum(product.reshape(-1, 8, product.shape[-1]), axis=0)


def late_kernel(freq, ids, cross, w5, w6, w7, block_re, block_im, total, *refs):
    row_refs, refs = refs[:10], refs[10:]
    sums, field_out, left, right, l_sem, w_sem, field, tot, sem, rows, row_sem = refs
    late = ids[7]
    step, part = pl.program_id(0), pl.program_id(1)
    width = w5.shape[2]
    first = weight_copies(freq, w5, right.at[0], w_sem.at[0]) + spectra_copies(
        freq, ids[0], cross, left.at[0], l_sem.at[0]
    )
    six = weight_copies(freq, w6, right.at[1], w_sem.at[1])
    seven = weight_copies(freq, w7, right.at[1], w_sem.at[1])
    second = spectra_copies(freq, ids[1], cross, left.at[1], l_sem.at[1])
    third = [
        pltpu.make_async_copy(
            ref.at[min(k, ref.shape[0] - 1), half],
            left.at[2, pl.ds(half * width, width), pl.ds(k * width, width)],
            l_sem.at[2 + half, k],
        )
        for k, ref in enumerate((block_re, block_im))
        for half in range(2)
    ]
    total_copy = pltpu.make_async_copy(total, tot, sem.at[0])
    late_rows = pl.ds(pl.multiple_of(jnp.minimum(late, 1) * width, width), width)
    out_copies = [
        pltpu.make_async_copy(field.at[k, late_rows], field_out.at[k], sem.at[1 + k])
        for k in range(2)
    ]

    @pl.when((step == 0) & (part == 0))
    def _():
        sums[...] = jnp.zeros_like(sums)
        for copy in first:
            copy.start()
        for copy in first:
            copy.wait()
        for copy in second:
            copy.start()

        @pl.when(ids[2] == 1)
        def _():
            for copy in seven:
                copy.start()

        @pl.when(ids[2] == 0)
        def _():
            for copy in six:
                copy.start()

        total_copy.start()
        start_rows(freq, ids, 3, row_refs, rows.at[0], row_sem.at[0])
        spread(right.at[0])

    @pl.when((step == 1) & (part == 0))
    def _():
        for copy in second + six:
            copy.wait()
        for copy in third:
            copy.start()
        start_rows(freq, ids, 5, row_refs, rows.at[1], row_sem.at[1])
        total_copy.wait()
        for slot in range(2):
            wait_rows(freq, slot, row_refs, rows.at[0], row_sem.at[0])
        spread(right.at[1])

    @pl.when((step == 2) & (part == 0))
    def _():
        for copy in third:
            copy.wait()
        for slot in range(2):
            wait_rows(freq, slot, row_refs, rows.at[1], row_sem.at[1])

    @pl.when(step == 0)
    def _():
        field[part] = dot(left[0], right[0, part])

    for k in range(2):

        @pl.when((step == 1) & (part == k))
        def _(k=k):
            field[k] = field[k] + tot[k] + dot(left[1], right[1, k])
            out_copies[k].start()
            for slot in range(2):

                @pl.when(late != slot)
                def _(slot=slot):
                    here = slice(slot * width, (slot + 1) * width)
                    sums[...] += fold(rows[0, k, here], field[k, here])

    @pl.when((step == 2) & (ids[2] == 1))
    def _():
        sums[...] += fold(rows[1, part], dot(left[2], right[0, part]))

    @pl.when((step == 2) & (part == 1))
    def _():
        for copy in out_copies:
            copy.wait()


def add_late(cross, freq, ids, pieces, blocks, total, row_refs):
    rows, (width, sources) = cross.shape[2], pieces[0].shape[2:]
    dtype = pieces[0].dtype
    return pl.pallas_call(
        functools.partial(late_kernel, freq),
        out_shape=(
            jax.ShapeDtypeStruct((8, sources), jnp.float32),
            jax.ShapeDtypeStruct((2, width, sources), jnp.float32),
        ),
        grid_spec=pltpu.PrefetchScalarGridSpec(
            num_scalar_prefetch=1,
            grid=(3, 2),
            in_specs=[ANYWHERE] * (7 + len(row_refs)),
            out_specs=(pl.BlockSpec((8, sources), lambda step, part, ids: (0, 0)), ANYWHERE),
            scratch_shapes=[
                pltpu.VMEM((3, rows, 2 * width), dtype),
                pltpu.VMEM((2, 2, 2 * width, sources), dtype),
                pltpu.SemaphoreType.DMA((4, 2)),
                pltpu.SemaphoreType.DMA((2, 2)),
                pltpu.VMEM((2, rows, sources), jnp.float32),
                pltpu.VMEM((2, rows, sources), jnp.float32),
                pltpu.SemaphoreType.DMA((3,)),
                pltpu.VMEM((2, 2, rows, sources), dtype),
                pltpu.SemaphoreType.DMA((2, 2)),
            ],
        ),
        compiler_params=pltpu.CompilerParams(vmem_limit_bytes=VMEM_LIMIT),
        cost_estimate=HINT,
    )(ids, cross, *pieces, *blocks, total, *row_refs)


def dot_kernel(ids, norms, *refs):
    groups, (out, rows, field, sem) = (refs[:6], refs[6:12]), refs[12:]
    for freq, (field_ref, _, *sources) in enumerate(groups):

        @pl.when(ids[0] < 4)
        def _(freq=freq, field_ref=field_ref):
            pltpu.make_async_copy(field_ref, field.at[freq], sem.at[0, freq]).start()

        for k, source in enumerate(sources):

            @pl.when(ids[0] == k)
            def _(freq=freq, source=source):
                pltpu.make_async_copy(source.at[0], rows.at[freq], sem.at[1, freq]).start()

    for freq, (field_ref, sums, *sources) in enumerate(groups):
        out[freq : freq + 1] = jnp.sum(sums[...], axis=0, keepdims=True)

        @pl.when(ids[0] < 4)
        def _(freq=freq, field_ref=field_ref, sources=sources):
            pltpu.make_async_copy(field_ref, field.at[freq], sem.at[0, freq]).wait()
            pltpu.make_async_copy(sources[0].at[0], rows.at[freq], sem.at[1, freq]).wait()
            more = sum(fold(rows[freq, part], field[freq, part]) for part in range(2))
            out[freq : freq + 1] += jnp.sum(more, axis=0, keepdims=True)

    out[2:4] = norms[...]


def dot_rows(ids, norms, groups):
    late_shape, dtype = groups[0][0].shape, groups[0][2].dtype
    sources = late_shape[-1]
    whole = lambda shape: pl.BlockSpec(shape, lambda i, ids: (0, 0))
    return pl.pallas_call(
        dot_kernel,
        out_shape=jax.ShapeDtypeStruct((4, sources), jnp.float32),
        grid_spec=pltpu.PrefetchScalarGridSpec(
            num_scalar_prefetch=1,
            grid=(1,),
            in_specs=[whole((2, sources))] + [ANYWHERE, whole((8, sources)), *[ANYWHERE] * 4] * 2,
            out_specs=whole((4, sources)),
            scratch_shapes=[
                pltpu.VMEM((2, *late_shape), dtype),
                pltpu.VMEM((2, *late_shape), jnp.float32),
                pltpu.SemaphoreType.DMA((2, 2)),
            ],
        ),
        compiler_params=pltpu.CompilerParams(vmem_limit_bytes=VMEM_LIMIT),
        cost_estimate=HINT,
    )(ids, norms, *groups[0], *groups[1])


def copy_kernel(inputs, jobs, ids, *refs):
    refs, (stage, in_sem, out_sem) = refs[:-3], refs[-3:]
    sources, targets = refs[:inputs], refs[inputs:]
    writes = [
        pltpu.make_async_copy(stage.at[k], target(targets), out_sem.at[k])
        for k, (_, target) in enumerate(jobs)
    ]

    def each(act):
        for k, (options, _) in enumerate(jobs):
            for value, source in options:

                @pl.when(ids[0] == value)
                def _(k=k, source=source):
                    act(k, pltpu.make_async_copy(source(sources, ids), stage.at[k], in_sem.at[k]))

    def pass_on(k, copy):
        copy.wait()
        writes[k].start()

    def finish(k, copy):
        writes[k].wait()

    each(lambda k, copy: copy.start())
    each(pass_on)
    each(finish)


def copies(ids, args, jobs, shapes, unit, dtype, alias=None):
    return pl.pallas_call(
        functools.partial(copy_kernel, len(args), jobs),
        out_shape=[jax.ShapeDtypeStruct(shape, dtype) for shape in shapes],
        grid_spec=pltpu.PrefetchScalarGridSpec(
            num_scalar_prefetch=1,
            grid=(1,),
            in_specs=[ANYWHERE] * len(args),
            out_specs=[ANYWHERE] * len(shapes),
            scratch_shapes=[
                pltpu.VMEM((len(jobs), *unit), dtype),
                pltpu.SemaphoreType.DMA((len(jobs),)),
                pltpu.SemaphoreType.DMA((len(jobs),)),
            ],
        ),
        input_output_aliases={} if alias is None else {1 + alias: 0},
        compiler_params=pltpu.CompilerParams(vmem_limit_bytes=VMEM_LIMIT),
        cost_estimate=HINT,
    )(ids, *args)


def block_source(at, freq, part, half, width):
    def source(refs, ids):
        columns = pl.ds(pl.multiple_of(ids[1] * width, width), width)
        return refs[at].at[freq, part, pl.ds(half * width, width), columns]

    return source


def entry(at, *index):
    return lambda refs, ids=None: refs[at].at[index]


def fill_block(ids, piece, cross):
    _, _, width, sources = piece.shape
    jobs = [
        ([(0, block_source(1, 0, part, half, width))], entry(0, part, half))
        for part in range(2)
        for half in range(2)
    ]
    return copies(ids, [piece, cross], jobs, [piece.shape], (width, sources), piece.dtype, 0)[0]


def take_pair(ids, own, x, n, m):
    freqs, _, width, sources = own.shape
    jobs = [
        (
            [(0, entry(slot, freq, part)), (1, entry(2 + slot, freq, part))],
            entry(0, freq, part, pl.ds(slot * width, width)),
        )
        for freq in range(freqs)
        for part in range(2)
        for slot in range(2)
    ]
    shape = (freqs, 2, 2 * width, sources)
    return copies(ids, [own, x, n, m], jobs, [shape], (width, sources), own.dtype)[0]


def take_next(freq, ids, ends, middles, cross):
    _, _, width, sources = ends.shape
    jobs = []
    for part in range(2):
        block = block_source(2, 1, freq, part, width)
        jobs.append(([(0, block), (1, entry(1, freq, part))], entry(1, 0, part)))
        jobs.append(([(0, entry(0, freq, part)), (1, entry(1, freq, part))], entry(0, 0, part)))
    shape = (1, 2, width, sources)
    args = [ends, middles, cross]
    return copies(ids, args, jobs, [shape, shape], (width, sources), ends.dtype)


def sums_by_swaps(cross, replicas, norms):
    rows, half = cross.shape[2], cross.shape[3]
    width = replicas.shape[3]
    me = lax.axis_index("row").astype(jnp.int32)
    col = lax.axis_index("col").astype(jnp.int32)
    holds = me * rows // half == col
    mid = ((me // 2) % 4 == 1) | ((me // 2) % 4 == 2)
    flag = lambda value: jnp.where(value, 1, 0).astype(jnp.int32).reshape(1)
    ids = lambda *wanted: me ^ jnp.array(wanted, jnp.int32)
    barrier = lambda *values: lax.optimization_barrier(values)

    slots = jnp.arange(2, dtype=jnp.int32)
    per_half = half // width
    own_masks = (2 * me % per_half + slots) ^ me
    next_masks = ((2 * (me ^ 2) % per_half + slots) ^ me) & 3
    table = lambda masks: sum(
        jnp.where(masks == mask, place, 0)
        for mask, place in enumerate((0, 1, 0, 2, 3, 5, 1, 4))
    ) + jnp.where(holds, 0, 6)
    late_slot = own_masks[0] & 1 ^ 1
    late_source = jnp.where(own_masks[0] & 2 != 0, 0, 1) + jnp.where(holds, 0, 2)
    ids_dot = jnp.where(mid, late_source, 4).astype(jnp.int32).reshape(1)
    late_ids = jnp.concatenate(
        [
            ids(5),
            jnp.where(mid, ids(7), ids(6)),
            flag(mid),
            table(own_masks),
            table(next_masks),
            jnp.where(mid, late_slot, 2).reshape(1),
        ]
    ).astype(jnp.int32)
    pair = flag(((me >> 1) ^ me) & 1 != 0)
    ids_a = jnp.concatenate([ids(1, 2, 6), flag(mid)])
    ids_z = jnp.concatenate([flag(mid), ids(7)])
    numbers = [ids_a, ids(3, 4), ids_z, late_ids, pair, ids_dot]

    own = replicas[:, :, 0]
    x = swap(own, "row", 1)
    n = swap(own, "row", 2)
    m = swap_middle(own)
    a0 = add_field(cross, 0, ids(0), [own])
    a1 = add_field(cross, 1, ids(0), [own])
    m = fill_block(ids_z, m, cross)
    x, n, m, a0, a1, norms, *numbers = barrier(x, n, m, a0, a1, norms, *numbers)
    ids_a, ids_b, ids_z, late_ids, pair, ids_dot = numbers

    z = swap(m, "row", 2)
    m2 = swap_middle(n)
    xn = swap(n, "row", 1)
    a0 = add_field(cross, 0, ids_a, [x, n, m], a0, gated=True)
    a1 = add_field(cross, 1, ids_a, [x, n, m], a1, gated=True)
    mine = take_pair(pair, own, x, n, m)
    x_a, x_b = x[0:1], x[1:2]
    z, m2, xn, a0, a1, mine, x_a, x_b = barrier(z, m2, xn, a0, a1, mine, x_a, x_b)

    w4_a, send_a = take_next(0, ids_z, z, m2, cross)
    x5_a = swap(w4_a, "row", 1)
    z_a = swap(send_a, "row", 2)
    w7_a = swap_middle(x_a)
    other = swap(mine, "col", 1)
    b0 = add_field(cross, 0, ids_b, [xn, w4_a], a0)
    w4_b, send_b = take_next(1, after(ids_z, b0), z, m2, cross)
    b1 = add_field(cross, 1, ids_b, [xn, w4_b], a1)
    x5_a, z_a, w7_a, other, b0, w4_b, send_b, x_b, xn, m2 = barrier(
        x5_a, z_a, w7_a, other, b0, w4_b, send_b, x_b, xn, m2
    )

    x5_b = swap(w4_b, "row", 1)
    z_b = swap(send_b, "row", 2)
    w7_b = swap_middle(x_b)
    other_xn = swap(xn, "col", 1)
    other_m2 = swap(m2, "col", 1)
    early = [mine, xn, m2, xn, xn, other, other_xn, other_m2, other_xn, other_xn]
    sums_a, field_a = add_late(cross, 0, late_ids, [x5_a, z_a, w7_a], [z, z], b0, early)
    x5_b, z_b, w7_b, sums_a, field_a, b1, other_xn, other_m2, x5_a, w7_a = barrier(
        x5_b, z_b, w7_b, sums_a, field_a, b1, other_xn, other_m2, x5_a, w7_a
    )

    late = [w7_a, x5_a, w7_b, x5_b]
    others = [swap(piece, "col", 1) for piece in late]
    early = [mine, xn, m2, xn, xn, other, other_xn, other_m2, other_xn, other_xn]
    sums_b, field_b = add_late(cross, 1, late_ids, [x5_b, z_b, w7_b], [z_a, z_b], b1, early)
    groups = [
        (field_a, sums_a, *late[:2], *others[:2]),
        (field_b, sums_b, *late[2:], *others[2:]),
    ]
    return dot_rows(ids_dot, norms, groups)


def sums_by_gather(cross, replicas, norms):
    rows, half = cross.shape[2], cross.shape[3]
    row_index, col_index = lax.axis_index("row"), lax.axis_index("col")
    first_row = row_index * rows
    holder = first_row // half
    whole = lax.all_gather(replicas, "row", axis=3, tiled=True)[:, :, 0]
    parts = jnp.einsum("fark,fbks->fabrs", cross, whole, preferred_element_type=jnp.float32)
    field = jnp.stack([parts[:, 0, 0] - parts[:, 1, 1], parts[:, 0, 1] + parts[:, 1, 0]], axis=1)
    own_rows = lax.dynamic_slice_in_dim(whole, first_row - holder * half, rows, 2)
    block_rows = jnp.where(holder == col_index, own_rows, swap(own_rows, "col", 1))
    numer = jnp.sum(block_rows.astype(jnp.float32) * field, axis=(1, 2))
    return jnp.concatenate([numer, norms])


def body(cross_spectra, replicas, tile_order):
    fnum = cross_spectra.shape[0]
    sources = replicas.shape[4]
    own = replicas[:, :, 0].astype(jnp.float32)
    norms = jnp.sum(own * own, axis=(1, 2))
    doubling = (
        lax.axis_size("row") == 8
        and fnum == 2
        and replicas.shape[3] % 128 == 0
        and cross_spectra.shape[2] == 2 * replicas.shape[3]
    )
    sums = (sums_by_swaps if doubling else sums_by_gather)(cross_spectra, replicas, norms)
    sums = sum_all(sums)
    numer, norms = sums[:fnum], sums[fnum:]
    beam = numer / (norms + 1e-06)
    width = sources // lax.axis_size("col")
    beam_half = lax.dynamic_slice_in_dim(beam, lax.axis_index("col") * width, width, 1)
    peak = jnp.max(jnp.abs(beam), axis=1) + 1e-06
    count = tile_order.shape[0]
    picker = (tile_order[:, None] == jnp.arange(count, dtype=jnp.int32)[None, :]).astype(jnp.float32)
    tiles = beam.reshape(fnum, count, sources // count)
    refined = (
        jnp.einsum("tu,fup->ftp", picker, tiles, precision=lax.Precision.HIGHEST)
        / peak[:, None, None]
    )
    return (beam_half, refined)


def solution(mesh):
    in_specs = (P("groups", None, "row", "col"), P("groups", None, "col", "row", None), P("groups"))
    out_specs = (P("groups", "col"), P("groups", None, None))
    return jax.shard_map(body, mesh=mesh, in_specs=in_specs, out_specs=out_specs, check_vma=False)
```

```python
import functools
import math

import jax
import jax.numpy as jnp
from jax import lax
from jax.experimental import pallas as pl
from jax.experimental.pallas import tpu as pltpu
from jax.sharding import PartitionSpec as P

VMEM_LIMIT = 63 * 1024 * 1024
HINT = pl.CostEstimate(flops=1, bytes_accessed=1, transcendentals=0)
ANYWHERE = pl.BlockSpec(memory_space=pl.ANY)


def swap(value, axis, mask):
    size = math.prod(lax.axis_size(name) for name in (axis if isinstance(axis, tuple) else (axis,)))
    return lax.ppermute(value, axis, [(source, source ^ mask) for source in range(size)])


def swap_middle(value):
    axes = ("row", "col")
    size = lax.axis_size("row") * lax.axis_size("col")
    target = lambda k: k ^ 12 if (k // 4) % 4 in (1, 2) else k ^ 1
    return lax.ppermute(value, axes, [(k, target(k)) for k in range(size)])


def after(value, *others):
    return lax.optimization_barrier((value, *others))[0]


def copies_to_all():
    size = lax.axis_size("row") * lax.axis_size("col")
    return size if size <= 16 else 1


def sum_all(copies):
    axes = ("row", "col")
    if copies.shape[0] == 1:
        return lax.psum(copies[0], axes)
    return jnp.sum(lax.all_to_all(copies, axes, 0, 0, tiled=True), axis=0)


def dot(a, b):
    return jnp.dot(a, b, preferred_element_type=jnp.float32)


def at_freq(ref, freq):
    return ref.at[freq if ref.shape[0] > 1 else 0]


def weight_copies(freq, ref, right, sem):
    low = pl.ds(0, ref.shape[2])
    source = at_freq(ref, freq)
    return [
        pltpu.make_async_copy(source.at[0], right.at[0, low], sem.at[0]),
        pltpu.make_async_copy(source.at[1], right.at[1, low], sem.at[1]),
    ]


def spread(right):
    width = right.shape[1] // 2
    right[0, width:] = -right[1, :width]
    right[1, width:] = right[0, :width]


def spectra_copies(freq, column, cross, left, sem):
    width = left.shape[1] // 2
    columns = pl.ds(pl.multiple_of(column * width, width), width)
    return [
        pltpu.make_async_copy(
            cross.at[freq, part, :, columns], left.at[:, pl.ds(part * width, width)], sem.at[part]
        )
        for part in range(2)
    ]


def field_kernel(freq, count, has_total, gated, ids, cross, *refs):
    w_refs, refs = refs[:count], refs[count:]
    total, refs = (refs[0], refs[1:]) if has_total else (None, refs)
    out, left, right, l_sem, w_sem, field, tot, tot_sem = refs
    piece, part = pl.program_id(0), pl.program_id(1)
    copies = [
        weight_copies(freq, ref, right.at[k], w_sem.at[k])
        + spectra_copies(freq, ids[k], cross, left.at[k], l_sem.at[k])
        for k, ref in enumerate(w_refs)
    ]
    for k, group in enumerate(copies):

        @pl.when((piece == k) & (part == 0))
        def _(k=k, group=group):
            if k == 0:
                for copy in group:
                    copy.start()
            for copy in group:
                copy.wait()
            if k + 1 < count:
                for copy in copies[k + 1]:
                    copy.start()
            if k == 0 and has_total:
                pltpu.make_async_copy(total, tot, tot_sem.at[0]).start()
            spread(right.at[k])

    last = piece == count - 1
    if count > 1:

        @pl.when(piece == 0)
        def _():
            field[part] = dot(left[piece], right[piece, part])

        @pl.when((piece > 0) & (piece < count - 1))
        def _():
            field[part] += dot(left[piece], right[piece, part])

    @pl.when(last)
    def _():
        value = dot(left[piece], right[piece, part])
        if gated:
            value = jnp.where(ids[count] == 1, value, 0.0)
        if count > 1:
            value += field[part]
        if has_total:

            @pl.when(part == 0)
            def _():
                pltpu.make_async_copy(total, tot, tot_sem.at[0]).wait()

            value += tot[part]
        out[0] = value


def add_field(cross, freq, ids, pieces, total=None, gated=False):
    rows, (width, sources) = cross.shape[2], pieces[0].shape[2:]
    count, dtype = len(pieces), pieces[0].dtype
    has_total = total is not None
    return pl.pallas_call(
        functools.partial(field_kernel, freq, count, has_total, gated),
        out_shape=jax.ShapeDtypeStruct((2, rows, sources), jnp.float32),
        grid_spec=pltpu.PrefetchScalarGridSpec(
            num_scalar_prefetch=1,
            grid=(count, 2),
            in_specs=[ANYWHERE] * (1 + count + has_total),
            out_specs=pl.BlockSpec(
                (1, rows, sources), lambda p, part, ids: (jnp.where(p == count - 1, part, 0), 0, 0)
            ),
            scratch_shapes=[
                pltpu.VMEM((count, rows, 2 * width), dtype),
                pltpu.VMEM((count, 2, 2 * width, sources), dtype),
                pltpu.SemaphoreType.DMA((count, 2)),
                pltpu.SemaphoreType.DMA((count, 2)),
                pltpu.VMEM((2, rows, sources), jnp.float32),
                pltpu.VMEM((2, rows, sources), jnp.float32),
                pltpu.SemaphoreType.DMA((1,)),
            ],
        ),
        compiler_params=pltpu.CompilerParams(vmem_limit_bytes=VMEM_LIMIT),
        cost_estimate=HINT,
    )(ids, cross, *pieces, *([total] if has_total else []))


def start_rows(freq, ids, base, refs, rows, sem):
    width = rows.shape[1] // 2
    views = []
    for picked, *pieces in (refs[:5], refs[5:]):
        views += [picked.at[freq, :, pl.ds(slot * width, width)] for slot in range(2)]
        views += [at_freq(ref, freq) for ref in pieces]
    for slot in range(2):
        here = pl.ds(slot * width, width)
        for k, source in enumerate(views):

            @pl.when(ids[base + slot] == k)
            def _(source=source, slot=slot, here=here):
                pltpu.make_async_copy(source, rows.at[:, here], sem.at[slot]).start()


def wait_rows(freq, slot, refs, rows, sem):
    width = rows.shape[1] // 2
    source = refs[0].at[freq, :, pl.ds(0, width)]
    here = rows.at[:, pl.ds(slot * width, width)]
    pltpu.make_async_copy(source, here, sem.at[slot]).wait()


def fold(rows, field):
    product = rows.astype(jnp.float32) * field
    return jnp.sum(product.reshape(-1, 8, product.shape[-1]), axis=0)


def late_kernel(freq, ids, cross, w5, w6, w7, block_re, block_im, total, *refs):
    row_refs, refs = refs[:10], refs[10:]
    sums, field_out, left, right, l_sem, w_sem, field, tot, sem, rows, row_sem = refs
    late = ids[7]
    step = pl.program_id(0)
    width, sources = w5.shape[2:]
    lanes = [slice(part * sources, (part + 1) * sources) for part in range(2)]

    def weights(ref, k):
        source = at_freq(ref, freq)
        return [
            pltpu.make_async_copy(
                source.at[part],
                right.at[k, pl.ds(0, width), pl.ds(part * sources, sources)],
                w_sem.at[k, part],
            )
            for part in range(2)
        ]

    def spread_lanes(k):
        right[k, width:, lanes[0]] = -right[k, :width, lanes[1]]
        right[k, width:, lanes[1]] = right[k, :width, lanes[0]]

    first = weights(w5, 0) + spectra_copies(freq, ids[0], cross, left.at[0], l_sem.at[0])
    six, seven = weights(w6, 1), weights(w7, 1)
    second = spectra_copies(freq, ids[1], cross, left.at[1], l_sem.at[1])
    third = [
        pltpu.make_async_copy(
            ref.at[min(k, ref.shape[0] - 1), half],
            left.at[2, pl.ds(half * width, width), pl.ds(k * width, width)],
            l_sem.at[2 + half, k],
        )
        for k, ref in enumerate((block_re, block_im))
        for half in range(2)
    ]
    total_copies = [
        pltpu.make_async_copy(
            total.at[part], tot.at[:, pl.ds(part * sources, sources)], sem.at[part]
        )
        for part in range(2)
    ]
    late_rows = pl.ds(pl.multiple_of(jnp.minimum(late, 1) * width, width), width)
    out_copies = [
        pltpu.make_async_copy(
            field.at[late_rows, pl.ds(part * sources, sources)], field_out.at[part], sem.at[2 + part]
        )
        for part in range(2)
    ]

    @pl.when(step == 0)
    def _():
        sums[...] = jnp.zeros_like(sums)
        for copy in first:
            copy.start()
        for copy in first:
            copy.wait()
        for copy in second:
            copy.start()

        @pl.when(ids[2] == 1)
        def _():
            for copy in seven:
                copy.start()

        @pl.when(ids[2] == 0)
        def _():
            for copy in six:
                copy.start()

        for copy in total_copies:
            copy.start()
        start_rows(freq, ids, 3, row_refs, rows.at[0], row_sem.at[0])
        spread_lanes(0)
        field[...] = dot(left[0], right[0])

    @pl.when(step == 1)
    def _():
        for copy in second + six:
            copy.wait()
        for copy in third:
            copy.start()
        start_rows(freq, ids, 5, row_refs, rows.at[1], row_sem.at[1])
        for copy in total_copies:
            copy.wait()
        spread_lanes(1)
        field[...] = field[...] + tot[...] + dot(left[1], right[1])
        for copy in out_copies:
            copy.start()
        for slot in range(2):
            wait_rows(freq, slot, row_refs, rows.at[0], row_sem.at[0])
        for slot in range(2):

            @pl.when(late != slot)
            def _(slot=slot):
                here = slice(slot * width, (slot + 1) * width)
                for part in range(2):
                    sums[...] += fold(rows[0, part, here], field[here, lanes[part]])

    @pl.when(step == 2)
    def _():
        for copy in third:
            copy.wait()
        for slot in range(2):
            wait_rows(freq, slot, row_refs, rows.at[1], row_sem.at[1])

        @pl.when(ids[2] == 1)
        def _():
            value = dot(left[2], right[0])
            for part in range(2):
                sums[...] += fold(rows[1, part], value[:, lanes[part]])

        for copy in out_copies:
            copy.wait()


def add_late(cross, freq, ids, pieces, blocks, total, row_refs):
    rows, (width, sources) = cross.shape[2], pieces[0].shape[2:]
    dtype = pieces[0].dtype
    return pl.pallas_call(
        functools.partial(late_kernel, freq),
        out_shape=(
            jax.ShapeDtypeStruct((8, sources), jnp.float32),
            jax.ShapeDtypeStruct((2, width, sources), jnp.float32),
        ),
        grid_spec=pltpu.PrefetchScalarGridSpec(
            num_scalar_prefetch=1,
            grid=(3,),
            in_specs=[ANYWHERE] * (7 + len(row_refs)),
            out_specs=(pl.BlockSpec((8, sources), lambda step, ids: (0, 0)), ANYWHERE),
            scratch_shapes=[
                pltpu.VMEM((3, rows, 2 * width), dtype),
                pltpu.VMEM((2, 2 * width, 2 * sources), dtype),
                pltpu.SemaphoreType.DMA((4, 2)),
                pltpu.SemaphoreType.DMA((2, 2)),
                pltpu.VMEM((rows, 2 * sources), jnp.float32),
                pltpu.VMEM((rows, 2 * sources), jnp.float32),
                pltpu.SemaphoreType.DMA((4,)),
                pltpu.VMEM((2, 2, rows, sources), dtype),
                pltpu.SemaphoreType.DMA((2, 2)),
            ],
        ),
        compiler_params=pltpu.CompilerParams(vmem_limit_bytes=VMEM_LIMIT),
        cost_estimate=HINT,
    )(ids, cross, *pieces, *blocks, total, *row_refs)


def dot_kernel(ids, norms, *refs):
    groups, (out, rows, field, sem, total) = (refs[:6], refs[6:12]), refs[12:]
    for freq, (field_ref, _, *sources) in enumerate(groups):

        @pl.when(ids[0] < 4)
        def _(freq=freq, field_ref=field_ref):
            pltpu.make_async_copy(field_ref, field.at[freq], sem.at[0, freq]).start()

        for k, source in enumerate(sources):

            @pl.when(ids[0] == k)
            def _(freq=freq, source=source):
                pltpu.make_async_copy(source.at[0], rows.at[freq], sem.at[1, freq]).start()

    for freq, (field_ref, sums, *sources) in enumerate(groups):
        total[freq : freq + 1] = jnp.sum(sums[...], axis=0, keepdims=True)

        @pl.when(ids[0] < 4)
        def _(freq=freq, field_ref=field_ref, sources=sources):
            pltpu.make_async_copy(field_ref, field.at[freq], sem.at[0, freq]).wait()
            pltpu.make_async_copy(sources[0].at[0], rows.at[freq], sem.at[1, freq]).wait()
            more = sum(fold(rows[freq, part], field[freq, part]) for part in range(2))
            total[freq : freq + 1] += jnp.sum(more, axis=0, keepdims=True)

    total[2:4] = norms[...]
    for k in range(out.shape[0]):
        out[k] = total[...]


def dot_rows(ids, norms, groups):
    late_shape, dtype = groups[0][0].shape, groups[0][2].dtype
    sources = late_shape[-1]
    whole = lambda shape: pl.BlockSpec(shape, lambda i, ids: (0, 0))
    return pl.pallas_call(
        dot_kernel,
        out_shape=jax.ShapeDtypeStruct((copies_to_all(), 4, sources), jnp.float32),
        grid_spec=pltpu.PrefetchScalarGridSpec(
            num_scalar_prefetch=1,
            grid=(1,),
            in_specs=[whole((2, sources))] + [ANYWHERE, whole((8, sources)), *[ANYWHERE] * 4] * 2,
            out_specs=pl.BlockSpec((copies_to_all(), 4, sources), lambda i, ids: (0, 0, 0)),
            scratch_shapes=[
                pltpu.VMEM((2, *late_shape), dtype),
                pltpu.VMEM((2, *late_shape), jnp.float32),
                pltpu.SemaphoreType.DMA((2, 2)),
                pltpu.VMEM((4, sources), jnp.float32),
            ],
        ),
        compiler_params=pltpu.CompilerParams(vmem_limit_bytes=VMEM_LIMIT),
        cost_estimate=HINT,
    )(ids, norms, *groups[0], *groups[1])


def copy_kernel(inputs, jobs, ids, *refs):
    refs, (stage, in_sem, out_sem) = refs[:-3], refs[-3:]
    sources, targets = refs[:inputs], refs[inputs:]
    writes = [
        pltpu.make_async_copy(stage.at[k], target(targets), out_sem.at[k])
        for k, (_, target) in enumerate(jobs)
    ]

    def each(act):
        for k, (options, _) in enumerate(jobs):
            for value, source in options:

                @pl.when(ids[0] == value)
                def _(k=k, source=source):
                    act(k, pltpu.make_async_copy(source(sources, ids), stage.at[k], in_sem.at[k]))

    def pass_on(k, copy):
        copy.wait()
        writes[k].start()

    def finish(k, copy):
        writes[k].wait()

    each(lambda k, copy: copy.start())
    each(pass_on)
    each(finish)


def copies(ids, args, jobs, shapes, unit, dtype, alias=None):
    return pl.pallas_call(
        functools.partial(copy_kernel, len(args), jobs),
        out_shape=[jax.ShapeDtypeStruct(shape, dtype) for shape in shapes],
        grid_spec=pltpu.PrefetchScalarGridSpec(
            num_scalar_prefetch=1,
            grid=(1,),
            in_specs=[ANYWHERE] * len(args),
            out_specs=[ANYWHERE] * len(shapes),
            scratch_shapes=[
                pltpu.VMEM((len(jobs), *unit), dtype),
                pltpu.SemaphoreType.DMA((len(jobs),)),
                pltpu.SemaphoreType.DMA((len(jobs),)),
            ],
        ),
        input_output_aliases={} if alias is None else {1 + alias: 0},
        compiler_params=pltpu.CompilerParams(vmem_limit_bytes=VMEM_LIMIT),
        cost_estimate=HINT,
    )(ids, *args)


def block_source(at, freq, part, half, width):
    def source(refs, ids):
        columns = pl.ds(pl.multiple_of(ids[1] * width, width), width)
        return refs[at].at[freq, part, pl.ds(half * width, width), columns]

    return source


def entry(at, *index):
    return lambda refs, ids=None: refs[at].at[index]


def fill_block(ids, piece, cross):
    _, _, width, sources = piece.shape
    jobs = [
        ([(0, block_source(1, 0, part, half, width))], entry(0, part, half))
        for part in range(2)
        for half in range(2)
    ]
    return copies(ids, [piece, cross], jobs, [piece.shape], (width, sources), piece.dtype, 0)[0]


def take_pair(ids, own, x, n, m):
    freqs, _, width, sources = own.shape
    jobs = [
        (
            [(0, entry(slot, freq, part)), (1, entry(2 + slot, freq, part))],
            entry(0, freq, part, pl.ds(slot * width, width)),
        )
        for freq in range(freqs)
        for part in range(2)
        for slot in range(2)
    ]
    shape = (freqs, 2, 2 * width, sources)
    return copies(ids, [own, x, n, m], jobs, [shape], (width, sources), own.dtype)[0]


def take_next(freq, ids, ends, middles, cross):
    _, _, width, sources = ends.shape
    jobs = []
    for part in range(2):
        block = block_source(2, 1, freq, part, width)
        jobs.append(([(0, block), (1, entry(1, freq, part))], entry(1, 0, part)))
        jobs.append(([(0, entry(0, freq, part)), (1, entry(1, freq, part))], entry(0, 0, part)))
    shape = (1, 2, width, sources)
    args = [ends, middles, cross]
    return copies(ids, args, jobs, [shape, shape], (width, sources), ends.dtype)


def sums_by_swaps(cross, replicas, norms):
    rows, half = cross.shape[2], cross.shape[3]
    width = replicas.shape[3]
    me = lax.axis_index("row").astype(jnp.int32)
    col = lax.axis_index("col").astype(jnp.int32)
    holds = me * rows // half == col
    mid = ((me // 2) % 4 == 1) | ((me // 2) % 4 == 2)
    flag = lambda value: jnp.where(value, 1, 0).astype(jnp.int32).reshape(1)
    ids = lambda *wanted: me ^ jnp.array(wanted, jnp.int32)
    barrier = lambda *values: lax.optimization_barrier(values)

    slots = jnp.arange(2, dtype=jnp.int32)
    per_half = half // width
    own_masks = (2 * me % per_half + slots) ^ me
    next_masks = ((2 * (me ^ 2) % per_half + slots) ^ me) & 3
    table = lambda masks: sum(
        jnp.where(masks == mask, place, 0)
        for mask, place in enumerate((0, 1, 0, 2, 3, 5, 1, 4))
    ) + jnp.where(holds, 0, 6)
    late_slot = own_masks[0] & 1 ^ 1
    late_source = jnp.where(own_masks[0] & 2 != 0, 0, 1) + jnp.where(holds, 0, 2)
    ids_dot = jnp.where(mid, late_source, 4).astype(jnp.int32).reshape(1)
    late_ids = jnp.concatenate(
        [
            ids(5),
            jnp.where(mid, ids(7), ids(6)),
            flag(mid),
            table(own_masks),
            table(next_masks),
            jnp.where(mid, late_slot, 2).reshape(1),
        ]
    ).astype(jnp.int32)
    pair = flag(((me >> 1) ^ me) & 1 != 0)
    ids_a = jnp.concatenate([ids(1, 2, 6), flag(mid)])
    ids_z = jnp.concatenate([flag(mid), ids(7)])
    numbers = [ids_a, ids(3, 4), ids_z, late_ids, pair, ids_dot]

    own = replicas[:, :, 0]
    x = swap(own, "row", 1)
    n = swap(own, "row", 2)
    m = swap_middle(own)
    a0 = add_field(cross, 0, ids(0), [own])
    a1 = add_field(cross, 1, ids(0), [own])
    m = fill_block(ids_z, m, cross)
    x, n, m, a0, a1, norms, *numbers = barrier(x, n, m, a0, a1, norms, *numbers)
    ids_a, ids_b, ids_z, late_ids, pair, ids_dot = numbers

    z = swap(m, "row", 2)
    m2 = swap_middle(n)
    xn = swap(n, "row", 1)
    a0 = add_field(cross, 0, ids_a, [x, n, m], a0, gated=True)
    a1 = add_field(cross, 1, ids_a, [x, n, m], a1, gated=True)
    mine = take_pair(pair, own, x, n, m)
    x_a, x_b = x[0:1], x[1:2]
    z, m2, xn, a0, a1, mine, x_a, x_b = barrier(z, m2, xn, a0, a1, mine, x_a, x_b)

    w4_a, send_a = take_next(0, ids_z, z, m2, cross)
    x5_a = swap(w4_a, "row", 1)
    z_a = swap(send_a, "row", 2)
    w7_a = swap_middle(x_a)
    other = swap(mine, "col", 1)
    b0 = add_field(cross, 0, ids_b, [xn, w4_a], a0)
    w4_b, send_b = take_next(1, after(ids_z, b0), z, m2, cross)
    b1 = add_field(cross, 1, ids_b, [xn, w4_b], a1)
    x5_a, z_a, w7_a, other, b0, w4_b, send_b, x_b, xn, m2 = barrier(
        x5_a, z_a, w7_a, other, b0, w4_b, send_b, x_b, xn, m2
    )

    x5_b = swap(w4_b, "row", 1)
    z_b = swap(send_b, "row", 2)
    w7_b = swap_middle(x_b)
    other_xn = swap(xn, "col", 1)
    other_m2 = swap(m2, "col", 1)
    early = [mine, xn, m2, xn, xn, other, other_xn, other_m2, other_xn, other_xn]
    sums_a, field_a = add_late(cross, 0, late_ids, [x5_a, z_a, w7_a], [z, z], b0, early)
    x5_b, z_b, w7_b, sums_a, field_a, b1, other_xn, other_m2, x5_a, w7_a = barrier(
        x5_b, z_b, w7_b, sums_a, field_a, b1, other_xn, other_m2, x5_a, w7_a
    )

    late = [w7_a, x5_a, w7_b, x5_b]
    others = [swap(piece, "col", 1) for piece in late]
    early = [mine, xn, m2, xn, xn, other, other_xn, other_m2, other_xn, other_xn]
    sums_b, field_b = add_late(cross, 1, late_ids, [x5_b, z_b, w7_b], [z_a, z_b], b1, early)
    groups = [
        (field_a, sums_a, *late[:2], *others[:2]),
        (field_b, sums_b, *late[2:], *others[2:]),
    ]
    return dot_rows(ids_dot, norms, groups)


def sums_by_gather(cross, replicas, norms):
    rows, half = cross.shape[2], cross.shape[3]
    row_index, col_index = lax.axis_index("row"), lax.axis_index("col")
    first_row = row_index * rows
    holder = first_row // half
    whole = lax.all_gather(replicas, "row", axis=3, tiled=True)[:, :, 0]
    parts = jnp.einsum("fark,fbks->fabrs", cross, whole, preferred_element_type=jnp.float32)
    field = jnp.stack([parts[:, 0, 0] - parts[:, 1, 1], parts[:, 0, 1] + parts[:, 1, 0]], axis=1)
    own_rows = lax.dynamic_slice_in_dim(whole, first_row - holder * half, rows, 2)
    block_rows = jnp.where(holder == col_index, own_rows, swap(own_rows, "col", 1))
    numer = jnp.sum(block_rows.astype(jnp.float32) * field, axis=(1, 2))
    sums = jnp.concatenate([numer, norms])
    return jnp.broadcast_to(sums[None], (copies_to_all(), *sums.shape))


def body(cross_spectra, replicas, tile_order):
    fnum = cross_spectra.shape[0]
    sources = replicas.shape[4]
    own = replicas[:, :, 0].astype(jnp.float32)
    norms = jnp.sum(own * own, axis=(1, 2))
    doubling = (
        lax.axis_size("row") == 8
        and fnum == 2
        and replicas.shape[3] % 128 == 0
        and cross_spectra.shape[2] == 2 * replicas.shape[3]
    )
    sums = (sums_by_swaps if doubling else sums_by_gather)(cross_spectra, replicas, norms)
    sums = sum_all(sums)
    numer, norms = sums[:fnum], sums[fnum:]
    beam = numer / (norms + 1e-06)
    width = sources // lax.axis_size("col")
    beam_half = lax.dynamic_slice_in_dim(beam, lax.axis_index("col") * width, width, 1)
    peak = jnp.max(jnp.abs(beam), axis=1) + 1e-06
    count = tile_order.shape[0]
    picker = (tile_order[:, None] == jnp.arange(count, dtype=jnp.int32)[None, :]).astype(jnp.float32)
    tiles = beam.reshape(fnum, count, sources // count)
    refined = (
        jnp.einsum("tu,fup->ftp", picker, tiles, precision=lax.Precision.HIGHEST)
        / peak[:, None, None]
    )
    return (beam_half, refined)


def solution(mesh):
    in_specs = (P("groups", None, "row", "col"), P("groups", None, "col", "row", None), P("groups"))
    out_specs = (P("groups", "col"), P("groups", None, None))
    return jax.shard_map(body, mesh=mesh, in_specs=in_specs, out_specs=out_specs, check_vma=False)
```

```python
import functools
import math

import jax
import jax.numpy as jnp
from jax import lax
from jax.experimental import pallas as pl
from jax.experimental.pallas import tpu as pltpu
from jax.sharding import PartitionSpec as P

VMEM_LIMIT = 63 * 1024 * 1024
HINT = pl.CostEstimate(flops=1, bytes_accessed=1, transcendentals=0)
ANYWHERE = pl.BlockSpec(memory_space=pl.ANY)


def swap(value, axis, mask):
    size = math.prod(lax.axis_size(name) for name in (axis if isinstance(axis, tuple) else (axis,)))
    return lax.ppermute(value, axis, [(source, source ^ mask) for source in range(size)])


def swap_middle(value):
    axes = ("row", "col")
    size = lax.axis_size("row") * lax.axis_size("col")
    target = lambda k: k ^ 12 if (k // 4) % 4 in (1, 2) else k ^ 1
    return lax.ppermute(value, axes, [(k, target(k)) for k in range(size)])


def after(value, *others):
    return lax.optimization_barrier((value, *others))[0]


def copies_to_all():
    size = lax.axis_size("row") * lax.axis_size("col")
    return size if size <= 16 else 1


def sum_all(copies):
    axes = ("row", "col")
    if copies.shape[0] == 1:
        return lax.psum(copies[0], axes)
    return jnp.sum(lax.all_to_all(copies, axes, 0, 0, tiled=True), axis=0)


def dot(a, b):
    return jnp.dot(a, b, preferred_element_type=jnp.float32)


def at_freq(ref, freq):
    return ref.at[freq if ref.shape[0] > 1 else 0]


def weight_copies(freq, ref, right, sem):
    low = pl.ds(0, ref.shape[2])
    source = at_freq(ref, freq)
    return [
        pltpu.make_async_copy(source.at[0], right.at[0, low], sem.at[0]),
        pltpu.make_async_copy(source.at[1], right.at[1, low], sem.at[1]),
    ]


def spread(right):
    width = right.shape[1] // 2
    right[0, width:] = -right[1, :width]
    right[1, width:] = right[0, :width]


def spectra_copies(freq, column, cross, left, sem):
    width = left.shape[1] // 2
    columns = pl.ds(pl.multiple_of(column * width, width), width)
    return [
        pltpu.make_async_copy(
            cross.at[freq, part, :, columns], left.at[:, pl.ds(part * width, width)], sem.at[part]
        )
        for part in range(2)
    ]


def field_kernel(freq, count, has_total, gated, ids, cross, *refs):
    w_refs, refs = refs[:count], refs[count:]
    total, refs = (refs[0], refs[1:]) if has_total else (None, refs)
    out, left, right, l_sem, w_sem, field, tot, tot_sem = refs
    piece, part = pl.program_id(0), pl.program_id(1)
    copies = [
        weight_copies(freq, ref, right.at[k], w_sem.at[k])
        + spectra_copies(freq, ids[k], cross, left.at[k], l_sem.at[k])
        for k, ref in enumerate(w_refs)
    ]
    for k, group in enumerate(copies):

        @pl.when((piece == k) & (part == 0))
        def _(k=k, group=group):
            if k == 0:
                for copy in group:
                    copy.start()
            for copy in group:
                copy.wait()
            if k + 1 < count:
                for copy in copies[k + 1]:
                    copy.start()
            if k == 0 and has_total:
                pltpu.make_async_copy(total, tot, tot_sem.at[0]).start()
            spread(right.at[k])

    last = piece == count - 1
    if count > 1:

        @pl.when(piece == 0)
        def _():
            field[part] = dot(left[piece], right[piece, part])

        @pl.when((piece > 0) & (piece < count - 1))
        def _():
            field[part] += dot(left[piece], right[piece, part])

    @pl.when(last)
    def _():
        value = dot(left[piece], right[piece, part])
        if gated:
            value = jnp.where(ids[count] == 1, value, 0.0)
        if count > 1:
            value += field[part]
        if has_total:

            @pl.when(part == 0)
            def _():
                pltpu.make_async_copy(total, tot, tot_sem.at[0]).wait()

            value += tot[part]
        out[0] = value


def add_field(cross, freq, ids, pieces, total=None, gated=False):
    rows, (width, sources) = cross.shape[2], pieces[0].shape[2:]
    count, dtype = len(pieces), pieces[0].dtype
    has_total = total is not None
    return pl.pallas_call(
        functools.partial(field_kernel, freq, count, has_total, gated),
        out_shape=jax.ShapeDtypeStruct((2, rows, sources), jnp.float32),
        grid_spec=pltpu.PrefetchScalarGridSpec(
            num_scalar_prefetch=1,
            grid=(count, 2),
            in_specs=[ANYWHERE] * (1 + count + has_total),
            out_specs=pl.BlockSpec(
                (1, rows, sources), lambda p, part, ids: (jnp.where(p == count - 1, part, 0), 0, 0)
            ),
            scratch_shapes=[
                pltpu.VMEM((count, rows, 2 * width), dtype),
                pltpu.VMEM((count, 2, 2 * width, sources), dtype),
                pltpu.SemaphoreType.DMA((count, 2)),
                pltpu.SemaphoreType.DMA((count, 2)),
                pltpu.VMEM((2, rows, sources), jnp.float32),
                pltpu.VMEM((2, rows, sources), jnp.float32),
                pltpu.SemaphoreType.DMA((1,)),
            ],
        ),
        compiler_params=pltpu.CompilerParams(vmem_limit_bytes=VMEM_LIMIT),
        cost_estimate=HINT,
    )(ids, cross, *pieces, *([total] if has_total else []))


def start_rows(freq, ids, base, refs, rows, sem):
    width = rows.shape[1] // 2
    views = []
    for picked, *pieces in (refs[:5], refs[5:]):
        views += [picked.at[freq, :, pl.ds(slot * width, width)] for slot in range(2)]
        views += [at_freq(ref, freq) for ref in pieces]
    for slot in range(2):
        here = pl.ds(slot * width, width)
        for k, source in enumerate(views):

            @pl.when(ids[base + slot] == k)
            def _(source=source, slot=slot, here=here):
                pltpu.make_async_copy(source, rows.at[:, here], sem.at[slot]).start()


def wait_rows(freq, slot, refs, rows, sem):
    width = rows.shape[1] // 2
    source = refs[0].at[freq, :, pl.ds(0, width)]
    here = rows.at[:, pl.ds(slot * width, width)]
    pltpu.make_async_copy(source, here, sem.at[slot]).wait()


def fold(rows, field):
    product = rows.astype(jnp.float32) * field
    return jnp.sum(product.reshape(-1, 8, product.shape[-1]), axis=0)


def late_kernel(freq, ids, cross, w5, w6, w7, block_re, block_im, total, *refs):
    row_refs, refs = refs[:10], refs[10:]
    sums, field_out, left, right, l_sem, w_sem, field, tot, sem, rows, row_sem = refs
    late = ids[7]
    step = pl.program_id(0)
    width, sources = w5.shape[2:]
    lanes = [slice(part * sources, (part + 1) * sources) for part in range(2)]

    def weights(ref, k):
        source = at_freq(ref, freq)
        return [
            pltpu.make_async_copy(
                source.at[part],
                right.at[k, pl.ds(0, width), pl.ds(part * sources, sources)],
                w_sem.at[k, part],
            )
            for part in range(2)
        ]

    def spread_lanes(k):
        right[k, width:, lanes[0]] = -right[k, :width, lanes[1]]
        right[k, width:, lanes[1]] = right[k, :width, lanes[0]]

    first = weights(w5, 0) + spectra_copies(freq, ids[0], cross, left.at[0], l_sem.at[0])
    six, seven = weights(w6, 1), weights(w7, 1)
    second = spectra_copies(freq, ids[1], cross, left.at[1], l_sem.at[1])
    third = [
        pltpu.make_async_copy(
            ref.at[min(k, ref.shape[0] - 1), half],
            left.at[2, pl.ds(half * width, width), pl.ds(k * width, width)],
            l_sem.at[2 + half, k],
        )
        for k, ref in enumerate((block_re, block_im))
        for half in range(2)
    ]
    total_copies = [
        pltpu.make_async_copy(
            total.at[part], tot.at[:, pl.ds(part * sources, sources)], sem.at[part]
        )
        for part in range(2)
    ]
    late_rows = pl.ds(pl.multiple_of(jnp.minimum(late, 1) * width, width), width)
    out_copies = [
        pltpu.make_async_copy(
            field.at[late_rows, pl.ds(part * sources, sources)], field_out.at[part], sem.at[2 + part]
        )
        for part in range(2)
    ]

    @pl.when(step == 0)
    def _():
        sums[...] = jnp.zeros_like(sums)
        for copy in first:
            copy.start()
        for copy in first:
            copy.wait()
        for copy in second:
            copy.start()

        @pl.when(ids[2] == 1)
        def _():
            for copy in seven:
                copy.start()

        @pl.when(ids[2] == 0)
        def _():
            for copy in six:
                copy.start()

        for copy in total_copies:
            copy.start()
        start_rows(freq, ids, 3, row_refs, rows.at[0], row_sem.at[0])
        spread_lanes(0)
        field[...] = dot(left[0], right[0])

    @pl.when(step == 1)
    def _():
        for copy in second + six:
            copy.wait()
        for copy in third:
            copy.start()
        start_rows(freq, ids, 5, row_refs, rows.at[1], row_sem.at[1])
        for copy in total_copies:
            copy.wait()
        spread_lanes(1)
        field[...] = field[...] + tot[...] + dot(left[1], right[1])
        for copy in out_copies:
            copy.start()
        for slot in range(2):
            wait_rows(freq, slot, row_refs, rows.at[0], row_sem.at[0])
        for slot in range(2):

            @pl.when(late != slot)
            def _(slot=slot):
                here = slice(slot * width, (slot + 1) * width)
                for part in range(2):
                    sums[...] += fold(rows[0, part, here], field[here, lanes[part]])

    @pl.when(step == 2)
    def _():
        for copy in third:
            copy.wait()
        for slot in range(2):
            wait_rows(freq, slot, row_refs, rows.at[1], row_sem.at[1])

        @pl.when(ids[2] == 1)
        def _():
            value = dot(left[2], right[0])
            for part in range(2):
                sums[...] += fold(rows[1, part], value[:, lanes[part]])

        for copy in out_copies:
            copy.wait()


def add_late(cross, freq, ids, pieces, blocks, total, row_refs):
    rows, (width, sources) = cross.shape[2], pieces[0].shape[2:]
    dtype = pieces[0].dtype
    return pl.pallas_call(
        functools.partial(late_kernel, freq),
        out_shape=(
            jax.ShapeDtypeStruct((8, sources), jnp.float32),
            jax.ShapeDtypeStruct((2, width, sources), jnp.float32),
        ),
        grid_spec=pltpu.PrefetchScalarGridSpec(
            num_scalar_prefetch=1,
            grid=(3,),
            in_specs=[ANYWHERE] * (7 + len(row_refs)),
            out_specs=(pl.BlockSpec((8, sources), lambda step, ids: (0, 0)), ANYWHERE),
            scratch_shapes=[
                pltpu.VMEM((3, rows, 2 * width), dtype),
                pltpu.VMEM((2, 2 * width, 2 * sources), dtype),
                pltpu.SemaphoreType.DMA((4, 2)),
                pltpu.SemaphoreType.DMA((2, 2)),
                pltpu.VMEM((rows, 2 * sources), jnp.float32),
                pltpu.VMEM((rows, 2 * sources), jnp.float32),
                pltpu.SemaphoreType.DMA((4,)),
                pltpu.VMEM((2, 2, rows, sources), dtype),
                pltpu.SemaphoreType.DMA((2, 2)),
            ],
        ),
        compiler_params=pltpu.CompilerParams(vmem_limit_bytes=VMEM_LIMIT),
        cost_estimate=HINT,
    )(ids, cross, *pieces, *blocks, total, *row_refs)


def dot_kernel(ids, *refs):
    groups, (out, rows, field, sem, total) = (refs[:6], refs[6:12]), refs[12:]
    for freq, (field_ref, _, *sources) in enumerate(groups):

        @pl.when(ids[0] < 4)
        def _(freq=freq, field_ref=field_ref):
            pltpu.make_async_copy(field_ref, field.at[freq], sem.at[0, freq]).start()

        for k, source in enumerate(sources):

            @pl.when(ids[0] == k)
            def _(freq=freq, source=source):
                pltpu.make_async_copy(source.at[0], rows.at[freq], sem.at[1, freq]).start()

    for freq, (field_ref, sums, *sources) in enumerate(groups):
        total[freq : freq + 1] = jnp.sum(sums[...], axis=0, keepdims=True)

        @pl.when(ids[0] < 4)
        def _(freq=freq, field_ref=field_ref, sources=sources):
            pltpu.make_async_copy(field_ref, field.at[freq], sem.at[0, freq]).wait()
            pltpu.make_async_copy(sources[0].at[0], rows.at[freq], sem.at[1, freq]).wait()
            more = sum(fold(rows[freq, part], field[freq, part]) for part in range(2))
            total[freq : freq + 1] += jnp.sum(more, axis=0, keepdims=True)

    for k in range(out.shape[0]):
        out[k] = total[...]


def dot_rows(ids, groups):
    late_shape, dtype = groups[0][0].shape, groups[0][2].dtype
    sources = late_shape[-1]
    whole = lambda shape: pl.BlockSpec(shape, lambda i, ids: (0, 0))
    return pl.pallas_call(
        dot_kernel,
        out_shape=jax.ShapeDtypeStruct((copies_to_all(), len(groups), sources), jnp.float32),
        grid_spec=pltpu.PrefetchScalarGridSpec(
            num_scalar_prefetch=1,
            grid=(1,),
            in_specs=[ANYWHERE, whole((8, sources)), *[ANYWHERE] * 4] * 2,
            out_specs=pl.BlockSpec(
                (copies_to_all(), len(groups), sources), lambda i, ids: (0, 0, 0)
            ),
            scratch_shapes=[
                pltpu.VMEM((2, *late_shape), dtype),
                pltpu.VMEM((2, *late_shape), jnp.float32),
                pltpu.SemaphoreType.DMA((2, 2)),
                pltpu.VMEM((len(groups), sources), jnp.float32),
            ],
        ),
        compiler_params=pltpu.CompilerParams(vmem_limit_bytes=VMEM_LIMIT),
        cost_estimate=HINT,
    )(ids, *groups[0], *groups[1])


def copy_kernel(inputs, jobs, ids, *refs):
    refs, (stage, in_sem, out_sem) = refs[:-3], refs[-3:]
    sources, targets = refs[:inputs], refs[inputs:]
    writes = [
        pltpu.make_async_copy(stage.at[k], target(targets), out_sem.at[k])
        for k, (_, target) in enumerate(jobs)
    ]

    def each(act):
        for k, (options, _) in enumerate(jobs):
            for value, source in options:

                @pl.when(ids[0] == value)
                def _(k=k, source=source):
                    act(k, pltpu.make_async_copy(source(sources, ids), stage.at[k], in_sem.at[k]))

    def pass_on(k, copy):
        copy.wait()
        writes[k].start()

    def finish(k, copy):
        writes[k].wait()

    each(lambda k, copy: copy.start())
    each(pass_on)
    each(finish)


def copies(ids, args, jobs, shapes, unit, dtype, alias=None):
    return pl.pallas_call(
        functools.partial(copy_kernel, len(args), jobs),
        out_shape=[jax.ShapeDtypeStruct(shape, dtype) for shape in shapes],
        grid_spec=pltpu.PrefetchScalarGridSpec(
            num_scalar_prefetch=1,
            grid=(1,),
            in_specs=[ANYWHERE] * len(args),
            out_specs=[ANYWHERE] * len(shapes),
            scratch_shapes=[
                pltpu.VMEM((len(jobs), *unit), dtype),
                pltpu.SemaphoreType.DMA((len(jobs),)),
                pltpu.SemaphoreType.DMA((len(jobs),)),
            ],
        ),
        input_output_aliases={} if alias is None else {1 + alias: 0},
        compiler_params=pltpu.CompilerParams(vmem_limit_bytes=VMEM_LIMIT),
        cost_estimate=HINT,
    )(ids, *args)


def block_source(at, freq, part, half, width):
    def source(refs, ids):
        columns = pl.ds(pl.multiple_of(ids[1] * width, width), width)
        return refs[at].at[freq, part, pl.ds(half * width, width), columns]

    return source


def entry(at, *index):
    return lambda refs, ids=None: refs[at].at[index]


def fill_block(ids, piece, cross):
    _, _, width, sources = piece.shape
    jobs = [
        ([(0, block_source(1, 0, part, half, width))], entry(0, part, half))
        for part in range(2)
        for half in range(2)
    ]
    return copies(ids, [piece, cross], jobs, [piece.shape], (width, sources), piece.dtype, 0)[0]


def take_pair(ids, own, x, n, m):
    freqs, _, width, sources = own.shape
    jobs = [
        (
            [(0, entry(slot, freq, part)), (1, entry(2 + slot, freq, part))],
            entry(0, freq, part, pl.ds(slot * width, width)),
        )
        for freq in range(freqs)
        for part in range(2)
        for slot in range(2)
    ]
    shape = (freqs, 2, 2 * width, sources)
    return copies(ids, [own, x, n, m], jobs, [shape], (width, sources), own.dtype)[0]


def next_kernel(freq, ids, ends, middles, cross, over_x, over_z, stage, in_sem, out_sem):
    width = ends.shape[2]
    columns = pl.ds(pl.multiple_of(ids[1] * width, width), width)
    block = [cross.at[1, freq, pl.ds(half * width, width), columns] for half in range(2)]
    plans = [
        [(ends.at[freq, 0], 0), (ends.at[freq, 1], 1), (block[0], 2), (block[1], 3)],
        [(middles.at[freq, 0], 0), (middles.at[freq, 1], 1)],
    ]
    for mid, plan in enumerate(plans):

        @pl.when(ids[0] == mid)
        def _(mid=mid, plan=plan):
            reads = [
                pltpu.make_async_copy(source, stage.at[k], in_sem.at[k]) for source, k in plan
            ]
            writes = [
                [pltpu.make_async_copy(stage.at[k], over_x.at[0, k], out_sem.at[k])]
                if k < 2
                else [pltpu.make_async_copy(stage.at[k], over_z.at[0, k - 2], out_sem.at[k])]
                for _, k in plan
            ]
            if mid:
                for k in range(2):
                    writes[k].append(
                        pltpu.make_async_copy(stage.at[k], over_z.at[0, k], out_sem.at[2 + k])
                    )
            for copy in reads:
                copy.start()
            for read, group in zip(reads, writes):
                read.wait()
                for copy in group:
                    copy.start()
            for group in writes:
                for copy in group:
                    copy.wait()


def take_next(freq, ids, ends, middles, cross):
    _, _, width, sources = ends.shape
    shape = jax.ShapeDtypeStruct((1, 2, width, sources), ends.dtype)
    return pl.pallas_call(
        functools.partial(next_kernel, freq),
        out_shape=[shape, shape],
        grid_spec=pltpu.PrefetchScalarGridSpec(
            num_scalar_prefetch=1,
            grid=(1,),
            in_specs=[ANYWHERE] * 3,
            out_specs=[ANYWHERE] * 2,
            scratch_shapes=[
                pltpu.VMEM((4, width, sources), ends.dtype),
                pltpu.SemaphoreType.DMA((4,)),
                pltpu.SemaphoreType.DMA((4,)),
            ],
        ),
        compiler_params=pltpu.CompilerParams(vmem_limit_bytes=VMEM_LIMIT),
        cost_estimate=HINT,
    )(ids, ends, middles, cross)


def sums_by_swaps(cross, replicas, norms):
    rows, half = cross.shape[2], cross.shape[3]
    width = replicas.shape[3]
    me = lax.axis_index("row").astype(jnp.int32)
    col = lax.axis_index("col").astype(jnp.int32)
    holds = me * rows // half == col
    mid = ((me // 2) % 4 == 1) | ((me // 2) % 4 == 2)
    flag = lambda value: jnp.where(value, 1, 0).astype(jnp.int32).reshape(1)
    ids = lambda *wanted: me ^ jnp.array(wanted, jnp.int32)
    barrier = lambda *values: lax.optimization_barrier(values)

    slots = jnp.arange(2, dtype=jnp.int32)
    per_half = half // width
    own_masks = (2 * me % per_half + slots) ^ me
    next_masks = ((2 * (me ^ 2) % per_half + slots) ^ me) & 3
    table = lambda masks: sum(
        jnp.where(masks == mask, place, 0)
        for mask, place in enumerate((0, 1, 0, 2, 3, 5, 1, 4))
    ) + jnp.where(holds, 0, 6)
    late_slot = own_masks[0] & 1 ^ 1
    late_source = jnp.where(own_masks[0] & 2 != 0, 0, 1) + jnp.where(holds, 0, 2)
    ids_dot = jnp.where(mid, late_source, 4).astype(jnp.int32).reshape(1)
    late_ids = jnp.concatenate(
        [
            ids(5),
            jnp.where(mid, ids(7), ids(6)),
            flag(mid),
            table(own_masks),
            table(next_masks),
            jnp.where(mid, late_slot, 2).reshape(1),
        ]
    ).astype(jnp.int32)
    pair = flag(((me >> 1) ^ me) & 1 != 0)
    ids_a = jnp.concatenate([ids(1, 2, 6), flag(mid)])
    ids_z = jnp.concatenate([flag(mid), ids(7)])
    numbers = [ids_a, ids(3, 4), ids_z, late_ids, pair, ids_dot]

    own = replicas[:, :, 0]
    x = swap(own, "row", 1)
    n = swap(own, "row", 2)
    m = swap_middle(own)
    a0 = add_field(cross, 0, ids(0), [own])
    a1 = add_field(cross, 1, ids(0), [own])
    m = fill_block(ids_z, m, cross)
    norms += swap(norms, "col", 1)
    x, n, m, a0, a1, norms, *numbers = barrier(x, n, m, a0, a1, norms, *numbers)
    ids_a, ids_b, ids_z, late_ids, pair, ids_dot = numbers

    z = swap(m, "row", 2)
    m2 = swap_middle(n)
    xn = swap(n, "row", 1)
    a0 = add_field(cross, 0, ids_a, [x, n, m], a0, gated=True)
    a1 = add_field(cross, 1, ids_a, [x, n, m], a1, gated=True)
    mine = take_pair(pair, own, x, n, m)
    x_a, x_b = x[0:1], x[1:2]
    norms += swap(norms, "row", 1)
    z, m2, xn, a0, a1, mine, x_a, x_b, norms = barrier(z, m2, xn, a0, a1, mine, x_a, x_b, norms)

    w4_a, send_a = take_next(0, ids_z, z, m2, cross)
    x5_a = swap(w4_a, "row", 1)
    z_a = swap(send_a, "row", 2)
    w7_a = swap_middle(after(x_a, w4_a))
    other = swap(mine, "col", 1)
    b0 = add_field(cross, 0, ids_b, [xn, w4_a], a0)
    w4_b, send_b = take_next(1, after(ids_z, b0), z, m2, cross)
    b1 = add_field(cross, 1, ids_b, [xn, w4_b], a1)
    norms += swap(norms, "row", 2)
    x5_a, z_a, w7_a, other, b0, w4_b, send_b, x_b, xn, m2, norms = barrier(
        x5_a, z_a, w7_a, other, b0, w4_b, send_b, x_b, xn, m2, norms
    )

    x5_b = swap(w4_b, "row", 1)
    z_b = swap(send_b, "row", 2)
    w7_b = swap_middle(x_b)
    other_xn = swap(xn, "col", 1)
    other_m2 = swap(m2, "col", 1)
    early = [mine, xn, m2, xn, xn, other, other_xn, other_m2, other_xn, other_xn]
    sums_a, field_a = add_late(cross, 0, late_ids, [x5_a, z_a, w7_a], [z, z], b0, early)
    norms += swap(after(norms, other_xn, other_m2), "row", 4)
    x5_b, z_b, w7_b, sums_a, field_a, b1, other_xn, other_m2, x5_a, w7_a, norms = barrier(
        x5_b, z_b, w7_b, sums_a, field_a, b1, other_xn, other_m2, x5_a, w7_a, norms
    )

    late = [w7_a, x5_a, w7_b, x5_b]
    others = [swap(piece, "col", 1) for piece in late]
    early = [mine, xn, m2, xn, xn, other, other_xn, other_m2, other_xn, other_xn]
    sums_b, field_b = add_late(cross, 1, late_ids, [x5_b, z_b, w7_b], [z_a, z_b], b1, early)
    groups = [
        (field_a, sums_a, *late[:2], *others[:2]),
        (field_b, sums_b, *late[2:], *others[2:]),
    ]
    return dot_rows(ids_dot, groups), norms


def sums_by_gather(cross, replicas, norms):
    rows, half = cross.shape[2], cross.shape[3]
    row_index, col_index = lax.axis_index("row"), lax.axis_index("col")
    first_row = row_index * rows
    holder = first_row // half
    whole = lax.all_gather(replicas, "row", axis=3, tiled=True)[:, :, 0]
    parts = jnp.einsum("fark,fbks->fabrs", cross, whole, preferred_element_type=jnp.float32)
    field = jnp.stack([parts[:, 0, 0] - parts[:, 1, 1], parts[:, 0, 1] + parts[:, 1, 0]], axis=1)
    own_rows = lax.dynamic_slice_in_dim(whole, first_row - holder * half, rows, 2)
    block_rows = jnp.where(holder == col_index, own_rows, swap(own_rows, "col", 1))
    numer = jnp.sum(block_rows.astype(jnp.float32) * field, axis=(1, 2))
    return jnp.broadcast_to(numer[None], (copies_to_all(), *numer.shape)), lax.psum(norms, ("row", "col"))


def body(cross_spectra, replicas, tile_order):
    fnum = cross_spectra.shape[0]
    sources = replicas.shape[4]
    own = replicas[:, :, 0].astype(jnp.float32)
    norms = jnp.sum(own * own, axis=(1, 2))
    doubling = (
        lax.axis_size("row") == 8
        and fnum == 2
        and replicas.shape[3] % 128 == 0
        and cross_spectra.shape[2] == 2 * replicas.shape[3]
    )
    copies, norms = (sums_by_swaps if doubling else sums_by_gather)(cross_spectra, replicas, norms)
    beam = sum_all(copies) / (norms + 1e-06)
    width = sources // lax.axis_size("col")
    beam_half = lax.dynamic_slice_in_dim(beam, lax.axis_index("col") * width, width, 1)
    peak = jnp.max(jnp.abs(beam), axis=1) + 1e-06
    count = tile_order.shape[0]
    picker = (tile_order[:, None] == jnp.arange(count, dtype=jnp.int32)[None, :]).astype(jnp.float32)
    tiles = beam.reshape(fnum, count, sources // count)
    refined = (
        jnp.einsum("tu,fup->ftp", picker, tiles, precision=lax.Precision.HIGHEST)
        / peak[:, None, None]
    )
    return (beam_half, refined)


def solution(mesh):
    in_specs = (P("groups", None, "row", "col"), P("groups", None, "col", "row", None), P("groups"))
    out_specs = (P("groups", "col"), P("groups", None, None))
    return jax.shard_map(body, mesh=mesh, in_specs=in_specs, out_specs=out_specs, check_vma=False)
```

```python
import functools
import math

import jax
import jax.numpy as jnp
from jax import lax
from jax.experimental import pallas as pl
from jax.experimental.pallas import tpu as pltpu
from jax.sharding import PartitionSpec as P

VMEM_LIMIT = 63 * 1024 * 1024
HINT = pl.CostEstimate(flops=1, bytes_accessed=1, transcendentals=0)
ANYWHERE = pl.BlockSpec(memory_space=pl.ANY)


def swap(value, axis, mask):
    size = math.prod(lax.axis_size(name) for name in (axis if isinstance(axis, tuple) else (axis,)))
    return lax.ppermute(value, axis, [(source, source ^ mask) for source in range(size)])


def swap_middle(value):
    axes = ("row", "col")
    size = lax.axis_size("row") * lax.axis_size("col")
    target = lambda k: k ^ 12 if (k // 4) % 4 in (1, 2) else k ^ 1
    return lax.ppermute(value, axes, [(k, target(k)) for k in range(size)])


def after(value, *others):
    return lax.optimization_barrier((value, *others))[0]


def copies_to_all():
    size = lax.axis_size("row") * lax.axis_size("col")
    return size if size <= 16 else 1


def sum_all(copies):
    axes = ("row", "col")
    if copies.shape[0] == 1:
        return lax.psum(copies[0], axes)
    return jnp.sum(lax.all_to_all(copies, axes, 0, 0, tiled=True), axis=0)


def dot(a, b):
    return jnp.dot(a, b, preferred_element_type=jnp.float32)


def at_freq(ref, freq):
    return ref.at[freq if ref.shape[0] > 1 else 0]


def weight_copies(freq, ref, right, sem):
    low = pl.ds(0, ref.shape[2])
    source = at_freq(ref, freq)
    return [
        pltpu.make_async_copy(source.at[0], right.at[0, low], sem.at[0]),
        pltpu.make_async_copy(source.at[1], right.at[1, low], sem.at[1]),
    ]


def spread(right):
    width = right.shape[1] // 2
    right[0, width:] = -right[1, :width]
    right[1, width:] = right[0, :width]


def spectra_copies(freq, column, cross, left, sem):
    width = left.shape[1] // 2
    columns = pl.ds(pl.multiple_of(column * width, width), width)
    return [
        pltpu.make_async_copy(
            cross.at[freq, part, :, columns], left.at[:, pl.ds(part * width, width)], sem.at[part]
        )
        for part in range(2)
    ]


def field_kernel(freq, count, has_total, gated, ids, cross, *refs):
    w_refs, refs = refs[:count], refs[count:]
    total, refs = (refs[0], refs[1:]) if has_total else (None, refs)
    out, left, right, l_sem, w_sem, field, tot, tot_sem = refs
    piece, part = pl.program_id(0), pl.program_id(1)
    copies = [
        weight_copies(freq, ref, right.at[k], w_sem.at[k])
        + spectra_copies(freq, ids[k], cross, left.at[k], l_sem.at[k])
        for k, ref in enumerate(w_refs)
    ]
    for k, group in enumerate(copies):

        @pl.when((piece == k) & (part == 0))
        def _(k=k, group=group):
            if k == 0:
                for copy in group:
                    copy.start()
            for copy in group:
                copy.wait()
            if k + 1 < count:
                for copy in copies[k + 1]:
                    copy.start()
            if k == 0 and has_total:
                pltpu.make_async_copy(total, tot, tot_sem.at[0]).start()
            spread(right.at[k])

    last = piece == count - 1
    if count > 1:

        @pl.when(piece == 0)
        def _():
            field[part] = dot(left[piece], right[piece, part])

        @pl.when((piece > 0) & (piece < count - 1))
        def _():
            field[part] += dot(left[piece], right[piece, part])

    @pl.when(last)
    def _():
        value = dot(left[piece], right[piece, part])
        if gated:
            value = jnp.where(ids[count] == 1, value, 0.0)
        if count > 1:
            value += field[part]
        if has_total:

            @pl.when(part == 0)
            def _():
                pltpu.make_async_copy(total, tot, tot_sem.at[0]).wait()

            value += tot[part]
        out[0] = value


def add_field(cross, freq, ids, pieces, total=None, gated=False):
    rows, (width, sources) = cross.shape[2], pieces[0].shape[2:]
    count, dtype = len(pieces), pieces[0].dtype
    has_total = total is not None
    return pl.pallas_call(
        functools.partial(field_kernel, freq, count, has_total, gated),
        out_shape=jax.ShapeDtypeStruct((2, rows, sources), jnp.float32),
        grid_spec=pltpu.PrefetchScalarGridSpec(
            num_scalar_prefetch=1,
            grid=(count, 2),
            in_specs=[ANYWHERE] * (1 + count + has_total),
            out_specs=pl.BlockSpec(
                (1, rows, sources), lambda p, part, ids: (jnp.where(p == count - 1, part, 0), 0, 0)
            ),
            scratch_shapes=[
                pltpu.VMEM((count, rows, 2 * width), dtype),
                pltpu.VMEM((count, 2, 2 * width, sources), dtype),
                pltpu.SemaphoreType.DMA((count, 2)),
                pltpu.SemaphoreType.DMA((count, 2)),
                pltpu.VMEM((2, rows, sources), jnp.float32),
                pltpu.VMEM((2, rows, sources), jnp.float32),
                pltpu.SemaphoreType.DMA((1,)),
            ],
        ),
        compiler_params=pltpu.CompilerParams(vmem_limit_bytes=VMEM_LIMIT),
        cost_estimate=HINT,
    )(ids, cross, *pieces, *([total] if has_total else []))


def start_rows(freq, ids, base, refs, rows, sem):
    width = rows.shape[1] // 2
    views = []
    for picked, *pieces in (refs[:5], refs[5:]):
        views += [picked.at[freq, :, pl.ds(slot * width, width)] for slot in range(2)]
        views += [at_freq(ref, freq) for ref in pieces]
    for slot in range(2):
        here = pl.ds(slot * width, width)
        for k, source in enumerate(views):

            @pl.when(ids[base + slot] == k)
            def _(source=source, slot=slot, here=here):
                pltpu.make_async_copy(source, rows.at[:, here], sem.at[slot]).start()


def wait_rows(freq, slot, refs, rows, sem):
    width = rows.shape[1] // 2
    source = refs[0].at[freq, :, pl.ds(0, width)]
    here = rows.at[:, pl.ds(slot * width, width)]
    pltpu.make_async_copy(source, here, sem.at[slot]).wait()


def fold(rows, field):
    product = rows.astype(jnp.float32) * field
    return jnp.sum(product.reshape(-1, 8, product.shape[-1]), axis=0)


def late_kernel(freq, ids, cross, w5, w6, w7, block_re, block_im, total, *refs):
    row_refs, refs = refs[:10], refs[10:]
    sums, field_out, left, right, l_sem, w_sem, field, tot, sem, rows, row_sem = refs
    late = ids[7]
    step = pl.program_id(0)
    width, sources = w5.shape[2:]
    lanes = [slice(part * sources, (part + 1) * sources) for part in range(2)]

    def weights(ref, k):
        source = at_freq(ref, freq)
        return [
            pltpu.make_async_copy(
                source.at[part],
                right.at[k, pl.ds(0, width), pl.ds(part * sources, sources)],
                w_sem.at[k, part],
            )
            for part in range(2)
        ]

    def spread_lanes(k):
        right[k, width:, lanes[0]] = -right[k, :width, lanes[1]]
        right[k, width:, lanes[1]] = right[k, :width, lanes[0]]

    first = weights(w5, 0) + spectra_copies(freq, ids[0], cross, left.at[0], l_sem.at[0])
    six, seven = weights(w6, 1), weights(w7, 1)
    second = spectra_copies(freq, ids[1], cross, left.at[1], l_sem.at[1])
    third = [
        pltpu.make_async_copy(
            ref.at[min(k, ref.shape[0] - 1), half],
            left.at[2, pl.ds(half * width, width), pl.ds(k * width, width)],
            l_sem.at[2 + half, k],
        )
        for k, ref in enumerate((block_re, block_im))
        for half in range(2)
    ]
    total_copies = [
        pltpu.make_async_copy(
            total.at[part], tot.at[:, pl.ds(part * sources, sources)], sem.at[part]
        )
        for part in range(2)
    ]
    late_rows = pl.ds(pl.multiple_of(jnp.minimum(late, 1) * width, width), width)
    out_copies = [
        pltpu.make_async_copy(
            field.at[late_rows, pl.ds(part * sources, sources)], field_out.at[part], sem.at[2 + part]
        )
        for part in range(2)
    ]

    @pl.when(step == 0)
    def _():
        sums[...] = jnp.zeros_like(sums)
        for copy in first:
            copy.start()
        for copy in first:
            copy.wait()
        for copy in second:
            copy.start()

        @pl.when(ids[2] == 1)
        def _():
            for copy in seven:
                copy.start()

        @pl.when(ids[2] == 0)
        def _():
            for copy in six:
                copy.start()

        for copy in total_copies:
            copy.start()
        start_rows(freq, ids, 3, row_refs, rows.at[0], row_sem.at[0])
        spread_lanes(0)
        field[...] = dot(left[0], right[0])

    @pl.when(step == 1)
    def _():
        for copy in second + six:
            copy.wait()
        for copy in third:
            copy.start()
        start_rows(freq, ids, 5, row_refs, rows.at[1], row_sem.at[1])
        for copy in total_copies:
            copy.wait()
        spread_lanes(1)
        field[...] = field[...] + tot[...] + dot(left[1], right[1])
        for copy in out_copies:
            copy.start()
        for slot in range(2):
            wait_rows(freq, slot, row_refs, rows.at[0], row_sem.at[0])
        for slot in range(2):

            @pl.when(late != slot)
            def _(slot=slot):
                here = slice(slot * width, (slot + 1) * width)
                for part in range(2):
                    sums[...] += fold(rows[0, part, here], field[here, lanes[part]])

    @pl.when(step == 2)
    def _():
        for copy in third:
            copy.wait()
        for slot in range(2):
            wait_rows(freq, slot, row_refs, rows.at[1], row_sem.at[1])

        @pl.when(ids[2] == 1)
        def _():
            value = dot(left[2], right[0])
            for part in range(2):
                sums[...] += fold(rows[1, part], value[:, lanes[part]])

        for copy in out_copies:
            copy.wait()


def add_late(cross, freq, ids, pieces, blocks, total, row_refs):
    rows, (width, sources) = cross.shape[2], pieces[0].shape[2:]
    dtype = pieces[0].dtype
    return pl.pallas_call(
        functools.partial(late_kernel, freq),
        out_shape=(
            jax.ShapeDtypeStruct((8, sources), jnp.float32),
            jax.ShapeDtypeStruct((2, width, sources), jnp.float32),
        ),
        grid_spec=pltpu.PrefetchScalarGridSpec(
            num_scalar_prefetch=1,
            grid=(3,),
            in_specs=[ANYWHERE] * (7 + len(row_refs)),
            out_specs=(pl.BlockSpec((8, sources), lambda step, ids: (0, 0)), ANYWHERE),
            scratch_shapes=[
                pltpu.VMEM((3, rows, 2 * width), dtype),
                pltpu.VMEM((2, 2 * width, 2 * sources), dtype),
                pltpu.SemaphoreType.DMA((4, 2)),
                pltpu.SemaphoreType.DMA((2, 2)),
                pltpu.VMEM((rows, 2 * sources), jnp.float32),
                pltpu.VMEM((rows, 2 * sources), jnp.float32),
                pltpu.SemaphoreType.DMA((4,)),
                pltpu.VMEM((2, 2, rows, sources), dtype),
                pltpu.SemaphoreType.DMA((2, 2)),
            ],
        ),
        compiler_params=pltpu.CompilerParams(vmem_limit_bytes=VMEM_LIMIT),
        cost_estimate=HINT,
    )(ids, cross, *pieces, *blocks, total, *row_refs)


def dot_kernel(ids, norms, *refs):
    groups, (out, rows, field, sem, total) = (refs[:6], refs[6:12]), refs[12:]
    for freq, (field_ref, _, *sources) in enumerate(groups):

        @pl.when(ids[0] < 4)
        def _(freq=freq, field_ref=field_ref):
            pltpu.make_async_copy(field_ref, field.at[freq], sem.at[0, freq]).start()

        for k, source in enumerate(sources):

            @pl.when(ids[0] == k)
            def _(freq=freq, source=source):
                pltpu.make_async_copy(source.at[0], rows.at[freq], sem.at[1, freq]).start()

    for freq, (field_ref, sums, *sources) in enumerate(groups):
        total[freq : freq + 1] = jnp.sum(sums[...], axis=0, keepdims=True)

        @pl.when(ids[0] < 4)
        def _(freq=freq, field_ref=field_ref, sources=sources):
            pltpu.make_async_copy(field_ref, field.at[freq], sem.at[0, freq]).wait()
            pltpu.make_async_copy(sources[0].at[0], rows.at[freq], sem.at[1, freq]).wait()
            more = sum(fold(rows[freq, part], field[freq, part]) for part in range(2))
            total[freq : freq + 1] += jnp.sum(more, axis=0, keepdims=True)

    total[2:4] = norms[...]
    for k in range(out.shape[0]):
        out[k] = total[...]


def dot_rows(ids, norms, groups):
    late_shape, dtype = groups[0][0].shape, groups[0][2].dtype
    sources = late_shape[-1]
    whole = lambda shape: pl.BlockSpec(shape, lambda i, ids: (0, 0))
    return pl.pallas_call(
        dot_kernel,
        out_shape=jax.ShapeDtypeStruct((copies_to_all(), 4, sources), jnp.float32),
        grid_spec=pltpu.PrefetchScalarGridSpec(
            num_scalar_prefetch=1,
            grid=(1,),
            in_specs=[whole((2, sources))] + [ANYWHERE, whole((8, sources)), *[ANYWHERE] * 4] * 2,
            out_specs=pl.BlockSpec((copies_to_all(), 4, sources), lambda i, ids: (0, 0, 0)),
            scratch_shapes=[
                pltpu.VMEM((2, *late_shape), dtype),
                pltpu.VMEM((2, *late_shape), jnp.float32),
                pltpu.SemaphoreType.DMA((2, 2)),
                pltpu.VMEM((4, sources), jnp.float32),
            ],
        ),
        compiler_params=pltpu.CompilerParams(vmem_limit_bytes=VMEM_LIMIT),
        cost_estimate=HINT,
    )(ids, norms, *groups[0], *groups[1])


def copy_kernel(inputs, jobs, ids, *refs):
    refs, (stage, in_sem, out_sem) = refs[:-3], refs[-3:]
    sources, targets = refs[:inputs], refs[inputs:]
    writes = [
        pltpu.make_async_copy(stage.at[k], target(targets), out_sem.at[k])
        for k, (_, target) in enumerate(jobs)
    ]

    def each(act):
        for k, (options, _) in enumerate(jobs):
            for value, source in options:

                @pl.when(ids[0] == value)
                def _(k=k, source=source):
                    act(k, pltpu.make_async_copy(source(sources, ids), stage.at[k], in_sem.at[k]))

    def pass_on(k, copy):
        copy.wait()
        writes[k].start()

    def finish(k, copy):
        writes[k].wait()

    each(lambda k, copy: copy.start())
    each(pass_on)
    each(finish)


def copies(ids, args, jobs, shapes, unit, dtype, alias=None):
    return pl.pallas_call(
        functools.partial(copy_kernel, len(args), jobs),
        out_shape=[jax.ShapeDtypeStruct(shape, dtype) for shape in shapes],
        grid_spec=pltpu.PrefetchScalarGridSpec(
            num_scalar_prefetch=1,
            grid=(1,),
            in_specs=[ANYWHERE] * len(args),
            out_specs=[ANYWHERE] * len(shapes),
            scratch_shapes=[
                pltpu.VMEM((len(jobs), *unit), dtype),
                pltpu.SemaphoreType.DMA((len(jobs),)),
                pltpu.SemaphoreType.DMA((len(jobs),)),
            ],
        ),
        input_output_aliases={} if alias is None else {1 + alias: 0},
        compiler_params=pltpu.CompilerParams(vmem_limit_bytes=VMEM_LIMIT),
        cost_estimate=HINT,
    )(ids, *args)


def block_source(at, freq, part, half, width):
    def source(refs, ids):
        columns = pl.ds(pl.multiple_of(ids[1] * width, width), width)
        return refs[at].at[freq, part, pl.ds(half * width, width), columns]

    return source


def entry(at, *index):
    return lambda refs, ids=None: refs[at].at[index]


def fill_block(ids, piece, cross):
    _, _, width, sources = piece.shape
    jobs = [
        ([(0, block_source(1, 0, part, half, width))], entry(0, part, half))
        for part in range(2)
        for half in range(2)
    ]
    return copies(ids, [piece, cross], jobs, [piece.shape], (width, sources), piece.dtype, 0)[0]


def take_pair(ids, own, x, n, m):
    freqs, _, width, sources = own.shape
    jobs = [
        (
            [(0, entry(slot, freq, part)), (1, entry(2 + slot, freq, part))],
            entry(0, freq, part, pl.ds(slot * width, width)),
        )
        for freq in range(freqs)
        for part in range(2)
        for slot in range(2)
    ]
    shape = (freqs, 2, 2 * width, sources)
    return copies(ids, [own, x, n, m], jobs, [shape], (width, sources), own.dtype)[0]


def next_kernel(freq, ids, ends, middles, cross, over_x, over_z, stage, in_sem, out_sem):
    width = ends.shape[2]
    columns = pl.ds(pl.multiple_of(ids[1] * width, width), width)
    block = [cross.at[1, freq, pl.ds(half * width, width), columns] for half in range(2)]
    plans = [
        [(ends.at[freq, 0], 0), (ends.at[freq, 1], 1), (block[0], 2), (block[1], 3)],
        [(middles.at[freq, 0], 0), (middles.at[freq, 1], 1)],
    ]
    for mid, plan in enumerate(plans):

        @pl.when(ids[0] == mid)
        def _(mid=mid, plan=plan):
            reads = [
                pltpu.make_async_copy(source, stage.at[k], in_sem.at[k]) for source, k in plan
            ]
            writes = [
                [pltpu.make_async_copy(stage.at[k], over_x.at[0, k], out_sem.at[k])]
                if k < 2
                else [pltpu.make_async_copy(stage.at[k], over_z.at[0, k - 2], out_sem.at[k])]
                for _, k in plan
            ]
            if mid:
                for k in range(2):
                    writes[k].append(
                        pltpu.make_async_copy(stage.at[k], over_z.at[0, k], out_sem.at[2 + k])
                    )
            for copy in reads:
                copy.start()
            for read, group in zip(reads, writes):
                read.wait()
                for copy in group:
                    copy.start()
            for group in writes:
                for copy in group:
                    copy.wait()


def take_next(freq, ids, ends, middles, cross):
    _, _, width, sources = ends.shape
    shape = jax.ShapeDtypeStruct((1, 2, width, sources), ends.dtype)
    return pl.pallas_call(
        functools.partial(next_kernel, freq),
        out_shape=[shape, shape],
        grid_spec=pltpu.PrefetchScalarGridSpec(
            num_scalar_prefetch=1,
            grid=(1,),
            in_specs=[ANYWHERE] * 3,
            out_specs=[ANYWHERE] * 2,
            scratch_shapes=[
                pltpu.VMEM((4, width, sources), ends.dtype),
                pltpu.SemaphoreType.DMA((4,)),
                pltpu.SemaphoreType.DMA((4,)),
            ],
        ),
        compiler_params=pltpu.CompilerParams(vmem_limit_bytes=VMEM_LIMIT),
        cost_estimate=HINT,
    )(ids, ends, middles, cross)


def sums_by_swaps(cross, replicas, norms):
    rows, half = cross.shape[2], cross.shape[3]
    width = replicas.shape[3]
    me = lax.axis_index("row").astype(jnp.int32)
    col = lax.axis_index("col").astype(jnp.int32)
    holds = me * rows // half == col
    mid = ((me // 2) % 4 == 1) | ((me // 2) % 4 == 2)
    flag = lambda value: jnp.where(value, 1, 0).astype(jnp.int32).reshape(1)
    ids = lambda *wanted: me ^ jnp.array(wanted, jnp.int32)
    barrier = lambda *values: lax.optimization_barrier(values)

    slots = jnp.arange(2, dtype=jnp.int32)
    per_half = half // width
    own_masks = (2 * me % per_half + slots) ^ me
    next_masks = ((2 * (me ^ 2) % per_half + slots) ^ me) & 3
    table = lambda masks: sum(
        jnp.where(masks == mask, place, 0)
        for mask, place in enumerate((0, 1, 0, 2, 3, 5, 1, 4))
    ) + jnp.where(holds, 0, 6)
    late_slot = own_masks[0] & 1 ^ 1
    late_source = jnp.where(own_masks[0] & 2 != 0, 0, 1) + jnp.where(holds, 0, 2)
    ids_dot = jnp.where(mid, late_source, 4).astype(jnp.int32).reshape(1)
    late_ids = jnp.concatenate(
        [
            ids(5),
            jnp.where(mid, ids(7), ids(6)),
            flag(mid),
            table(own_masks),
            table(next_masks),
            jnp.where(mid, late_slot, 2).reshape(1),
        ]
    ).astype(jnp.int32)
    pair = flag(((me >> 1) ^ me) & 1 != 0)
    ids_a = jnp.concatenate([ids(1, 2, 6), flag(mid)])
    ids_z = jnp.concatenate([flag(mid), ids(7)])
    numbers = [ids_a, ids(3, 4), ids_z, late_ids, pair, ids_dot]

    own = replicas[:, :, 0]
    x = swap(own, "row", 1)
    n = swap(own, "row", 2)
    m = swap_middle(own)
    a0 = add_field(cross, 0, ids(0), [own])
    a1 = add_field(cross, 1, ids(0), [own])
    m = fill_block(ids_z, m, cross)
    x, n, m, a0, a1, norms, *numbers = barrier(x, n, m, a0, a1, norms, *numbers)
    ids_a, ids_b, ids_z, late_ids, pair, ids_dot = numbers

    z = swap(m, "row", 2)
    m2 = swap_middle(n)
    xn = swap(n, "row", 1)
    a0 = add_field(cross, 0, ids_a, [x, n, m], a0, gated=True)
    a1 = add_field(cross, 1, ids_a, [x, n, m], a1, gated=True)
    mine = take_pair(pair, own, x, n, m)
    x_a, x_b = x[0:1], x[1:2]
    z, m2, xn, a0, a1, mine, x_a, x_b = barrier(z, m2, xn, a0, a1, mine, x_a, x_b)

    w4_a, send_a = take_next(0, ids_z, z, m2, cross)
    x5_a = swap(w4_a, "row", 1)
    z_a = swap(send_a, "row", 2)
    w7_a = swap_middle(after(x_a, w4_a))
    other = swap(mine, "col", 1)
    b0 = add_field(cross, 0, ids_b, [xn, w4_a], a0)
    w4_b, send_b = take_next(1, after(ids_z, b0), z, m2, cross)
    b1 = add_field(cross, 1, ids_b, [xn, w4_b], a1)
    x5_a, z_a, w7_a, other, b0, w4_b, send_b, x_b, xn, m2 = barrier(
        x5_a, z_a, w7_a, other, b0, w4_b, send_b, x_b, xn, m2
    )

    x5_b = swap(w4_b, "row", 1)
    z_b = swap(send_b, "row", 2)
    w7_b = swap_middle(x_b)
    other_xn = swap(xn, "col", 1)
    other_m2 = swap(m2, "col", 1)
    early = [mine, xn, m2, xn, xn, other, other_xn, other_m2, other_xn, other_xn]
    sums_a, field_a = add_late(cross, 0, late_ids, [x5_a, z_a, w7_a], [z, z], b0, early)
    x5_b, z_b, w7_b, sums_a, field_a, b1, other_xn, other_m2, x5_a, w7_a = barrier(
        x5_b, z_b, w7_b, sums_a, field_a, b1, other_xn, other_m2, x5_a, w7_a
    )

    late = [w7_a, x5_a, w7_b, x5_b]
    others = [swap(piece, "col", 1) for piece in late]
    early = [mine, xn, m2, xn, xn, other, other_xn, other_m2, other_xn, other_xn]
    sums_b, field_b = add_late(cross, 1, late_ids, [x5_b, z_b, w7_b], [z_a, z_b], b1, early)
    groups = [
        (field_a, sums_a, *late[:2], *others[:2]),
        (field_b, sums_b, *late[2:], *others[2:]),
    ]
    return dot_rows(ids_dot, norms, groups)


def sums_by_gather(cross, replicas, norms):
    rows, half = cross.shape[2], cross.shape[3]
    row_index, col_index = lax.axis_index("row"), lax.axis_index("col")
    first_row = row_index * rows
    holder = first_row // half
    whole = lax.all_gather(replicas, "row", axis=3, tiled=True)[:, :, 0]
    parts = jnp.einsum("fark,fbks->fabrs", cross, whole, preferred_element_type=jnp.float32)
    field = jnp.stack([parts[:, 0, 0] - parts[:, 1, 1], parts[:, 0, 1] + parts[:, 1, 0]], axis=1)
    own_rows = lax.dynamic_slice_in_dim(whole, first_row - holder * half, rows, 2)
    block_rows = jnp.where(holder == col_index, own_rows, swap(own_rows, "col", 1))
    numer = jnp.sum(block_rows.astype(jnp.float32) * field, axis=(1, 2))
    sums = jnp.concatenate([numer, norms])
    return jnp.broadcast_to(sums[None], (copies_to_all(), *sums.shape))


def body(cross_spectra, replicas, tile_order):
    fnum = cross_spectra.shape[0]
    sources = replicas.shape[4]
    own = replicas[:, :, 0].astype(jnp.float32)
    norms = jnp.sum(own * own, axis=(1, 2))
    doubling = (
        lax.axis_size("row") == 8
        and fnum == 2
        and replicas.shape[3] % 128 == 0
        and cross_spectra.shape[2] == 2 * replicas.shape[3]
    )
    sums = (sums_by_swaps if doubling else sums_by_gather)(cross_spectra, replicas, norms)
    sums = sum_all(sums)
    numer, norms = sums[:fnum], sums[fnum:]
    beam = numer / (norms + 1e-06)
    width = sources // lax.axis_size("col")
    beam_half = lax.dynamic_slice_in_dim(beam, lax.axis_index("col") * width, width, 1)
    peak = jnp.max(jnp.abs(beam), axis=1) + 1e-06
    count = tile_order.shape[0]
    picker = (tile_order[:, None] == jnp.arange(count, dtype=jnp.int32)[None, :]).astype(jnp.float32)
    tiles = beam.reshape(fnum, count, sources // count)
    refined = (
        jnp.einsum("tu,fup->ftp", picker, tiles, precision=lax.Precision.HIGHEST)
        / peak[:, None, None]
    )
    return (beam_half, refined)


def solution(mesh):
    in_specs = (P("groups", None, "row", "col"), P("groups", None, "col", "row", None), P("groups"))
    out_specs = (P("groups", "col"), P("groups", None, None))
    return jax.shard_map(body, mesh=mesh, in_specs=in_specs, out_specs=out_specs, check_vma=False)
```

```python
import functools
import math

import jax
import jax.numpy as jnp
from jax import lax
from jax.experimental import pallas as pl
from jax.experimental.pallas import tpu as pltpu
from jax.sharding import PartitionSpec as P

VMEM_LIMIT = 63 * 1024 * 1024
HINT = pl.CostEstimate(flops=1, bytes_accessed=1, transcendentals=0)
ANYWHERE = pl.BlockSpec(memory_space=pl.ANY)


def swap(value, axis, mask):
    size = math.prod(lax.axis_size(name) for name in (axis if isinstance(axis, tuple) else (axis,)))
    return lax.ppermute(value, axis, [(source, source ^ mask) for source in range(size)])


def swap_middle(value):
    axes = ("row", "col")
    size = lax.axis_size("row") * lax.axis_size("col")
    target = lambda k: k ^ 12 if (k // 4) % 4 in (1, 2) else k ^ 1
    return lax.ppermute(value, axes, [(k, target(k)) for k in range(size)])


def after(value, *others):
    return lax.optimization_barrier((value, *others))[0]


def copies_to_all():
    size = lax.axis_size("row") * lax.axis_size("col")
    return size if size <= 16 else 1


def sum_all(copies):
    axes = ("row", "col")
    if copies.shape[0] == 1:
        return lax.psum(copies[0], axes)
    return jnp.sum(lax.all_to_all(copies, axes, 0, 0, tiled=True), axis=0)


def dot(a, b):
    return jnp.dot(a, b, preferred_element_type=jnp.float32)


def at_freq(ref, freq):
    return ref.at[freq if ref.shape[0] > 1 else 0]


def weight_copies(freq, ref, right, sem):
    low = pl.ds(0, ref.shape[2])
    source = at_freq(ref, freq)
    return [
        pltpu.make_async_copy(source.at[0], right.at[0, low], sem.at[0]),
        pltpu.make_async_copy(source.at[1], right.at[1, low], sem.at[1]),
    ]


def spread(right):
    width = right.shape[1] // 2
    right[0, width:] = -right[1, :width]
    right[1, width:] = right[0, :width]


def spectra_copies(freq, column, cross, left, sem):
    width = left.shape[1] // 2
    columns = pl.ds(pl.multiple_of(column * width, width), width)
    return [
        pltpu.make_async_copy(
            cross.at[freq, part, :, columns], left.at[:, pl.ds(part * width, width)], sem.at[part]
        )
        for part in range(2)
    ]


def field_kernel(freq, count, has_total, gated, ids, cross, *refs):
    w_refs, refs = refs[:count], refs[count:]
    total, refs = (refs[0], refs[1:]) if has_total else (None, refs)
    out, left, right, l_sem, w_sem, field, tot, tot_sem = refs
    piece, part = pl.program_id(0), pl.program_id(1)
    copies = [
        weight_copies(freq, ref, right.at[k], w_sem.at[k])
        + spectra_copies(freq, ids[k], cross, left.at[k], l_sem.at[k])
        for k, ref in enumerate(w_refs)
    ]
    for k, group in enumerate(copies):

        @pl.when((piece == k) & (part == 0))
        def _(k=k, group=group):
            if k == 0:
                for copy in group:
                    copy.start()
            for copy in group:
                copy.wait()
            if k + 1 < count:
                for copy in copies[k + 1]:
                    copy.start()
            if k == 0 and has_total:
                pltpu.make_async_copy(total, tot, tot_sem.at[0]).start()
            spread(right.at[k])

    last = piece == count - 1
    if count > 1:

        @pl.when(piece == 0)
        def _():
            field[part] = dot(left[piece], right[piece, part])

        @pl.when((piece > 0) & (piece < count - 1))
        def _():
            field[part] += dot(left[piece], right[piece, part])

    @pl.when(last)
    def _():
        value = dot(left[piece], right[piece, part])
        if gated:
            value = jnp.where(ids[count] == 1, value, 0.0)
        if count > 1:
            value += field[part]
        if has_total:

            @pl.when(part == 0)
            def _():
                pltpu.make_async_copy(total, tot, tot_sem.at[0]).wait()

            value += tot[part]
        out[0] = value


def add_field(cross, freq, ids, pieces, total=None, gated=False):
    rows, (width, sources) = cross.shape[2], pieces[0].shape[2:]
    count, dtype = len(pieces), pieces[0].dtype
    has_total = total is not None
    return pl.pallas_call(
        functools.partial(field_kernel, freq, count, has_total, gated),
        out_shape=jax.ShapeDtypeStruct((2, rows, sources), jnp.float32),
        grid_spec=pltpu.PrefetchScalarGridSpec(
            num_scalar_prefetch=1,
            grid=(count, 2),
            in_specs=[ANYWHERE] * (1 + count + has_total),
            out_specs=pl.BlockSpec(
                (1, rows, sources), lambda p, part, ids: (jnp.where(p == count - 1, part, 0), 0, 0)
            ),
            scratch_shapes=[
                pltpu.VMEM((count, rows, 2 * width), dtype),
                pltpu.VMEM((count, 2, 2 * width, sources), dtype),
                pltpu.SemaphoreType.DMA((count, 2)),
                pltpu.SemaphoreType.DMA((count, 2)),
                pltpu.VMEM((2, rows, sources), jnp.float32),
                pltpu.VMEM((2, rows, sources), jnp.float32),
                pltpu.SemaphoreType.DMA((1,)),
            ],
        ),
        compiler_params=pltpu.CompilerParams(vmem_limit_bytes=VMEM_LIMIT),
        cost_estimate=HINT,
    )(ids, cross, *pieces, *([total] if has_total else []))


def start_rows(freq, ids, base, refs, rows, sem):
    width = rows.shape[1] // 2
    views = []
    for picked, *pieces in (refs[:5], refs[5:]):
        views += [picked.at[freq, :, pl.ds(slot * width, width)] for slot in range(2)]
        views += [at_freq(ref, freq) for ref in pieces]
    for slot in range(2):
        here = pl.ds(slot * width, width)
        for k, source in enumerate(views):

            @pl.when(ids[base + slot] == k)
            def _(source=source, slot=slot, here=here):
                pltpu.make_async_copy(source, rows.at[:, here], sem.at[slot]).start()


def wait_rows(freq, slot, refs, rows, sem):
    width = rows.shape[1] // 2
    source = refs[0].at[freq, :, pl.ds(0, width)]
    here = rows.at[:, pl.ds(slot * width, width)]
    pltpu.make_async_copy(source, here, sem.at[slot]).wait()


def fold(rows, field):
    product = rows.astype(jnp.float32) * field
    return jnp.sum(product.reshape(-1, 8, product.shape[-1]), axis=0)


def late_kernel(freq, ids, cross, w5, w6, w7, block_re, block_im, total, *refs):
    row_refs, refs = refs[:10], refs[10:]
    sums, field_out, left, right, l_sem, w_sem, field, tot, sem, rows, row_sem = refs
    late = ids[7]
    step = pl.program_id(0)
    width, sources = w5.shape[2:]
    lanes = [slice(part * sources, (part + 1) * sources) for part in range(2)]

    def weights(ref, k):
        source = at_freq(ref, freq)
        return [
            pltpu.make_async_copy(
                source.at[part],
                right.at[k, pl.ds(0, width), pl.ds(part * sources, sources)],
                w_sem.at[k, part],
            )
            for part in range(2)
        ]

    def spread_lanes(k):
        right[k, width:, lanes[0]] = -right[k, :width, lanes[1]]
        right[k, width:, lanes[1]] = right[k, :width, lanes[0]]

    first = weights(w5, 0) + spectra_copies(freq, ids[0], cross, left.at[0], l_sem.at[0])
    six, seven = weights(w6, 1), weights(w7, 1)
    second = spectra_copies(freq, ids[1], cross, left.at[1], l_sem.at[1])
    third = [
        pltpu.make_async_copy(
            ref.at[min(k, ref.shape[0] - 1), half],
            left.at[2, pl.ds(half * width, width), pl.ds(k * width, width)],
            l_sem.at[2 + half, k],
        )
        for k, ref in enumerate((block_re, block_im))
        for half in range(2)
    ]
    total_copies = [
        pltpu.make_async_copy(
            total.at[part], tot.at[:, pl.ds(part * sources, sources)], sem.at[part]
        )
        for part in range(2)
    ]
    late_rows = pl.ds(pl.multiple_of(jnp.minimum(late, 1) * width, width), width)
    out_copies = [
        pltpu.make_async_copy(
            field.at[late_rows, pl.ds(part * sources, sources)], field_out.at[part], sem.at[2 + part]
        )
        for part in range(2)
    ]

    @pl.when(step == 0)
    def _():
        sums[...] = jnp.zeros_like(sums)
        for copy in first:
            copy.start()
        for copy in first:
            copy.wait()
        for copy in second:
            copy.start()

        @pl.when(ids[2] == 1)
        def _():
            for copy in seven:
                copy.start()

        @pl.when(ids[2] == 0)
        def _():
            for copy in six:
                copy.start()

        for copy in total_copies:
            copy.start()
        start_rows(freq, ids, 3, row_refs, rows.at[0], row_sem.at[0])
        spread_lanes(0)
        field[...] = dot(left[0], right[0])

    @pl.when(step == 1)
    def _():
        for copy in second + six:
            copy.wait()
        for copy in third:
            copy.start()
        start_rows(freq, ids, 5, row_refs, rows.at[1], row_sem.at[1])
        for copy in total_copies:
            copy.wait()
        spread_lanes(1)
        field[...] = field[...] + tot[...] + dot(left[1], right[1])
        for copy in out_copies:
            copy.start()
        for slot in range(2):
            wait_rows(freq, slot, row_refs, rows.at[0], row_sem.at[0])
        for slot in range(2):

            @pl.when(late != slot)
            def _(slot=slot):
                here = slice(slot * width, (slot + 1) * width)
                for part in range(2):
                    sums[...] += fold(rows[0, part, here], field[here, lanes[part]])

    @pl.when(step == 2)
    def _():
        for copy in third:
            copy.wait()
        for slot in range(2):
            wait_rows(freq, slot, row_refs, rows.at[1], row_sem.at[1])

        @pl.when(ids[2] == 1)
        def _():
            value = dot(left[2], right[0])
            for part in range(2):
                sums[...] += fold(rows[1, part], value[:, lanes[part]])

        for copy in out_copies:
            copy.wait()


def add_late(cross, freq, ids, pieces, blocks, total, row_refs):
    rows, (width, sources) = cross.shape[2], pieces[0].shape[2:]
    dtype = pieces[0].dtype
    return pl.pallas_call(
        functools.partial(late_kernel, freq),
        out_shape=(
            jax.ShapeDtypeStruct((8, sources), jnp.float32),
            jax.ShapeDtypeStruct((2, width, sources), jnp.float32),
        ),
        grid_spec=pltpu.PrefetchScalarGridSpec(
            num_scalar_prefetch=1,
            grid=(3,),
            in_specs=[ANYWHERE] * (7 + len(row_refs)),
            out_specs=(pl.BlockSpec((8, sources), lambda step, ids: (0, 0)), ANYWHERE),
            scratch_shapes=[
                pltpu.VMEM((3, rows, 2 * width), dtype),
                pltpu.VMEM((2, 2 * width, 2 * sources), dtype),
                pltpu.SemaphoreType.DMA((4, 2)),
                pltpu.SemaphoreType.DMA((2, 2)),
                pltpu.VMEM((rows, 2 * sources), jnp.float32),
                pltpu.VMEM((rows, 2 * sources), jnp.float32),
                pltpu.SemaphoreType.DMA((4,)),
                pltpu.VMEM((2, 2, rows, sources), dtype),
                pltpu.SemaphoreType.DMA((2, 2)),
            ],
        ),
        compiler_params=pltpu.CompilerParams(vmem_limit_bytes=VMEM_LIMIT),
        cost_estimate=HINT,
    )(ids, cross, *pieces, *blocks, total, *row_refs)


def dot_kernel(ids, norms, *refs):
    groups, (out, rows, field, sem, total) = (refs[:6], refs[6:12]), refs[12:]
    for freq, (field_ref, _, *sources) in enumerate(groups):

        @pl.when(ids[0] < 4)
        def _(freq=freq, field_ref=field_ref):
            pltpu.make_async_copy(field_ref, field.at[freq], sem.at[0, freq]).start()

        for k, source in enumerate(sources):

            @pl.when(ids[0] == k)
            def _(freq=freq, source=source):
                pltpu.make_async_copy(source.at[0], rows.at[freq], sem.at[1, freq]).start()

    for freq, (field_ref, sums, *sources) in enumerate(groups):
        total[freq : freq + 1] = jnp.sum(sums[...], axis=0, keepdims=True)

        @pl.when(ids[0] < 4)
        def _(freq=freq, field_ref=field_ref, sources=sources):
            pltpu.make_async_copy(field_ref, field.at[freq], sem.at[0, freq]).wait()
            pltpu.make_async_copy(sources[0].at[0], rows.at[freq], sem.at[1, freq]).wait()
            more = sum(fold(rows[freq, part], field[freq, part]) for part in range(2))
            total[freq : freq + 1] += jnp.sum(more, axis=0, keepdims=True)

    total[2:4] = norms[...]
    for k in range(out.shape[0]):
        out[k] = total[...]


def dot_rows(ids, norms, groups):
    late_shape, dtype = groups[0][0].shape, groups[0][2].dtype
    sources = late_shape[-1]
    whole = lambda shape: pl.BlockSpec(shape, lambda i, ids: (0, 0))
    return pl.pallas_call(
        dot_kernel,
        out_shape=jax.ShapeDtypeStruct((copies_to_all(), 4, sources), jnp.float32),
        grid_spec=pltpu.PrefetchScalarGridSpec(
            num_scalar_prefetch=1,
            grid=(1,),
            in_specs=[whole((2, sources))] + [ANYWHERE, whole((8, sources)), *[ANYWHERE] * 4] * 2,
            out_specs=pl.BlockSpec((copies_to_all(), 4, sources), lambda i, ids: (0, 0, 0)),
            scratch_shapes=[
                pltpu.VMEM((2, *late_shape), dtype),
                pltpu.VMEM((2, *late_shape), jnp.float32),
                pltpu.SemaphoreType.DMA((2, 2)),
                pltpu.VMEM((4, sources), jnp.float32),
            ],
        ),
        compiler_params=pltpu.CompilerParams(vmem_limit_bytes=VMEM_LIMIT),
        cost_estimate=HINT,
    )(ids, norms, *groups[0], *groups[1])


def copy_kernel(inputs, jobs, ids, *refs):
    refs, (stage, in_sem, out_sem) = refs[:-3], refs[-3:]
    sources, targets = refs[:inputs], refs[inputs:]
    writes = [
        pltpu.make_async_copy(stage.at[k], target(targets), out_sem.at[k])
        for k, (_, target) in enumerate(jobs)
    ]

    def each(act):
        for k, (options, _) in enumerate(jobs):
            for value, source in options:

                @pl.when(ids[0] == value)
                def _(k=k, source=source):
                    act(k, pltpu.make_async_copy(source(sources, ids), stage.at[k], in_sem.at[k]))

    def pass_on(k, copy):
        copy.wait()
        writes[k].start()

    def finish(k, copy):
        writes[k].wait()

    each(lambda k, copy: copy.start())
    each(pass_on)
    each(finish)


def copies(ids, args, jobs, shapes, unit, dtype, alias=None):
    return pl.pallas_call(
        functools.partial(copy_kernel, len(args), jobs),
        out_shape=[jax.ShapeDtypeStruct(shape, dtype) for shape in shapes],
        grid_spec=pltpu.PrefetchScalarGridSpec(
            num_scalar_prefetch=1,
            grid=(1,),
            in_specs=[ANYWHERE] * len(args),
            out_specs=[ANYWHERE] * len(shapes),
            scratch_shapes=[
                pltpu.VMEM((len(jobs), *unit), dtype),
                pltpu.SemaphoreType.DMA((len(jobs),)),
                pltpu.SemaphoreType.DMA((len(jobs),)),
            ],
        ),
        input_output_aliases={} if alias is None else {1 + alias: 0},
        compiler_params=pltpu.CompilerParams(vmem_limit_bytes=VMEM_LIMIT),
        cost_estimate=HINT,
    )(ids, *args)


def block_source(at, freq, part, half, width):
    def source(refs, ids):
        columns = pl.ds(pl.multiple_of(ids[1] * width, width), width)
        return refs[at].at[freq, part, pl.ds(half * width, width), columns]

    return source


def entry(at, *index):
    return lambda refs, ids=None: refs[at].at[index]


def fill_block(ids, piece, cross):
    _, _, width, sources = piece.shape
    jobs = [
        ([(0, block_source(1, 0, part, half, width))], entry(0, part, half))
        for part in range(2)
        for half in range(2)
    ]
    return copies(ids, [piece, cross], jobs, [piece.shape], (width, sources), piece.dtype, 0)[0]


def take_pair(ids, own, x, n, m):
    freqs, _, width, sources = own.shape
    jobs = [
        (
            [(0, entry(slot, freq, part)), (1, entry(2 + slot, freq, part))],
            entry(0, freq, part, pl.ds(slot * width, width)),
        )
        for freq in range(freqs)
        for part in range(2)
        for slot in range(2)
    ]
    shape = (freqs, 2, 2 * width, sources)
    return copies(ids, [own, x, n, m], jobs, [shape], (width, sources), own.dtype)[0]


def next_kernel(freq, ids, ends, middles, cross, over_x, over_z, stage, in_sem, out_sem):
    width = ends.shape[2]
    columns = pl.ds(pl.multiple_of(ids[1] * width, width), width)
    chunk = width // 4
    plans = [[], []]
    for part in range(2):
        for k in range(4):
            here = pl.ds(k * chunk, chunk)
            block = cross.at[1, freq, pl.ds(part * width + k * chunk, chunk), columns]
            plans[0].append((ends.at[freq, part, here], over_x.at[0, part, here]))
            plans[0].append((block, over_z.at[0, part, here]))
            plans[1].append((middles.at[freq, part, here], over_x.at[0, part, here]))
            plans[1].append((None, over_z.at[0, part, here]))
    for mid, plan in enumerate(plans):

        @pl.when(ids[0] == mid)
        def _(plan=plan):
            reads, writes = [], []
            for k, (source, target) in enumerate(plan):
                place = k if source is not None else k - 1
                if source is not None:
                    reads.append(pltpu.make_async_copy(source, stage.at[k], in_sem.at[k]))
                    writes.append([])
                writes[-1].append(pltpu.make_async_copy(stage.at[place], target, out_sem.at[k]))
            for copy in reads:
                copy.start()
            for read, group in zip(reads, writes):
                read.wait()
                for copy in group:
                    copy.start()
            for group in writes:
                for copy in group:
                    copy.wait()


def take_next(freq, ids, ends, middles, cross):
    _, _, width, sources = ends.shape
    shape = jax.ShapeDtypeStruct((1, 2, width, sources), ends.dtype)
    return pl.pallas_call(
        functools.partial(next_kernel, freq),
        out_shape=[shape, shape],
        grid_spec=pltpu.PrefetchScalarGridSpec(
            num_scalar_prefetch=1,
            grid=(1,),
            in_specs=[ANYWHERE] * 3,
            out_specs=[ANYWHERE] * 2,
            scratch_shapes=[
                pltpu.VMEM((16, width // 4, sources), ends.dtype),
                pltpu.SemaphoreType.DMA((16,)),
                pltpu.SemaphoreType.DMA((16,)),
            ],
        ),
        compiler_params=pltpu.CompilerParams(vmem_limit_bytes=VMEM_LIMIT),
        cost_estimate=HINT,
    )(ids, ends, middles, cross)


def sums_by_swaps(cross, replicas, norms):
    rows, half = cross.shape[2], cross.shape[3]
    width = replicas.shape[3]
    me = lax.axis_index("row").astype(jnp.int32)
    col = lax.axis_index("col").astype(jnp.int32)
    holds = me * rows // half == col
    mid = ((me // 2) % 4 == 1) | ((me // 2) % 4 == 2)
    flag = lambda value: jnp.where(value, 1, 0).astype(jnp.int32).reshape(1)
    ids = lambda *wanted: me ^ jnp.array(wanted, jnp.int32)
    barrier = lambda *values: lax.optimization_barrier(values)

    slots = jnp.arange(2, dtype=jnp.int32)
    per_half = half // width
    own_masks = (2 * me % per_half + slots) ^ me
    next_masks = ((2 * (me ^ 2) % per_half + slots) ^ me) & 3
    table = lambda masks: sum(
        jnp.where(masks == mask, place, 0)
        for mask, place in enumerate((0, 1, 0, 2, 3, 5, 1, 4))
    ) + jnp.where(holds, 0, 6)
    late_slot = own_masks[0] & 1 ^ 1
    late_source = jnp.where(own_masks[0] & 2 != 0, 0, 1) + jnp.where(holds, 0, 2)
    ids_dot = jnp.where(mid, late_source, 4).astype(jnp.int32).reshape(1)
    late_ids = jnp.concatenate(
        [
            ids(5),
            jnp.where(mid, ids(7), ids(6)),
            flag(mid),
            table(own_masks),
            table(next_masks),
            jnp.where(mid, late_slot, 2).reshape(1),
        ]
    ).astype(jnp.int32)
    pair = flag(((me >> 1) ^ me) & 1 != 0)
    ids_a = jnp.concatenate([ids(1, 2, 6), flag(mid)])
    ids_z = jnp.concatenate([flag(mid), ids(7)])
    numbers = [ids_a, ids(3, 4), ids_z, late_ids, pair, ids_dot]

    own = replicas[:, :, 0]
    x = swap(own, "row", 1)
    n = swap(own, "row", 2)
    m = swap_middle(own)
    a0 = add_field(cross, 0, ids(0), [own])
    a1 = add_field(cross, 1, ids(0), [own])
    m = fill_block(ids_z, m, cross)
    x, n, m, a0, a1, norms, *numbers = barrier(x, n, m, a0, a1, norms, *numbers)
    ids_a, ids_b, ids_z, late_ids, pair, ids_dot = numbers

    z = swap(m, "row", 2)
    m2 = swap_middle(n)
    xn = swap(n, "row", 1)
    a0 = add_field(cross, 0, ids_a, [x, n, m], a0, gated=True)
    a1 = add_field(cross, 1, ids_a, [x, n, m], a1, gated=True)
    mine = take_pair(pair, own, x, n, m)
    x_a, x_b = x[0:1], x[1:2]
    z, m2, xn, a0, a1, mine, x_a, x_b = barrier(z, m2, xn, a0, a1, mine, x_a, x_b)

    w4_a, send_a = take_next(0, ids_z, z, m2, cross)
    x5_a = swap(w4_a, "row", 1)
    z_a = swap(send_a, "row", 2)
    w7_a = swap_middle(after(x_a, w4_a))
    other = swap(mine, "col", 1)
    b0 = add_field(cross, 0, ids_b, [xn, w4_a], a0)
    w4_b, send_b = take_next(1, after(ids_z, b0), z, m2, cross)
    b1 = add_field(cross, 1, ids_b, [xn, w4_b], a1)
    x5_a, z_a, w7_a, other, b0, w4_b, send_b, x_b, xn, m2 = barrier(
        x5_a, z_a, w7_a, other, b0, w4_b, send_b, x_b, xn, m2
    )

    x5_b = swap(w4_b, "row", 1)
    z_b = swap(send_b, "row", 2)
    w7_b = swap_middle(x_b)
    other_xn = swap(xn, "col", 1)
    other_m2 = swap(m2, "col", 1)
    early = [mine, xn, m2, xn, xn, other, other_xn, other_m2, other_xn, other_xn]
    sums_a, field_a = add_late(cross, 0, late_ids, [x5_a, z_a, w7_a], [z, z], b0, early)
    x5_b, z_b, w7_b, sums_a, field_a, b1, other_xn, other_m2, x5_a, w7_a = barrier(
        x5_b, z_b, w7_b, sums_a, field_a, b1, other_xn, other_m2, x5_a, w7_a
    )

    late = [w7_a, x5_a, w7_b, x5_b]
    others = [swap(piece, "col", 1) for piece in late]
    early = [mine, xn, m2, xn, xn, other, other_xn, other_m2, other_xn, other_xn]
    sums_b, field_b = add_late(cross, 1, late_ids, [x5_b, z_b, w7_b], [z_a, z_b], b1, early)
    groups = [
        (field_a, sums_a, *late[:2], *others[:2]),
        (field_b, sums_b, *late[2:], *others[2:]),
    ]
    return dot_rows(ids_dot, norms, groups)


def sums_by_gather(cross, replicas, norms):
    rows, half = cross.shape[2], cross.shape[3]
    row_index, col_index = lax.axis_index("row"), lax.axis_index("col")
    first_row = row_index * rows
    holder = first_row // half
    whole = lax.all_gather(replicas, "row", axis=3, tiled=True)[:, :, 0]
    parts = jnp.einsum("fark,fbks->fabrs", cross, whole, preferred_element_type=jnp.float32)
    field = jnp.stack([parts[:, 0, 0] - parts[:, 1, 1], parts[:, 0, 1] + parts[:, 1, 0]], axis=1)
    own_rows = lax.dynamic_slice_in_dim(whole, first_row - holder * half, rows, 2)
    block_rows = jnp.where(holder == col_index, own_rows, swap(own_rows, "col", 1))
    numer = jnp.sum(block_rows.astype(jnp.float32) * field, axis=(1, 2))
    sums = jnp.concatenate([numer, norms])
    return jnp.broadcast_to(sums[None], (copies_to_all(), *sums.shape))


def body(cross_spectra, replicas, tile_order):
    fnum = cross_spectra.shape[0]
    sources = replicas.shape[4]
    own = replicas[:, :, 0].astype(jnp.float32)
    norms = jnp.sum(own * own, axis=(1, 2))
    doubling = (
        lax.axis_size("row") == 8
        and fnum == 2
        and replicas.shape[3] % 128 == 0
        and cross_spectra.shape[2] == 2 * replicas.shape[3]
    )
    sums = (sums_by_swaps if doubling else sums_by_gather)(cross_spectra, replicas, norms)
    sums = sum_all(sums)
    numer, norms = sums[:fnum], sums[fnum:]
    beam = numer / (norms + 1e-06)
    width = sources // lax.axis_size("col")
    beam_half = lax.dynamic_slice_in_dim(beam, lax.axis_index("col") * width, width, 1)
    peak = jnp.max(jnp.abs(beam), axis=1) + 1e-06
    count = tile_order.shape[0]
    picker = (tile_order[:, None] == jnp.arange(count, dtype=jnp.int32)[None, :]).astype(jnp.float32)
    tiles = beam.reshape(fnum, count, sources // count)
    refined = (
        jnp.einsum("tu,fup->ftp", picker, tiles, precision=lax.Precision.HIGHEST)
        / peak[:, None, None]
    )
    return (beam_half, refined)


def solution(mesh):
    in_specs = (P("groups", None, "row", "col"), P("groups", None, "col", "row", None), P("groups"))
    out_specs = (P("groups", "col"), P("groups", None, None))
    return jax.shard_map(body, mesh=mesh, in_specs=in_specs, out_specs=out_specs, check_vma=False)
```

```python
import functools
import math

import jax
import jax.numpy as jnp
from jax import lax
from jax.experimental import pallas as pl
from jax.experimental.pallas import tpu as pltpu
from jax.sharding import PartitionSpec as P

VMEM_LIMIT = 63 * 1024 * 1024
LATE_LIMIT = 40 * 1024 * 1024
HINT = pl.CostEstimate(flops=1, bytes_accessed=1, transcendentals=0)
ANYWHERE = pl.BlockSpec(memory_space=pl.ANY)


def swap(value, axis, mask):
    size = math.prod(lax.axis_size(name) for name in (axis if isinstance(axis, tuple) else (axis,)))
    return lax.ppermute(value, axis, [(source, source ^ mask) for source in range(size)])


def swap_middle(value):
    axes = ("row", "col")
    size = lax.axis_size("row") * lax.axis_size("col")
    target = lambda k: k ^ 12 if (k // 4) % 4 in (1, 2) else k ^ 1
    return lax.ppermute(value, axes, [(k, target(k)) for k in range(size)])


def after(value, *others):
    return lax.optimization_barrier((value, *others))[0]


def copies_to_all():
    size = lax.axis_size("row") * lax.axis_size("col")
    return size if size <= 16 else 1


def sum_all(copies):
    axes = ("row", "col")
    if copies.shape[0] == 1:
        return lax.psum(copies[0], axes)
    return jnp.sum(lax.all_to_all(copies, axes, 0, 0, tiled=True), axis=0)


def dot(a, b):
    return jnp.dot(a, b, preferred_element_type=jnp.float32)


def at_freq(ref, freq):
    return ref.at[freq if ref.shape[0] > 1 else 0]


def weight_copies(freq, ref, right, sem):
    low = pl.ds(0, ref.shape[2])
    source = at_freq(ref, freq)
    return [
        pltpu.make_async_copy(source.at[0], right.at[0, low], sem.at[0]),
        pltpu.make_async_copy(source.at[1], right.at[1, low], sem.at[1]),
    ]


def spread(right):
    width = right.shape[1] // 2
    right[0, width:] = -right[1, :width]
    right[1, width:] = right[0, :width]


def spectra_copies(freq, column, cross, left, sem):
    width = left.shape[1] // 2
    columns = pl.ds(pl.multiple_of(column * width, width), width)
    return [
        pltpu.make_async_copy(
            cross.at[freq, part, :, columns], left.at[:, pl.ds(part * width, width)], sem.at[part]
        )
        for part in range(2)
    ]


def field_kernel(freq, count, has_total, gated, ids, cross, *refs):
    w_refs, refs = refs[:count], refs[count:]
    total, refs = (refs[0], refs[1:]) if has_total else (None, refs)
    out, left, right, l_sem, w_sem, field, tot, tot_sem = refs
    piece, part = pl.program_id(0), pl.program_id(1)
    copies = [
        weight_copies(freq, ref, right.at[k], w_sem.at[k])
        + spectra_copies(freq, ids[k], cross, left.at[k], l_sem.at[k])
        for k, ref in enumerate(w_refs)
    ]
    for k, group in enumerate(copies):

        @pl.when((piece == k) & (part == 0))
        def _(k=k, group=group):
            if k == 0:
                for copy in group:
                    copy.start()
            for copy in group:
                copy.wait()
            if k + 1 < count:
                for copy in copies[k + 1]:
                    copy.start()
            if k == 0 and has_total:
                pltpu.make_async_copy(total, tot, tot_sem.at[0]).start()
            spread(right.at[k])

    last = piece == count - 1
    if count > 1:

        @pl.when(piece == 0)
        def _():
            field[part] = dot(left[piece], right[piece, part])

        @pl.when((piece > 0) & (piece < count - 1))
        def _():
            field[part] += dot(left[piece], right[piece, part])

    @pl.when(last)
    def _():
        value = dot(left[piece], right[piece, part])
        if gated:
            value = jnp.where(ids[count] == 1, value, 0.0)
        if count > 1:
            value += field[part]
        if has_total:

            @pl.when(part == 0)
            def _():
                pltpu.make_async_copy(total, tot, tot_sem.at[0]).wait()

            value += tot[part]
        out[0] = value


def add_field(cross, freq, ids, pieces, total=None, gated=False):
    rows, (width, sources) = cross.shape[2], pieces[0].shape[2:]
    count, dtype = len(pieces), pieces[0].dtype
    has_total = total is not None
    return pl.pallas_call(
        functools.partial(field_kernel, freq, count, has_total, gated),
        out_shape=jax.ShapeDtypeStruct((2, rows, sources), jnp.float32),
        grid_spec=pltpu.PrefetchScalarGridSpec(
            num_scalar_prefetch=1,
            grid=(count, 2),
            in_specs=[ANYWHERE] * (1 + count + has_total),
            out_specs=pl.BlockSpec(
                (1, rows, sources), lambda p, part, ids: (jnp.where(p == count - 1, part, 0), 0, 0)
            ),
            scratch_shapes=[
                pltpu.VMEM((count, rows, 2 * width), dtype),
                pltpu.VMEM((count, 2, 2 * width, sources), dtype),
                pltpu.SemaphoreType.DMA((count, 2)),
                pltpu.SemaphoreType.DMA((count, 2)),
                pltpu.VMEM((2, rows, sources), jnp.float32),
                pltpu.VMEM((2, rows, sources), jnp.float32),
                pltpu.SemaphoreType.DMA((1,)),
            ],
        ),
        compiler_params=pltpu.CompilerParams(vmem_limit_bytes=VMEM_LIMIT),
        cost_estimate=HINT,
    )(ids, cross, *pieces, *([total] if has_total else []))


def start_rows(freq, ids, base, refs, rows, sem):
    width = rows.shape[1] // 2
    views = []
    for picked, *pieces in (refs[:5], refs[5:]):
        views += [picked.at[freq, :, pl.ds(slot * width, width)] for slot in range(2)]
        views += [at_freq(ref, freq) for ref in pieces]
    for slot in range(2):
        here = pl.ds(slot * width, width)
        for k, source in enumerate(views):

            @pl.when(ids[base + slot] == k)
            def _(source=source, slot=slot, here=here):
                pltpu.make_async_copy(source, rows.at[:, here], sem.at[slot]).start()


def wait_rows(freq, slot, refs, rows, sem):
    width = rows.shape[1] // 2
    source = refs[0].at[freq, :, pl.ds(0, width)]
    here = rows.at[:, pl.ds(slot * width, width)]
    pltpu.make_async_copy(source, here, sem.at[slot]).wait()


def fold(rows, field):
    product = rows.astype(jnp.float32) * field
    return jnp.sum(product.reshape(-1, 8, product.shape[-1]), axis=0)


def late_kernel(freq, ids, cross, w5, w6, w7, block_re, block_im, total, *refs):
    row_refs, refs = refs[:10], refs[10:]
    sums, field_out, left, right, l_sem, w_sem, field, tot, sem, rows, row_sem = refs
    late = ids[7]
    step = pl.program_id(0)
    width, sources = w5.shape[2:]
    lanes = [slice(part * sources, (part + 1) * sources) for part in range(2)]

    def weights(ref, k):
        source = at_freq(ref, freq)
        return [
            pltpu.make_async_copy(
                source.at[part],
                right.at[k, pl.ds(0, width), pl.ds(part * sources, sources)],
                w_sem.at[k, part],
            )
            for part in range(2)
        ]

    def spread_lanes(k):
        right[k, width:, lanes[0]] = -right[k, :width, lanes[1]]
        right[k, width:, lanes[1]] = right[k, :width, lanes[0]]

    first = weights(w5, 0) + spectra_copies(freq, ids[0], cross, left.at[0], l_sem.at[0])
    six, seven = weights(w6, 1), weights(w7, 1)
    second = spectra_copies(freq, ids[1], cross, left.at[1], l_sem.at[1])
    third = [
        pltpu.make_async_copy(
            ref.at[min(k, ref.shape[0] - 1), half],
            left.at[2, pl.ds(half * width, width), pl.ds(k * width, width)],
            l_sem.at[2 + half, k],
        )
        for k, ref in enumerate((block_re, block_im))
        for half in range(2)
    ]
    total_copies = [
        pltpu.make_async_copy(
            total.at[part], tot.at[:, pl.ds(part * sources, sources)], sem.at[part]
        )
        for part in range(2)
    ]
    late_rows = pl.ds(pl.multiple_of(jnp.minimum(late, 1) * width, width), width)
    out_copies = [
        pltpu.make_async_copy(
            field.at[late_rows, pl.ds(part * sources, sources)], field_out.at[part], sem.at[2 + part]
        )
        for part in range(2)
    ]

    @pl.when(step == 0)
    def _():
        sums[...] = jnp.zeros_like(sums)
        for copy in first:
            copy.start()
        for copy in first:
            copy.wait()
        for copy in second:
            copy.start()

        @pl.when(ids[2] == 1)
        def _():
            for copy in seven:
                copy.start()

        @pl.when(ids[2] == 0)
        def _():
            for copy in six:
                copy.start()

        for copy in total_copies:
            copy.start()
        start_rows(freq, ids, 3, row_refs, rows.at[0], row_sem.at[0])
        spread_lanes(0)
        field[...] = dot(left[0], right[0])

    @pl.when(step == 1)
    def _():
        for copy in second + six:
            copy.wait()
        for copy in third:
            copy.start()
        start_rows(freq, ids, 5, row_refs, rows.at[1], row_sem.at[1])
        for copy in total_copies:
            copy.wait()
        spread_lanes(1)
        field[...] = field[...] + tot[...] + dot(left[1], right[1])
        for copy in out_copies:
            copy.start()
        for slot in range(2):
            wait_rows(freq, slot, row_refs, rows.at[0], row_sem.at[0])
        for slot in range(2):

            @pl.when(late != slot)
            def _(slot=slot):
                here = slice(slot * width, (slot + 1) * width)
                for part in range(2):
                    sums[...] += fold(rows[0, part, here], field[here, lanes[part]])

    @pl.when(step == 2)
    def _():
        for copy in third:
            copy.wait()
        for slot in range(2):
            wait_rows(freq, slot, row_refs, rows.at[1], row_sem.at[1])

        @pl.when(ids[2] == 1)
        def _():
            value = dot(left[2], right[0])
            for part in range(2):
                sums[...] += fold(rows[1, part], value[:, lanes[part]])

        for copy in out_copies:
            copy.wait()


def add_late(cross, freq, ids, pieces, blocks, total, row_refs):
    rows, (width, sources) = cross.shape[2], pieces[0].shape[2:]
    dtype = pieces[0].dtype
    return pl.pallas_call(
        functools.partial(late_kernel, freq),
        out_shape=(
            jax.ShapeDtypeStruct((8, sources), jnp.float32),
            jax.ShapeDtypeStruct((2, width, sources), jnp.float32),
        ),
        grid_spec=pltpu.PrefetchScalarGridSpec(
            num_scalar_prefetch=1,
            grid=(3,),
            in_specs=[ANYWHERE] * (7 + len(row_refs)),
            out_specs=(pl.BlockSpec((8, sources), lambda step, ids: (0, 0)), ANYWHERE),
            scratch_shapes=[
                pltpu.VMEM((3, rows, 2 * width), dtype),
                pltpu.VMEM((2, 2 * width, 2 * sources), dtype),
                pltpu.SemaphoreType.DMA((4, 2)),
                pltpu.SemaphoreType.DMA((2, 2)),
                pltpu.VMEM((rows, 2 * sources), jnp.float32),
                pltpu.VMEM((rows, 2 * sources), jnp.float32),
                pltpu.SemaphoreType.DMA((4,)),
                pltpu.VMEM((2, 2, rows, sources), dtype),
                pltpu.SemaphoreType.DMA((2, 2)),
            ],
        ),
        compiler_params=pltpu.CompilerParams(vmem_limit_bytes=LATE_LIMIT),
        cost_estimate=HINT,
    )(ids, cross, *pieces, *blocks, total, *row_refs)


def dot_kernel(ids, norms, *refs):
    groups, (out, rows, field, sem, total) = (refs[:6], refs[6:12]), refs[12:]
    for freq, (field_ref, _, *sources) in enumerate(groups):

        @pl.when(ids[0] < 4)
        def _(freq=freq, field_ref=field_ref):
            pltpu.make_async_copy(field_ref, field.at[freq], sem.at[0, freq]).start()

        for k, source in enumerate(sources):

            @pl.when(ids[0] == k)
            def _(freq=freq, source=source):
                pltpu.make_async_copy(source.at[0], rows.at[freq], sem.at[1, freq]).start()

    for freq, (field_ref, sums, *sources) in enumerate(groups):
        total[freq : freq + 1] = jnp.sum(sums[...], axis=0, keepdims=True)

        @pl.when(ids[0] < 4)
        def _(freq=freq, field_ref=field_ref, sources=sources):
            pltpu.make_async_copy(field_ref, field.at[freq], sem.at[0, freq]).wait()
            pltpu.make_async_copy(sources[0].at[0], rows.at[freq], sem.at[1, freq]).wait()
            more = sum(fold(rows[freq, part], field[freq, part]) for part in range(2))
            total[freq : freq + 1] += jnp.sum(more, axis=0, keepdims=True)

    total[2:4] = norms[...]
    for k in range(out.shape[0]):
        out[k] = total[...]


def dot_rows(ids, norms, groups):
    late_shape, dtype = groups[0][0].shape, groups[0][2].dtype
    sources = late_shape[-1]
    whole = lambda shape: pl.BlockSpec(shape, lambda i, ids: (0, 0))
    return pl.pallas_call(
        dot_kernel,
        out_shape=jax.ShapeDtypeStruct((copies_to_all(), 4, sources), jnp.float32),
        grid_spec=pltpu.PrefetchScalarGridSpec(
            num_scalar_prefetch=1,
            grid=(1,),
            in_specs=[whole((2, sources))] + [ANYWHERE, whole((8, sources)), *[ANYWHERE] * 4] * 2,
            out_specs=pl.BlockSpec((copies_to_all(), 4, sources), lambda i, ids: (0, 0, 0)),
            scratch_shapes=[
                pltpu.VMEM((2, *late_shape), dtype),
                pltpu.VMEM((2, *late_shape), jnp.float32),
                pltpu.SemaphoreType.DMA((2, 2)),
                pltpu.VMEM((4, sources), jnp.float32),
            ],
        ),
        compiler_params=pltpu.CompilerParams(vmem_limit_bytes=LATE_LIMIT),
        cost_estimate=HINT,
    )(ids, norms, *groups[0], *groups[1])


def copy_kernel(inputs, jobs, ids, *refs):
    refs, (stage, in_sem, out_sem) = refs[:-3], refs[-3:]
    sources, targets = refs[:inputs], refs[inputs:]
    writes = [
        pltpu.make_async_copy(stage.at[k], target(targets), out_sem.at[k])
        for k, (_, target) in enumerate(jobs)
    ]

    def each(act):
        for k, (options, _) in enumerate(jobs):
            for value, source in options:

                @pl.when(ids[0] == value)
                def _(k=k, source=source):
                    act(k, pltpu.make_async_copy(source(sources, ids), stage.at[k], in_sem.at[k]))

    def pass_on(k, copy):
        copy.wait()
        writes[k].start()

    def finish(k, copy):
        writes[k].wait()

    each(lambda k, copy: copy.start())
    each(pass_on)
    each(finish)


def copies(ids, args, jobs, shapes, unit, dtype, alias=None):
    return pl.pallas_call(
        functools.partial(copy_kernel, len(args), jobs),
        out_shape=[jax.ShapeDtypeStruct(shape, dtype) for shape in shapes],
        grid_spec=pltpu.PrefetchScalarGridSpec(
            num_scalar_prefetch=1,
            grid=(1,),
            in_specs=[ANYWHERE] * len(args),
            out_specs=[ANYWHERE] * len(shapes),
            scratch_shapes=[
                pltpu.VMEM((len(jobs), *unit), dtype),
                pltpu.SemaphoreType.DMA((len(jobs),)),
                pltpu.SemaphoreType.DMA((len(jobs),)),
            ],
        ),
        input_output_aliases={} if alias is None else {1 + alias: 0},
        compiler_params=pltpu.CompilerParams(vmem_limit_bytes=VMEM_LIMIT),
        cost_estimate=HINT,
    )(ids, *args)


def block_source(at, freq, part, half, width):
    def source(refs, ids):
        columns = pl.ds(pl.multiple_of(ids[1] * width, width), width)
        return refs[at].at[freq, part, pl.ds(half * width, width), columns]

    return source


def entry(at, *index):
    return lambda refs, ids=None: refs[at].at[index]


def fill_block(ids, piece, cross):
    _, _, width, sources = piece.shape
    jobs = [
        ([(0, block_source(1, 0, part, half, width))], entry(0, part, half))
        for part in range(2)
        for half in range(2)
    ]
    return copies(ids, [piece, cross], jobs, [piece.shape], (width, sources), piece.dtype, 0)[0]


def take_pair(ids, own, x, n, m):
    freqs, _, width, sources = own.shape
    jobs = [
        (
            [(0, entry(slot, freq, part)), (1, entry(2 + slot, freq, part))],
            entry(0, freq, part, pl.ds(slot * width, width)),
        )
        for freq in range(freqs)
        for part in range(2)
        for slot in range(2)
    ]
    shape = (freqs, 2, 2 * width, sources)
    return copies(ids, [own, x, n, m], jobs, [shape], (width, sources), own.dtype)[0]


def next_kernel(freq, ids, ends, middles, cross, over_x, over_z, stage, in_sem, out_sem):
    width = ends.shape[2]
    columns = pl.ds(pl.multiple_of(ids[1] * width, width), width)
    block = [cross.at[1, freq, pl.ds(half * width, width), columns] for half in range(2)]
    plans = [
        [(ends.at[freq, 0], 0), (ends.at[freq, 1], 1), (block[0], 2), (block[1], 3)],
        [(middles.at[freq, 0], 0), (middles.at[freq, 1], 1)],
    ]
    for mid, plan in enumerate(plans):

        @pl.when(ids[0] == mid)
        def _(mid=mid, plan=plan):
            reads = [
                pltpu.make_async_copy(source, stage.at[k], in_sem.at[k]) for source, k in plan
            ]
            writes = [
                [pltpu.make_async_copy(stage.at[k], over_x.at[0, k], out_sem.at[k])]
                if k < 2
                else [pltpu.make_async_copy(stage.at[k], over_z.at[0, k - 2], out_sem.at[k])]
                for _, k in plan
            ]
            if mid:
                for k in range(2):
                    writes[k].append(
                        pltpu.make_async_copy(stage.at[k], over_z.at[0, k], out_sem.at[2 + k])
                    )
            for copy in reads:
                copy.start()
            for read, group in zip(reads, writes):
                read.wait()
                for copy in group:
                    copy.start()
            for group in writes:
                for copy in group:
                    copy.wait()


def take_next(freq, ids, ends, middles, cross):
    _, _, width, sources = ends.shape
    shape = jax.ShapeDtypeStruct((1, 2, width, sources), ends.dtype)
    return pl.pallas_call(
        functools.partial(next_kernel, freq),
        out_shape=[shape, shape],
        grid_spec=pltpu.PrefetchScalarGridSpec(
            num_scalar_prefetch=1,
            grid=(1,),
            in_specs=[ANYWHERE] * 3,
            out_specs=[ANYWHERE] * 2,
            scratch_shapes=[
                pltpu.VMEM((4, width, sources), ends.dtype),
                pltpu.SemaphoreType.DMA((4,)),
                pltpu.SemaphoreType.DMA((4,)),
            ],
        ),
        compiler_params=pltpu.CompilerParams(vmem_limit_bytes=VMEM_LIMIT),
        cost_estimate=HINT,
    )(ids, ends, middles, cross)


def sums_by_swaps(cross, replicas, norms):
    rows, half = cross.shape[2], cross.shape[3]
    width = replicas.shape[3]
    me = lax.axis_index("row").astype(jnp.int32)
    col = lax.axis_index("col").astype(jnp.int32)
    holds = me * rows // half == col
    mid = ((me // 2) % 4 == 1) | ((me // 2) % 4 == 2)
    flag = lambda value: jnp.where(value, 1, 0).astype(jnp.int32).reshape(1)
    ids = lambda *wanted: me ^ jnp.array(wanted, jnp.int32)
    barrier = lambda *values: lax.optimization_barrier(values)

    slots = jnp.arange(2, dtype=jnp.int32)
    per_half = half // width
    own_masks = (2 * me % per_half + slots) ^ me
    next_masks = ((2 * (me ^ 2) % per_half + slots) ^ me) & 3
    table = lambda masks: sum(
        jnp.where(masks == mask, place, 0)
        for mask, place in enumerate((0, 1, 0, 2, 3, 5, 1, 4))
    ) + jnp.where(holds, 0, 6)
    late_slot = own_masks[0] & 1 ^ 1
    late_source = jnp.where(own_masks[0] & 2 != 0, 0, 1) + jnp.where(holds, 0, 2)
    ids_dot = jnp.where(mid, late_source, 4).astype(jnp.int32).reshape(1)
    late_ids = jnp.concatenate(
        [
            ids(5),
            jnp.where(mid, ids(7), ids(6)),
            flag(mid),
            table(own_masks),
            table(next_masks),
            jnp.where(mid, late_slot, 2).reshape(1),
        ]
    ).astype(jnp.int32)
    pair = flag(((me >> 1) ^ me) & 1 != 0)
    ids_a = jnp.concatenate([ids(1, 2, 6), flag(mid)])
    ids_z = jnp.concatenate([flag(mid), ids(7)])
    numbers = [ids_a, ids(3, 4), ids_z, late_ids, pair, ids_dot]

    own = replicas[:, :, 0]
    x = swap(own, "row", 1)
    n = swap(own, "row", 2)
    m = swap_middle(own)
    a0 = add_field(cross, 0, ids(0), [own])
    a1 = add_field(cross, 1, ids(0), [own])
    m = fill_block(ids_z, m, cross)
    x, n, m, a0, a1, norms, *numbers = barrier(x, n, m, a0, a1, norms, *numbers)
    ids_a, ids_b, ids_z, late_ids, pair, ids_dot = numbers

    z = swap(m, "row", 2)
    m2 = swap_middle(n)
    xn = swap(n, "row", 1)
    a0 = add_field(cross, 0, ids_a, [x, n, m], a0, gated=True)
    a1 = add_field(cross, 1, ids_a, [x, n, m], a1, gated=True)
    mine = take_pair(pair, own, x, n, m)
    x_a, x_b = x[0:1], x[1:2]
    z, m2, xn, a0, a1, mine, x_a, x_b = barrier(z, m2, xn, a0, a1, mine, x_a, x_b)

    w4_a, send_a = take_next(0, ids_z, z, m2, cross)
    x5_a = swap(w4_a, "row", 1)
    z_a = swap(send_a, "row", 2)
    w7_a = swap_middle(after(x_a, w4_a))
    other = swap(mine, "col", 1)
    b0 = add_field(cross, 0, ids_b, [xn, w4_a], a0)
    w4_b, send_b = take_next(1, after(ids_z, b0), z, m2, cross)
    b1 = add_field(cross, 1, ids_b, [xn, w4_b], a1)
    x5_a, z_a, w7_a, other, b0, w4_b, send_b, x_b, xn, m2 = barrier(
        x5_a, z_a, w7_a, other, b0, w4_b, send_b, x_b, xn, m2
    )

    x5_b = swap(w4_b, "row", 1)
    z_b = swap(send_b, "row", 2)
    w7_b = swap_middle(x_b)
    other_xn = swap(xn, "col", 1)
    other_m2 = swap(m2, "col", 1)
    early = [mine, xn, m2, xn, xn, other, other_xn, other_m2, other_xn, other_xn]
    sums_a, field_a = add_late(cross, 0, late_ids, [x5_a, z_a, w7_a], [z, z], b0, early)
    x5_b, z_b, w7_b, sums_a, field_a, b1, other_xn, other_m2, x5_a, w7_a = barrier(
        x5_b, z_b, w7_b, sums_a, field_a, b1, other_xn, other_m2, x5_a, w7_a
    )

    late = [w7_a, x5_a, w7_b, x5_b]
    others = [swap(piece, "col", 1) for piece in late]
    early = [mine, xn, m2, xn, xn, other, other_xn, other_m2, other_xn, other_xn]
    sums_b, field_b = add_late(cross, 1, late_ids, [x5_b, z_b, w7_b], [z_a, z_b], b1, early)
    groups = [
        (field_a, sums_a, *late[:2], *others[:2]),
        (field_b, sums_b, *late[2:], *others[2:]),
    ]
    return dot_rows(ids_dot, norms, groups)


def sums_by_gather(cross, replicas, norms):
    rows, half = cross.shape[2], cross.shape[3]
    row_index, col_index = lax.axis_index("row"), lax.axis_index("col")
    first_row = row_index * rows
    holder = first_row // half
    whole = lax.all_gather(replicas, "row", axis=3, tiled=True)[:, :, 0]
    parts = jnp.einsum("fark,fbks->fabrs", cross, whole, preferred_element_type=jnp.float32)
    field = jnp.stack([parts[:, 0, 0] - parts[:, 1, 1], parts[:, 0, 1] + parts[:, 1, 0]], axis=1)
    own_rows = lax.dynamic_slice_in_dim(whole, first_row - holder * half, rows, 2)
    block_rows = jnp.where(holder == col_index, own_rows, swap(own_rows, "col", 1))
    numer = jnp.sum(block_rows.astype(jnp.float32) * field, axis=(1, 2))
    sums = jnp.concatenate([numer, norms])
    return jnp.broadcast_to(sums[None], (copies_to_all(), *sums.shape))


def body(cross_spectra, replicas, tile_order):
    fnum = cross_spectra.shape[0]
    sources = replicas.shape[4]
    own = replicas[:, :, 0].astype(jnp.float32)
    norms = jnp.sum(own * own, axis=(1, 2))
    doubling = (
        lax.axis_size("row") == 8
        and fnum == 2
        and replicas.shape[3] % 128 == 0
        and cross_spectra.shape[2] == 2 * replicas.shape[3]
    )
    sums = (sums_by_swaps if doubling else sums_by_gather)(cross_spectra, replicas, norms)
    sums = sum_all(sums)
    numer, norms = sums[:fnum], sums[fnum:]
    beam = numer / (norms + 1e-06)
    width = sources // lax.axis_size("col")
    beam_half = lax.dynamic_slice_in_dim(beam, lax.axis_index("col") * width, width, 1)
    peak = jnp.max(jnp.abs(beam), axis=1) + 1e-06
    count = tile_order.shape[0]
    picker = (tile_order[:, None] == jnp.arange(count, dtype=jnp.int32)[None, :]).astype(jnp.float32)
    tiles = beam.reshape(fnum, count, sources // count)
    refined = (
        jnp.einsum("tu,fup->ftp", picker, tiles, precision=lax.Precision.HIGHEST)
        / peak[:, None, None]
    )
    return (beam_half, refined)


def solution(mesh):
    in_specs = (P("groups", None, "row", "col"), P("groups", None, "col", "row", None), P("groups"))
    out_specs = (P("groups", "col"), P("groups", None, None))
    return jax.shard_map(body, mesh=mesh, in_specs=in_specs, out_specs=out_specs, check_vma=False)
```

```python
import functools
import math

import jax
import jax.numpy as jnp
from jax import lax
from jax.experimental import pallas as pl
from jax.experimental.pallas import tpu as pltpu
from jax.sharding import PartitionSpec as P

VMEM_LIMIT = 63 * 1024 * 1024
LATE_LIMIT = 30 * 1024 * 1024
HINT = pl.CostEstimate(flops=1, bytes_accessed=1, transcendentals=0)
ANYWHERE = pl.BlockSpec(memory_space=pl.ANY)


def swap(value, axis, mask):
    size = math.prod(lax.axis_size(name) for name in (axis if isinstance(axis, tuple) else (axis,)))
    return lax.ppermute(value, axis, [(source, source ^ mask) for source in range(size)])


def swap_middle(value):
    axes = ("row", "col")
    size = lax.axis_size("row") * lax.axis_size("col")
    target = lambda k: k ^ 12 if (k // 4) % 4 in (1, 2) else k ^ 1
    return lax.ppermute(value, axes, [(k, target(k)) for k in range(size)])


def after(value, *others):
    return lax.optimization_barrier((value, *others))[0]


def copies_to_all():
    size = lax.axis_size("row") * lax.axis_size("col")
    return size if size <= 16 else 1


def sum_all(copies):
    axes = ("row", "col")
    if copies.shape[0] == 1:
        return lax.psum(copies[0], axes)
    return jnp.sum(lax.all_to_all(copies, axes, 0, 0, tiled=True), axis=0)


def dot(a, b):
    return jnp.dot(a, b, preferred_element_type=jnp.float32)


def at_freq(ref, freq):
    return ref.at[freq if ref.shape[0] > 1 else 0]


def weight_copies(freq, ref, right, sem):
    low = pl.ds(0, ref.shape[2])
    source = at_freq(ref, freq)
    return [
        pltpu.make_async_copy(source.at[0], right.at[0, low], sem.at[0]),
        pltpu.make_async_copy(source.at[1], right.at[1, low], sem.at[1]),
    ]


def spread(right):
    width = right.shape[1] // 2
    right[0, width:] = -right[1, :width]
    right[1, width:] = right[0, :width]


def spectra_copies(freq, column, cross, left, sem):
    width = left.shape[1] // 2
    columns = pl.ds(pl.multiple_of(column * width, width), width)
    return [
        pltpu.make_async_copy(
            cross.at[freq, part, :, columns], left.at[:, pl.ds(part * width, width)], sem.at[part]
        )
        for part in range(2)
    ]


def field_kernel(freq, count, has_total, gated, ids, cross, *refs):
    w_refs, refs = refs[:count], refs[count:]
    total, refs = (refs[0], refs[1:]) if has_total else (None, refs)
    out, left, right, l_sem, w_sem, field, tot, tot_sem = refs
    piece, part = pl.program_id(0), pl.program_id(1)
    copies = [
        weight_copies(freq, ref, right.at[k], w_sem.at[k])
        + spectra_copies(freq, ids[k], cross, left.at[k], l_sem.at[k])
        for k, ref in enumerate(w_refs)
    ]
    for k, group in enumerate(copies):

        @pl.when((piece == k) & (part == 0))
        def _(k=k, group=group):
            if k == 0:
                for copy in group:
                    copy.start()
            for copy in group:
                copy.wait()
            if k + 1 < count:
                for copy in copies[k + 1]:
                    copy.start()
            if k == 0 and has_total:
                pltpu.make_async_copy(total, tot, tot_sem.at[0]).start()
            spread(right.at[k])

    last = piece == count - 1
    if count > 1:

        @pl.when(piece == 0)
        def _():
            field[part] = dot(left[piece], right[piece, part])

        @pl.when((piece > 0) & (piece < count - 1))
        def _():
            field[part] += dot(left[piece], right[piece, part])

    @pl.when(last)
    def _():
        value = dot(left[piece], right[piece, part])
        if gated:
            value = jnp.where(ids[count] == 1, value, 0.0)
        if count > 1:
            value += field[part]
        if has_total:

            @pl.when(part == 0)
            def _():
                pltpu.make_async_copy(total, tot, tot_sem.at[0]).wait()

            value += tot[part]
        out[0] = value


def add_field(cross, freq, ids, pieces, total=None, gated=False):
    rows, (width, sources) = cross.shape[2], pieces[0].shape[2:]
    count, dtype = len(pieces), pieces[0].dtype
    has_total = total is not None
    return pl.pallas_call(
        functools.partial(field_kernel, freq, count, has_total, gated),
        out_shape=jax.ShapeDtypeStruct((2, rows, sources), jnp.float32),
        grid_spec=pltpu.PrefetchScalarGridSpec(
            num_scalar_prefetch=1,
            grid=(count, 2),
            in_specs=[ANYWHERE] * (1 + count + has_total),
            out_specs=pl.BlockSpec(
                (1, rows, sources), lambda p, part, ids: (jnp.where(p == count - 1, part, 0), 0, 0)
            ),
            scratch_shapes=[
                pltpu.VMEM((count, rows, 2 * width), dtype),
                pltpu.VMEM((count, 2, 2 * width, sources), dtype),
                pltpu.SemaphoreType.DMA((count, 2)),
                pltpu.SemaphoreType.DMA((count, 2)),
                pltpu.VMEM((2, rows, sources), jnp.float32),
                pltpu.VMEM((2, rows, sources), jnp.float32),
                pltpu.SemaphoreType.DMA((1,)),
            ],
        ),
        compiler_params=pltpu.CompilerParams(vmem_limit_bytes=VMEM_LIMIT),
        cost_estimate=HINT,
    )(ids, cross, *pieces, *([total] if has_total else []))


def start_rows(freq, ids, base, refs, rows, sem):
    width = rows.shape[1] // 2
    views = []
    for picked, *pieces in (refs[:5], refs[5:]):
        views += [picked.at[freq, :, pl.ds(slot * width, width)] for slot in range(2)]
        views += [at_freq(ref, freq) for ref in pieces]
    for slot in range(2):
        here = pl.ds(slot * width, width)
        for k, source in enumerate(views):

            @pl.when(ids[base + slot] == k)
            def _(source=source, slot=slot, here=here):
                pltpu.make_async_copy(source, rows.at[:, here], sem.at[slot]).start()


def wait_rows(freq, slot, refs, rows, sem):
    width = rows.shape[1] // 2
    source = refs[0].at[freq, :, pl.ds(0, width)]
    here = rows.at[:, pl.ds(slot * width, width)]
    pltpu.make_async_copy(source, here, sem.at[slot]).wait()


def fold(rows, field):
    product = rows.astype(jnp.float32) * field
    return jnp.sum(product.reshape(-1, 8, product.shape[-1]), axis=0)


def late_kernel(freq, ids, cross, w5, w6, w7, block_re, block_im, total, *refs):
    row_refs, refs = refs[:10], refs[10:]
    sums, field_out, left, right, l_sem, w_sem, field, tot, sem, rows, row_sem = refs
    late = ids[7]
    step = pl.program_id(0)
    width, sources = w5.shape[2:]
    lanes = [slice(part * sources, (part + 1) * sources) for part in range(2)]

    def weights(ref, k):
        source = at_freq(ref, freq)
        return [
            pltpu.make_async_copy(
                source.at[part],
                right.at[k, pl.ds(0, width), pl.ds(part * sources, sources)],
                w_sem.at[k, part],
            )
            for part in range(2)
        ]

    def spread_lanes(k):
        right[k, width:, lanes[0]] = -right[k, :width, lanes[1]]
        right[k, width:, lanes[1]] = right[k, :width, lanes[0]]

    first = weights(w5, 0) + spectra_copies(freq, ids[0], cross, left.at[0], l_sem.at[0])
    six, seven = weights(w6, 1), weights(w7, 1)
    second = spectra_copies(freq, ids[1], cross, left.at[1], l_sem.at[1])
    third = [
        pltpu.make_async_copy(
            ref.at[min(k, ref.shape[0] - 1), half],
            left.at[2, pl.ds(half * width, width), pl.ds(k * width, width)],
            l_sem.at[2 + half, k],
        )
        for k, ref in enumerate((block_re, block_im))
        for half in range(2)
    ]
    total_copies = [
        pltpu.make_async_copy(
            total.at[part], tot.at[:, pl.ds(part * sources, sources)], sem.at[part]
        )
        for part in range(2)
    ]
    late_rows = pl.ds(pl.multiple_of(jnp.minimum(late, 1) * width, width), width)
    out_copies = [
        pltpu.make_async_copy(
            field.at[late_rows, pl.ds(part * sources, sources)], field_out.at[part], sem.at[2 + part]
        )
        for part in range(2)
    ]

    @pl.when(step == 0)
    def _():
        sums[...] = jnp.zeros_like(sums)
        for copy in first:
            copy.start()
        for copy in first:
            copy.wait()
        for copy in second:
            copy.start()

        @pl.when(ids[2] == 1)
        def _():
            for copy in seven:
                copy.start()

        @pl.when(ids[2] == 0)
        def _():
            for copy in six:
                copy.start()

        for copy in total_copies:
            copy.start()
        start_rows(freq, ids, 3, row_refs, rows.at[0], row_sem.at[0])
        spread_lanes(0)
        field[...] = dot(left[0], right[0])

    @pl.when(step == 1)
    def _():
        for copy in second + six:
            copy.wait()
        for copy in third:
            copy.start()
        start_rows(freq, ids, 5, row_refs, rows.at[1], row_sem.at[1])
        for copy in total_copies:
            copy.wait()
        spread_lanes(1)
        field[...] = field[...] + tot[...] + dot(left[1], right[1])
        for copy in out_copies:
            copy.start()
        for slot in range(2):
            wait_rows(freq, slot, row_refs, rows.at[0], row_sem.at[0])
        for slot in range(2):

            @pl.when(late != slot)
            def _(slot=slot):
                here = slice(slot * width, (slot + 1) * width)
                for part in range(2):
                    sums[...] += fold(rows[0, part, here], field[here, lanes[part]])

    @pl.when(step == 2)
    def _():
        for copy in third:
            copy.wait()
        for slot in range(2):
            wait_rows(freq, slot, row_refs, rows.at[1], row_sem.at[1])

        @pl.when(ids[2] == 1)
        def _():
            value = dot(left[2], right[0])
            for part in range(2):
                sums[...] += fold(rows[1, part], value[:, lanes[part]])

        for copy in out_copies:
            copy.wait()


def add_late(cross, freq, ids, pieces, blocks, total, row_refs):
    rows, (width, sources) = cross.shape[2], pieces[0].shape[2:]
    dtype = pieces[0].dtype
    return pl.pallas_call(
        functools.partial(late_kernel, freq),
        out_shape=(
            jax.ShapeDtypeStruct((8, sources), jnp.float32),
            jax.ShapeDtypeStruct((2, width, sources), jnp.float32),
        ),
        grid_spec=pltpu.PrefetchScalarGridSpec(
            num_scalar_prefetch=1,
            grid=(3,),
            in_specs=[ANYWHERE] * (7 + len(row_refs)),
            out_specs=(pl.BlockSpec((8, sources), lambda step, ids: (0, 0)), ANYWHERE),
            scratch_shapes=[
                pltpu.VMEM((3, rows, 2 * width), dtype),
                pltpu.VMEM((2, 2 * width, 2 * sources), dtype),
                pltpu.SemaphoreType.DMA((4, 2)),
                pltpu.SemaphoreType.DMA((2, 2)),
                pltpu.VMEM((rows, 2 * sources), jnp.float32),
                pltpu.VMEM((rows, 2 * sources), jnp.float32),
                pltpu.SemaphoreType.DMA((4,)),
                pltpu.VMEM((2, 2, rows, sources), dtype),
                pltpu.SemaphoreType.DMA((2, 2)),
            ],
        ),
        compiler_params=pltpu.CompilerParams(vmem_limit_bytes=LATE_LIMIT),
        cost_estimate=HINT,
    )(ids, cross, *pieces, *blocks, total, *row_refs)


def dot_kernel(ids, norms, *refs):
    groups, (out, rows, field, sem, total) = (refs[:6], refs[6:12]), refs[12:]
    for freq, (field_ref, _, *sources) in enumerate(groups):

        @pl.when(ids[0] < 4)
        def _(freq=freq, field_ref=field_ref):
            pltpu.make_async_copy(field_ref, field.at[freq], sem.at[0, freq]).start()

        for k, source in enumerate(sources):

            @pl.when(ids[0] == k)
            def _(freq=freq, source=source):
                pltpu.make_async_copy(source.at[0], rows.at[freq], sem.at[1, freq]).start()

    for freq, (field_ref, sums, *sources) in enumerate(groups):
        total[freq : freq + 1] = jnp.sum(sums[...], axis=0, keepdims=True)

        @pl.when(ids[0] < 4)
        def _(freq=freq, field_ref=field_ref, sources=sources):
            pltpu.make_async_copy(field_ref, field.at[freq], sem.at[0, freq]).wait()
            pltpu.make_async_copy(sources[0].at[0], rows.at[freq], sem.at[1, freq]).wait()
            more = sum(fold(rows[freq, part], field[freq, part]) for part in range(2))
            total[freq : freq + 1] += jnp.sum(more, axis=0, keepdims=True)

    total[2:4] = norms[...]
    for k in range(out.shape[0]):
        out[k] = total[...]


def dot_rows(ids, norms, groups):
    late_shape, dtype = groups[0][0].shape, groups[0][2].dtype
    sources = late_shape[-1]
    whole = lambda shape: pl.BlockSpec(shape, lambda i, ids: (0, 0))
    return pl.pallas_call(
        dot_kernel,
        out_shape=jax.ShapeDtypeStruct((copies_to_all(), 4, sources), jnp.float32),
        grid_spec=pltpu.PrefetchScalarGridSpec(
            num_scalar_prefetch=1,
            grid=(1,),
            in_specs=[whole((2, sources))] + [ANYWHERE, whole((8, sources)), *[ANYWHERE] * 4] * 2,
            out_specs=pl.BlockSpec((copies_to_all(), 4, sources), lambda i, ids: (0, 0, 0)),
            scratch_shapes=[
                pltpu.VMEM((2, *late_shape), dtype),
                pltpu.VMEM((2, *late_shape), jnp.float32),
                pltpu.SemaphoreType.DMA((2, 2)),
                pltpu.VMEM((4, sources), jnp.float32),
            ],
        ),
        compiler_params=pltpu.CompilerParams(vmem_limit_bytes=LATE_LIMIT),
        cost_estimate=HINT,
    )(ids, norms, *groups[0], *groups[1])


def copy_kernel(inputs, jobs, ids, *refs):
    refs, (stage, in_sem, out_sem) = refs[:-3], refs[-3:]
    sources, targets = refs[:inputs], refs[inputs:]
    writes = [
        pltpu.make_async_copy(stage.at[k], target(targets), out_sem.at[k])
        for k, (_, target) in enumerate(jobs)
    ]

    def each(act):
        for k, (options, _) in enumerate(jobs):
            for value, source in options:

                @pl.when(ids[0] == value)
                def _(k=k, source=source):
                    act(k, pltpu.make_async_copy(source(sources, ids), stage.at[k], in_sem.at[k]))

    def pass_on(k, copy):
        copy.wait()
        writes[k].start()

    def finish(k, copy):
        writes[k].wait()

    each(lambda k, copy: copy.start())
    each(pass_on)
    each(finish)


def copies(ids, args, jobs, shapes, unit, dtype, alias=None):
    return pl.pallas_call(
        functools.partial(copy_kernel, len(args), jobs),
        out_shape=[jax.ShapeDtypeStruct(shape, dtype) for shape in shapes],
        grid_spec=pltpu.PrefetchScalarGridSpec(
            num_scalar_prefetch=1,
            grid=(1,),
            in_specs=[ANYWHERE] * len(args),
            out_specs=[ANYWHERE] * len(shapes),
            scratch_shapes=[
                pltpu.VMEM((len(jobs), *unit), dtype),
                pltpu.SemaphoreType.DMA((len(jobs),)),
                pltpu.SemaphoreType.DMA((len(jobs),)),
            ],
        ),
        input_output_aliases={} if alias is None else {1 + alias: 0},
        compiler_params=pltpu.CompilerParams(vmem_limit_bytes=VMEM_LIMIT),
        cost_estimate=HINT,
    )(ids, *args)


def block_source(at, freq, part, half, width):
    def source(refs, ids):
        columns = pl.ds(pl.multiple_of(ids[1] * width, width), width)
        return refs[at].at[freq, part, pl.ds(half * width, width), columns]

    return source


def entry(at, *index):
    return lambda refs, ids=None: refs[at].at[index]


def fill_block(ids, piece, cross):
    _, _, width, sources = piece.shape
    jobs = [
        ([(0, block_source(1, 0, part, half, width))], entry(0, part, half))
        for part in range(2)
        for half in range(2)
    ]
    return copies(ids, [piece, cross], jobs, [piece.shape], (width, sources), piece.dtype, 0)[0]


def take_pair(ids, own, x, n, m):
    freqs, _, width, sources = own.shape
    jobs = [
        (
            [(0, entry(slot, freq, part)), (1, entry(2 + slot, freq, part))],
            entry(0, freq, part, pl.ds(slot * width, width)),
        )
        for freq in range(freqs)
        for part in range(2)
        for slot in range(2)
    ]
    shape = (freqs, 2, 2 * width, sources)
    return copies(ids, [own, x, n, m], jobs, [shape], (width, sources), own.dtype)[0]


def next_kernel(freq, ids, ends, middles, cross, over_x, over_z, stage, in_sem, out_sem):
    width = ends.shape[2]
    columns = pl.ds(pl.multiple_of(ids[1] * width, width), width)
    block = [cross.at[1, freq, pl.ds(half * width, width), columns] for half in range(2)]
    plans = [
        [(ends.at[freq, 0], 0), (ends.at[freq, 1], 1), (block[0], 2), (block[1], 3)],
        [(middles.at[freq, 0], 0), (middles.at[freq, 1], 1)],
    ]
    for mid, plan in enumerate(plans):

        @pl.when(ids[0] == mid)
        def _(mid=mid, plan=plan):
            reads = [
                pltpu.make_async_copy(source, stage.at[k], in_sem.at[k]) for source, k in plan
            ]
            writes = [
                [pltpu.make_async_copy(stage.at[k], over_x.at[0, k], out_sem.at[k])]
                if k < 2
                else [pltpu.make_async_copy(stage.at[k], over_z.at[0, k - 2], out_sem.at[k])]
                for _, k in plan
            ]
            if mid:
                for k in range(2):
                    writes[k].append(
                        pltpu.make_async_copy(stage.at[k], over_z.at[0, k], out_sem.at[2 + k])
                    )
            for copy in reads:
                copy.start()
            for read, group in zip(reads, writes):
                read.wait()
                for copy in group:
                    copy.start()
            for group in writes:
                for copy in group:
                    copy.wait()


def take_next(freq, ids, ends, middles, cross):
    _, _, width, sources = ends.shape
    shape = jax.ShapeDtypeStruct((1, 2, width, sources), ends.dtype)
    return pl.pallas_call(
        functools.partial(next_kernel, freq),
        out_shape=[shape, shape],
        grid_spec=pltpu.PrefetchScalarGridSpec(
            num_scalar_prefetch=1,
            grid=(1,),
            in_specs=[ANYWHERE] * 3,
            out_specs=[ANYWHERE] * 2,
            scratch_shapes=[
                pltpu.VMEM((4, width, sources), ends.dtype),
                pltpu.SemaphoreType.DMA((4,)),
                pltpu.SemaphoreType.DMA((4,)),
            ],
        ),
        compiler_params=pltpu.CompilerParams(vmem_limit_bytes=VMEM_LIMIT),
        cost_estimate=HINT,
    )(ids, ends, middles, cross)


def sums_by_swaps(cross, replicas, norms):
    rows, half = cross.shape[2], cross.shape[3]
    width = replicas.shape[3]
    me = lax.axis_index("row").astype(jnp.int32)
    col = lax.axis_index("col").astype(jnp.int32)
    holds = me * rows // half == col
    mid = ((me // 2) % 4 == 1) | ((me // 2) % 4 == 2)
    flag = lambda value: jnp.where(value, 1, 0).astype(jnp.int32).reshape(1)
    ids = lambda *wanted: me ^ jnp.array(wanted, jnp.int32)
    barrier = lambda *values: lax.optimization_barrier(values)

    slots = jnp.arange(2, dtype=jnp.int32)
    per_half = half // width
    own_masks = (2 * me % per_half + slots) ^ me
    next_masks = ((2 * (me ^ 2) % per_half + slots) ^ me) & 3
    table = lambda masks: sum(
        jnp.where(masks == mask, place, 0)
        for mask, place in enumerate((0, 1, 0, 2, 3, 5, 1, 4))
    ) + jnp.where(holds, 0, 6)
    late_slot = own_masks[0] & 1 ^ 1
    late_source = jnp.where(own_masks[0] & 2 != 0, 0, 1) + jnp.where(holds, 0, 2)
    ids_dot = jnp.where(mid, late_source, 4).astype(jnp.int32).reshape(1)
    late_ids = jnp.concatenate(
        [
            ids(5),
            jnp.where(mid, ids(7), ids(6)),
            flag(mid),
            table(own_masks),
            table(next_masks),
            jnp.where(mid, late_slot, 2).reshape(1),
        ]
    ).astype(jnp.int32)
    pair = flag(((me >> 1) ^ me) & 1 != 0)
    ids_a = jnp.concatenate([ids(1, 2, 6), flag(mid)])
    ids_z = jnp.concatenate([flag(mid), ids(7)])
    numbers = [ids_a, ids(3, 4), ids_z, late_ids, pair, ids_dot]

    own = replicas[:, :, 0]
    x = swap(own, "row", 1)
    n = swap(own, "row", 2)
    m = swap_middle(own)
    a0 = add_field(cross, 0, ids(0), [own])
    a1 = add_field(cross, 1, ids(0), [own])
    m = fill_block(ids_z, m, cross)
    x, n, m, a0, a1, norms, *numbers = barrier(x, n, m, a0, a1, norms, *numbers)
    ids_a, ids_b, ids_z, late_ids, pair, ids_dot = numbers

    z = swap(m, "row", 2)
    m2 = swap_middle(n)
    xn = swap(n, "row", 1)
    a0 = add_field(cross, 0, ids_a, [x, n, m], a0, gated=True)
    a1 = add_field(cross, 1, ids_a, [x, n, m], a1, gated=True)
    mine = take_pair(pair, own, x, n, m)
    x_a, x_b = x[0:1], x[1:2]
    z, m2, xn, a0, a1, mine, x_a, x_b = barrier(z, m2, xn, a0, a1, mine, x_a, x_b)

    w4_a, send_a = take_next(0, ids_z, z, m2, cross)
    x5_a = swap(w4_a, "row", 1)
    z_a = swap(send_a, "row", 2)
    w7_a = swap_middle(after(x_a, w4_a))
    other = swap(mine, "col", 1)
    b0 = add_field(cross, 0, ids_b, [xn, w4_a], a0)
    w4_b, send_b = take_next(1, after(ids_z, b0), z, m2, cross)
    b1 = add_field(cross, 1, ids_b, [xn, w4_b], a1)
    x5_a, z_a, w7_a, other, b0, w4_b, send_b, x_b, xn, m2 = barrier(
        x5_a, z_a, w7_a, other, b0, w4_b, send_b, x_b, xn, m2
    )

    x5_b = swap(w4_b, "row", 1)
    z_b = swap(send_b, "row", 2)
    w7_b = swap_middle(x_b)
    other_xn = swap(xn, "col", 1)
    other_m2 = swap(m2, "col", 1)
    early = [mine, xn, m2, xn, xn, other, other_xn, other_m2, other_xn, other_xn]
    sums_a, field_a = add_late(cross, 0, late_ids, [x5_a, z_a, w7_a], [z, z], b0, early)
    x5_b, z_b, w7_b, sums_a, field_a, b1, other_xn, other_m2, x5_a, w7_a = barrier(
        x5_b, z_b, w7_b, sums_a, field_a, b1, other_xn, other_m2, x5_a, w7_a
    )

    late = [w7_a, x5_a, w7_b, x5_b]
    others = [swap(piece, "col", 1) for piece in late]
    early = [mine, xn, m2, xn, xn, other, other_xn, other_m2, other_xn, other_xn]
    sums_b, field_b = add_late(cross, 1, late_ids, [x5_b, z_b, w7_b], [z_a, z_b], b1, early)
    groups = [
        (field_a, sums_a, *late[:2], *others[:2]),
        (field_b, sums_b, *late[2:], *others[2:]),
    ]
    return dot_rows(ids_dot, norms, groups)


def sums_by_gather(cross, replicas, norms):
    rows, half = cross.shape[2], cross.shape[3]
    row_index, col_index = lax.axis_index("row"), lax.axis_index("col")
    first_row = row_index * rows
    holder = first_row // half
    whole = lax.all_gather(replicas, "row", axis=3, tiled=True)[:, :, 0]
    parts = jnp.einsum("fark,fbks->fabrs", cross, whole, preferred_element_type=jnp.float32)
    field = jnp.stack([parts[:, 0, 0] - parts[:, 1, 1], parts[:, 0, 1] + parts[:, 1, 0]], axis=1)
    own_rows = lax.dynamic_slice_in_dim(whole, first_row - holder * half, rows, 2)
    block_rows = jnp.where(holder == col_index, own_rows, swap(own_rows, "col", 1))
    numer = jnp.sum(block_rows.astype(jnp.float32) * field, axis=(1, 2))
    sums = jnp.concatenate([numer, norms])
    return jnp.broadcast_to(sums[None], (copies_to_all(), *sums.shape))


def body(cross_spectra, replicas, tile_order):
    fnum = cross_spectra.shape[0]
    sources = replicas.shape[4]
    own = replicas[:, :, 0].astype(jnp.float32)
    norms = jnp.sum(own * own, axis=(1, 2))
    doubling = (
        lax.axis_size("row") == 8
        and fnum == 2
        and replicas.shape[3] % 128 == 0
        and cross_spectra.shape[2] == 2 * replicas.shape[3]
    )
    sums = (sums_by_swaps if doubling else sums_by_gather)(cross_spectra, replicas, norms)
    sums = sum_all(sums)
    numer, norms = sums[:fnum], sums[fnum:]
    beam = numer / (norms + 1e-06)
    width = sources // lax.axis_size("col")
    beam_half = lax.dynamic_slice_in_dim(beam, lax.axis_index("col") * width, width, 1)
    peak = jnp.max(jnp.abs(beam), axis=1) + 1e-06
    count = tile_order.shape[0]
    picker = (tile_order[:, None] == jnp.arange(count, dtype=jnp.int32)[None, :]).astype(jnp.float32)
    tiles = beam.reshape(fnum, count, sources // count)
    refined = (
        jnp.einsum("tu,fup->ftp", picker, tiles, precision=lax.Precision.HIGHEST)
        / peak[:, None, None]
    )
    return (beam_half, refined)


def solution(mesh):
    in_specs = (P("groups", None, "row", "col"), P("groups", None, "col", "row", None), P("groups"))
    out_specs = (P("groups", "col"), P("groups", None, None))
    return jax.shard_map(body, mesh=mesh, in_specs=in_specs, out_specs=out_specs, check_vma=False)
```

```python
import functools
import math

import jax
import jax.numpy as jnp
from jax import lax
from jax.experimental import pallas as pl
from jax.experimental.pallas import tpu as pltpu
from jax.sharding import PartitionSpec as P

VMEM_LIMIT = 63 * 1024 * 1024
LATE_LIMIT = 30 * 1024 * 1024
MIDDLE_LIMIT = 44 * 1024 * 1024
HINT = pl.CostEstimate(flops=1, bytes_accessed=1, transcendentals=0)
ANYWHERE = pl.BlockSpec(memory_space=pl.ANY)


def swap(value, axis, mask):
    size = math.prod(lax.axis_size(name) for name in (axis if isinstance(axis, tuple) else (axis,)))
    return lax.ppermute(value, axis, [(source, source ^ mask) for source in range(size)])


def swap_middle(value):
    axes = ("row", "col")
    size = lax.axis_size("row") * lax.axis_size("col")
    target = lambda k: k ^ 12 if (k // 4) % 4 in (1, 2) else k ^ 1
    return lax.ppermute(value, axes, [(k, target(k)) for k in range(size)])


def after(value, *others):
    return lax.optimization_barrier((value, *others))[0]


def copies_to_all():
    size = lax.axis_size("row") * lax.axis_size("col")
    return size if size <= 16 else 1


def sum_all(copies):
    axes = ("row", "col")
    if copies.shape[0] == 1:
        return lax.psum(copies[0], axes)
    return jnp.sum(lax.all_to_all(copies, axes, 0, 0, tiled=True), axis=0)


def dot(a, b):
    return jnp.dot(a, b, preferred_element_type=jnp.float32)


def at_freq(ref, freq):
    return ref.at[freq if ref.shape[0] > 1 else 0]


def weight_copies(freq, ref, right, sem):
    low = pl.ds(0, ref.shape[2])
    source = at_freq(ref, freq)
    return [
        pltpu.make_async_copy(source.at[0], right.at[0, low], sem.at[0]),
        pltpu.make_async_copy(source.at[1], right.at[1, low], sem.at[1]),
    ]


def spread(right):
    width = right.shape[1] // 2
    right[0, width:] = -right[1, :width]
    right[1, width:] = right[0, :width]


def spectra_copies(freq, column, cross, left, sem):
    width = left.shape[1] // 2
    columns = pl.ds(pl.multiple_of(column * width, width), width)
    return [
        pltpu.make_async_copy(
            cross.at[freq, part, :, columns], left.at[:, pl.ds(part * width, width)], sem.at[part]
        )
        for part in range(2)
    ]


def field_kernel(freq, count, has_total, gated, ids, cross, *refs):
    w_refs, refs = refs[:count], refs[count:]
    total, refs = (refs[0], refs[1:]) if has_total else (None, refs)
    out, left, right, l_sem, w_sem, field, tot, tot_sem = refs
    piece, part = pl.program_id(0), pl.program_id(1)
    copies = [
        weight_copies(freq, ref, right.at[k], w_sem.at[k])
        + spectra_copies(freq, ids[k], cross, left.at[k], l_sem.at[k])
        for k, ref in enumerate(w_refs)
    ]
    for k, group in enumerate(copies):

        @pl.when((piece == k) & (part == 0))
        def _(k=k, group=group):
            if k == 0:
                for copy in group:
                    copy.start()
            for copy in group:
                copy.wait()
            if k + 1 < count:
                for copy in copies[k + 1]:
                    copy.start()
            if k == 0 and has_total:
                pltpu.make_async_copy(total, tot, tot_sem.at[0]).start()
            spread(right.at[k])

    last = piece == count - 1
    if count > 1:

        @pl.when(piece == 0)
        def _():
            field[part] = dot(left[piece], right[piece, part])

        @pl.when((piece > 0) & (piece < count - 1))
        def _():
            field[part] += dot(left[piece], right[piece, part])

    @pl.when(last)
    def _():
        value = dot(left[piece], right[piece, part])
        if gated:
            value = jnp.where(ids[count] == 1, value, 0.0)
        if count > 1:
            value += field[part]
        if has_total:

            @pl.when(part == 0)
            def _():
                pltpu.make_async_copy(total, tot, tot_sem.at[0]).wait()

            value += tot[part]
        out[0] = value


def add_field(cross, freq, ids, pieces, total=None, gated=False):
    rows, (width, sources) = cross.shape[2], pieces[0].shape[2:]
    count, dtype = len(pieces), pieces[0].dtype
    has_total = total is not None
    return pl.pallas_call(
        functools.partial(field_kernel, freq, count, has_total, gated),
        out_shape=jax.ShapeDtypeStruct((2, rows, sources), jnp.float32),
        grid_spec=pltpu.PrefetchScalarGridSpec(
            num_scalar_prefetch=1,
            grid=(count, 2),
            in_specs=[ANYWHERE] * (1 + count + has_total),
            out_specs=pl.BlockSpec(
                (1, rows, sources), lambda p, part, ids: (jnp.where(p == count - 1, part, 0), 0, 0)
            ),
            scratch_shapes=[
                pltpu.VMEM((count, rows, 2 * width), dtype),
                pltpu.VMEM((count, 2, 2 * width, sources), dtype),
                pltpu.SemaphoreType.DMA((count, 2)),
                pltpu.SemaphoreType.DMA((count, 2)),
                pltpu.VMEM((2, rows, sources), jnp.float32),
                pltpu.VMEM((2, rows, sources), jnp.float32),
                pltpu.SemaphoreType.DMA((1,)),
            ],
        ),
        compiler_params=pltpu.CompilerParams(vmem_limit_bytes=VMEM_LIMIT),
        cost_estimate=HINT,
    )(ids, cross, *pieces, *([total] if has_total else []))


def start_rows(freq, ids, base, refs, rows, sem):
    width = rows.shape[1] // 2
    views = []
    for picked, *pieces in (refs[:5], refs[5:]):
        views += [picked.at[freq, :, pl.ds(slot * width, width)] for slot in range(2)]
        views += [at_freq(ref, freq) for ref in pieces]
    for slot in range(2):
        here = pl.ds(slot * width, width)
        for k, source in enumerate(views):

            @pl.when(ids[base + slot] == k)
            def _(source=source, slot=slot, here=here):
                pltpu.make_async_copy(source, rows.at[:, here], sem.at[slot]).start()


def wait_rows(freq, slot, refs, rows, sem):
    width = rows.shape[1] // 2
    source = refs[0].at[freq, :, pl.ds(0, width)]
    here = rows.at[:, pl.ds(slot * width, width)]
    pltpu.make_async_copy(source, here, sem.at[slot]).wait()


def fold(rows, field):
    product = rows.astype(jnp.float32) * field
    return jnp.sum(product.reshape(-1, 8, product.shape[-1]), axis=0)


def late_kernel(freq, ids, cross, w5, w6, w7, block_re, block_im, total, *refs):
    row_refs, refs = refs[:10], refs[10:]
    sums, field_out, left, right, l_sem, w_sem, field, tot, sem, rows, row_sem = refs
    late = ids[7]
    step = pl.program_id(0)
    width, sources = w5.shape[2:]
    lanes = [slice(part * sources, (part + 1) * sources) for part in range(2)]

    def weights(ref, k):
        source = at_freq(ref, freq)
        return [
            pltpu.make_async_copy(
                source.at[part],
                right.at[k, pl.ds(0, width), pl.ds(part * sources, sources)],
                w_sem.at[k, part],
            )
            for part in range(2)
        ]

    def spread_lanes(k):
        right[k, width:, lanes[0]] = -right[k, :width, lanes[1]]
        right[k, width:, lanes[1]] = right[k, :width, lanes[0]]

    first = weights(w5, 0) + spectra_copies(freq, ids[0], cross, left.at[0], l_sem.at[0])
    six, seven = weights(w6, 1), weights(w7, 1)
    second = spectra_copies(freq, ids[1], cross, left.at[1], l_sem.at[1])
    third = [
        pltpu.make_async_copy(
            ref.at[min(k, ref.shape[0] - 1), half],
            left.at[2, pl.ds(half * width, width), pl.ds(k * width, width)],
            l_sem.at[2 + half, k],
        )
        for k, ref in enumerate((block_re, block_im))
        for half in range(2)
    ]
    total_copies = [
        pltpu.make_async_copy(
            total.at[part], tot.at[:, pl.ds(part * sources, sources)], sem.at[part]
        )
        for part in range(2)
    ]
    late_rows = pl.ds(pl.multiple_of(jnp.minimum(late, 1) * width, width), width)
    out_copies = [
        pltpu.make_async_copy(
            field.at[late_rows, pl.ds(part * sources, sources)], field_out.at[part], sem.at[2 + part]
        )
        for part in range(2)
    ]

    @pl.when(step == 0)
    def _():
        sums[...] = jnp.zeros_like(sums)
        for copy in first:
            copy.start()
        for copy in first:
            copy.wait()
        for copy in second:
            copy.start()

        @pl.when(ids[2] == 1)
        def _():
            for copy in seven:
                copy.start()

        @pl.when(ids[2] == 0)
        def _():
            for copy in six:
                copy.start()

        for copy in total_copies:
            copy.start()
        start_rows(freq, ids, 3, row_refs, rows.at[0], row_sem.at[0])
        spread_lanes(0)
        field[...] = dot(left[0], right[0])

    @pl.when(step == 1)
    def _():
        for copy in second + six:
            copy.wait()
        for copy in third:
            copy.start()
        start_rows(freq, ids, 5, row_refs, rows.at[1], row_sem.at[1])
        for copy in total_copies:
            copy.wait()
        spread_lanes(1)
        field[...] = field[...] + tot[...] + dot(left[1], right[1])
        for copy in out_copies:
            copy.start()
        for slot in range(2):
            wait_rows(freq, slot, row_refs, rows.at[0], row_sem.at[0])
        for slot in range(2):

            @pl.when(late != slot)
            def _(slot=slot):
                here = slice(slot * width, (slot + 1) * width)
                for part in range(2):
                    sums[...] += fold(rows[0, part, here], field[here, lanes[part]])

    @pl.when(step == 2)
    def _():
        for copy in third:
            copy.wait()
        for slot in range(2):
            wait_rows(freq, slot, row_refs, rows.at[1], row_sem.at[1])

        @pl.when(ids[2] == 1)
        def _():
            value = dot(left[2], right[0])
            for part in range(2):
                sums[...] += fold(rows[1, part], value[:, lanes[part]])

        for copy in out_copies:
            copy.wait()


def add_late(cross, freq, ids, pieces, blocks, total, row_refs, limit):
    rows, (width, sources) = cross.shape[2], pieces[0].shape[2:]
    dtype = pieces[0].dtype
    return pl.pallas_call(
        functools.partial(late_kernel, freq),
        out_shape=(
            jax.ShapeDtypeStruct((8, sources), jnp.float32),
            jax.ShapeDtypeStruct((2, width, sources), jnp.float32),
        ),
        grid_spec=pltpu.PrefetchScalarGridSpec(
            num_scalar_prefetch=1,
            grid=(3,),
            in_specs=[ANYWHERE] * (7 + len(row_refs)),
            out_specs=(pl.BlockSpec((8, sources), lambda step, ids: (0, 0)), ANYWHERE),
            scratch_shapes=[
                pltpu.VMEM((3, rows, 2 * width), dtype),
                pltpu.VMEM((2, 2 * width, 2 * sources), dtype),
                pltpu.SemaphoreType.DMA((4, 2)),
                pltpu.SemaphoreType.DMA((2, 2)),
                pltpu.VMEM((rows, 2 * sources), jnp.float32),
                pltpu.VMEM((rows, 2 * sources), jnp.float32),
                pltpu.SemaphoreType.DMA((4,)),
                pltpu.VMEM((2, 2, rows, sources), dtype),
                pltpu.SemaphoreType.DMA((2, 2)),
            ],
        ),
        compiler_params=pltpu.CompilerParams(vmem_limit_bytes=limit),
        cost_estimate=HINT,
    )(ids, cross, *pieces, *blocks, total, *row_refs)


def dot_kernel(ids, norms, *refs):
    groups, (out, rows, field, sem, total) = (refs[:6], refs[6:12]), refs[12:]
    for freq, (field_ref, _, *sources) in enumerate(groups):

        @pl.when(ids[0] < 4)
        def _(freq=freq, field_ref=field_ref):
            pltpu.make_async_copy(field_ref, field.at[freq], sem.at[0, freq]).start()

        for k, source in enumerate(sources):

            @pl.when(ids[0] == k)
            def _(freq=freq, source=source):
                pltpu.make_async_copy(source.at[0], rows.at[freq], sem.at[1, freq]).start()

    for freq, (field_ref, sums, *sources) in enumerate(groups):
        total[freq : freq + 1] = jnp.sum(sums[...], axis=0, keepdims=True)

        @pl.when(ids[0] < 4)
        def _(freq=freq, field_ref=field_ref, sources=sources):
            pltpu.make_async_copy(field_ref, field.at[freq], sem.at[0, freq]).wait()
            pltpu.make_async_copy(sources[0].at[0], rows.at[freq], sem.at[1, freq]).wait()
            more = sum(fold(rows[freq, part], field[freq, part]) for part in range(2))
            total[freq : freq + 1] += jnp.sum(more, axis=0, keepdims=True)

    total[2:4] = norms[...]
    for k in range(out.shape[0]):
        out[k] = total[...]


def dot_rows(ids, norms, groups):
    late_shape, dtype = groups[0][0].shape, groups[0][2].dtype
    sources = late_shape[-1]
    whole = lambda shape: pl.BlockSpec(shape, lambda i, ids: (0, 0))
    return pl.pallas_call(
        dot_kernel,
        out_shape=jax.ShapeDtypeStruct((copies_to_all(), 4, sources), jnp.float32),
        grid_spec=pltpu.PrefetchScalarGridSpec(
            num_scalar_prefetch=1,
            grid=(1,),
            in_specs=[whole((2, sources))] + [ANYWHERE, whole((8, sources)), *[ANYWHERE] * 4] * 2,
            out_specs=pl.BlockSpec((copies_to_all(), 4, sources), lambda i, ids: (0, 0, 0)),
            scratch_shapes=[
                pltpu.VMEM((2, *late_shape), dtype),
                pltpu.VMEM((2, *late_shape), jnp.float32),
                pltpu.SemaphoreType.DMA((2, 2)),
                pltpu.VMEM((4, sources), jnp.float32),
            ],
        ),
        compiler_params=pltpu.CompilerParams(vmem_limit_bytes=LATE_LIMIT),
        cost_estimate=HINT,
    )(ids, norms, *groups[0], *groups[1])


def copy_kernel(inputs, jobs, ids, *refs):
    refs, (stage, in_sem, out_sem) = refs[:-3], refs[-3:]
    sources, targets = refs[:inputs], refs[inputs:]
    writes = [
        pltpu.make_async_copy(stage.at[k], target(targets), out_sem.at[k])
        for k, (_, target) in enumerate(jobs)
    ]

    def each(act):
        for k, (options, _) in enumerate(jobs):
            for value, source in options:

                @pl.when(ids[0] == value)
                def _(k=k, source=source):
                    act(k, pltpu.make_async_copy(source(sources, ids), stage.at[k], in_sem.at[k]))

    def pass_on(k, copy):
        copy.wait()
        writes[k].start()

    def finish(k, copy):
        writes[k].wait()

    each(lambda k, copy: copy.start())
    each(pass_on)
    each(finish)


def copies(ids, args, jobs, shapes, unit, dtype, alias=None):
    return pl.pallas_call(
        functools.partial(copy_kernel, len(args), jobs),
        out_shape=[jax.ShapeDtypeStruct(shape, dtype) for shape in shapes],
        grid_spec=pltpu.PrefetchScalarGridSpec(
            num_scalar_prefetch=1,
            grid=(1,),
            in_specs=[ANYWHERE] * len(args),
            out_specs=[ANYWHERE] * len(shapes),
            scratch_shapes=[
                pltpu.VMEM((len(jobs), *unit), dtype),
                pltpu.SemaphoreType.DMA((len(jobs),)),
                pltpu.SemaphoreType.DMA((len(jobs),)),
            ],
        ),
        input_output_aliases={} if alias is None else {1 + alias: 0},
        compiler_params=pltpu.CompilerParams(vmem_limit_bytes=VMEM_LIMIT),
        cost_estimate=HINT,
    )(ids, *args)


def block_source(at, freq, part, half, width):
    def source(refs, ids):
        columns = pl.ds(pl.multiple_of(ids[1] * width, width), width)
        return refs[at].at[freq, part, pl.ds(half * width, width), columns]

    return source


def entry(at, *index):
    return lambda refs, ids=None: refs[at].at[index]


def fill_block(ids, piece, cross):
    _, _, width, sources = piece.shape
    jobs = [
        ([(0, block_source(1, 0, part, half, width))], entry(0, part, half))
        for part in range(2)
        for half in range(2)
    ]
    return copies(ids, [piece, cross], jobs, [piece.shape], (width, sources), piece.dtype, 0)[0]


def take_pair(ids, own, x, n, m):
    freqs, _, width, sources = own.shape
    jobs = [
        (
            [(0, entry(slot, freq, part)), (1, entry(2 + slot, freq, part))],
            entry(0, freq, part, pl.ds(slot * width, width)),
        )
        for freq in range(freqs)
        for part in range(2)
        for slot in range(2)
    ]
    shape = (freqs, 2, 2 * width, sources)
    return copies(ids, [own, x, n, m], jobs, [shape], (width, sources), own.dtype)[0]


def next_kernel(freq, ids, ends, middles, cross, over_x, over_z, stage, in_sem, out_sem):
    width = ends.shape[2]
    columns = pl.ds(pl.multiple_of(ids[1] * width, width), width)
    block = [cross.at[1, freq, pl.ds(half * width, width), columns] for half in range(2)]
    plans = [
        [(ends.at[freq, 0], 0), (ends.at[freq, 1], 1), (block[0], 2), (block[1], 3)],
        [(middles.at[freq, 0], 0), (middles.at[freq, 1], 1)],
    ]
    for mid, plan in enumerate(plans):

        @pl.when(ids[0] == mid)
        def _(mid=mid, plan=plan):
            reads = [
                pltpu.make_async_copy(source, stage.at[k], in_sem.at[k]) for source, k in plan
            ]
            writes = [
                [pltpu.make_async_copy(stage.at[k], over_x.at[0, k], out_sem.at[k])]
                if k < 2
                else [pltpu.make_async_copy(stage.at[k], over_z.at[0, k - 2], out_sem.at[k])]
                for _, k in plan
            ]
            if mid:
                for k in range(2):
                    writes[k].append(
                        pltpu.make_async_copy(stage.at[k], over_z.at[0, k], out_sem.at[2 + k])
                    )
            for copy in reads:
                copy.start()
            for read, group in zip(reads, writes):
                read.wait()
                for copy in group:
                    copy.start()
            for group in writes:
                for copy in group:
                    copy.wait()


def take_next(freq, ids, ends, middles, cross):
    _, _, width, sources = ends.shape
    shape = jax.ShapeDtypeStruct((1, 2, width, sources), ends.dtype)
    return pl.pallas_call(
        functools.partial(next_kernel, freq),
        out_shape=[shape, shape],
        grid_spec=pltpu.PrefetchScalarGridSpec(
            num_scalar_prefetch=1,
            grid=(1,),
            in_specs=[ANYWHERE] * 3,
            out_specs=[ANYWHERE] * 2,
            scratch_shapes=[
                pltpu.VMEM((4, width, sources), ends.dtype),
                pltpu.SemaphoreType.DMA((4,)),
                pltpu.SemaphoreType.DMA((4,)),
            ],
        ),
        compiler_params=pltpu.CompilerParams(vmem_limit_bytes=VMEM_LIMIT),
        cost_estimate=HINT,
    )(ids, ends, middles, cross)


def sums_by_swaps(cross, replicas, norms):
    rows, half = cross.shape[2], cross.shape[3]
    width = replicas.shape[3]
    me = lax.axis_index("row").astype(jnp.int32)
    col = lax.axis_index("col").astype(jnp.int32)
    holds = me * rows // half == col
    mid = ((me // 2) % 4 == 1) | ((me // 2) % 4 == 2)
    flag = lambda value: jnp.where(value, 1, 0).astype(jnp.int32).reshape(1)
    ids = lambda *wanted: me ^ jnp.array(wanted, jnp.int32)
    barrier = lambda *values: lax.optimization_barrier(values)

    slots = jnp.arange(2, dtype=jnp.int32)
    per_half = half // width
    own_masks = (2 * me % per_half + slots) ^ me
    next_masks = ((2 * (me ^ 2) % per_half + slots) ^ me) & 3
    table = lambda masks: sum(
        jnp.where(masks == mask, place, 0)
        for mask, place in enumerate((0, 1, 0, 2, 3, 5, 1, 4))
    ) + jnp.where(holds, 0, 6)
    late_slot = own_masks[0] & 1 ^ 1
    late_source = jnp.where(own_masks[0] & 2 != 0, 0, 1) + jnp.where(holds, 0, 2)
    ids_dot = jnp.where(mid, late_source, 4).astype(jnp.int32).reshape(1)
    late_ids = jnp.concatenate(
        [
            ids(5),
            jnp.where(mid, ids(7), ids(6)),
            flag(mid),
            table(own_masks),
            table(next_masks),
            jnp.where(mid, late_slot, 2).reshape(1),
        ]
    ).astype(jnp.int32)
    pair = flag(((me >> 1) ^ me) & 1 != 0)
    ids_a = jnp.concatenate([ids(1, 2, 6), flag(mid)])
    ids_z = jnp.concatenate([flag(mid), ids(7)])
    numbers = [ids_a, ids(3, 4), ids_z, late_ids, pair, ids_dot]

    own = replicas[:, :, 0]
    x = swap(own, "row", 1)
    n = swap(own, "row", 2)
    m = swap_middle(own)
    a0 = add_field(cross, 0, ids(0), [own])
    a1 = add_field(cross, 1, ids(0), [own])
    m = fill_block(ids_z, m, cross)
    x, n, m, a0, a1, norms, *numbers = barrier(x, n, m, a0, a1, norms, *numbers)
    ids_a, ids_b, ids_z, late_ids, pair, ids_dot = numbers

    z = swap(m, "row", 2)
    m2 = swap_middle(n)
    xn = swap(n, "row", 1)
    a0 = add_field(cross, 0, ids_a, [x, n, m], a0, gated=True)
    a1 = add_field(cross, 1, ids_a, [x, n, m], a1, gated=True)
    mine = take_pair(pair, own, x, n, m)
    x_a, x_b = x[0:1], x[1:2]
    z, m2, xn, a0, a1, mine, x_a, x_b = barrier(z, m2, xn, a0, a1, mine, x_a, x_b)

    w4_a, send_a = take_next(0, ids_z, z, m2, cross)
    x5_a = swap(w4_a, "row", 1)
    z_a = swap(send_a, "row", 2)
    w7_a = swap_middle(after(x_a, w4_a))
    other = swap(mine, "col", 1)
    b0 = add_field(cross, 0, ids_b, [xn, w4_a], a0)
    w4_b, send_b = take_next(1, after(ids_z, b0), z, m2, cross)
    b1 = add_field(cross, 1, ids_b, [xn, w4_b], a1)
    x5_a, z_a, w7_a, other, b0, w4_b, send_b, x_b, xn, m2 = barrier(
        x5_a, z_a, w7_a, other, b0, w4_b, send_b, x_b, xn, m2
    )

    x5_b = swap(w4_b, "row", 1)
    z_b = swap(send_b, "row", 2)
    w7_b = swap_middle(x_b)
    other_xn = swap(xn, "col", 1)
    other_m2 = swap(m2, "col", 1)
    early = [mine, xn, m2, xn, xn, other, other_xn, other_m2, other_xn, other_xn]
    sums_a, field_a = add_late(cross, 0, late_ids, [x5_a, z_a, w7_a], [z, z], b0, early, MIDDLE_LIMIT)
    x5_b, z_b, w7_b, sums_a, field_a, b1, other_xn, other_m2, x5_a, w7_a = barrier(
        x5_b, z_b, w7_b, sums_a, field_a, b1, other_xn, other_m2, x5_a, w7_a
    )

    late = [w7_a, x5_a, w7_b, x5_b]
    others = [swap(piece, "col", 1) for piece in late]
    early = [mine, xn, m2, xn, xn, other, other_xn, other_m2, other_xn, other_xn]
    sums_b, field_b = add_late(cross, 1, late_ids, [x5_b, z_b, w7_b], [z_a, z_b], b1, early, LATE_LIMIT)
    groups = [
        (field_a, sums_a, *late[:2], *others[:2]),
        (field_b, sums_b, *late[2:], *others[2:]),
    ]
    return dot_rows(ids_dot, norms, groups)


def sums_by_gather(cross, replicas, norms):
    rows, half = cross.shape[2], cross.shape[3]
    row_index, col_index = lax.axis_index("row"), lax.axis_index("col")
    first_row = row_index * rows
    holder = first_row // half
    whole = lax.all_gather(replicas, "row", axis=3, tiled=True)[:, :, 0]
    parts = jnp.einsum("fark,fbks->fabrs", cross, whole, preferred_element_type=jnp.float32)
    field = jnp.stack([parts[:, 0, 0] - parts[:, 1, 1], parts[:, 0, 1] + parts[:, 1, 0]], axis=1)
    own_rows = lax.dynamic_slice_in_dim(whole, first_row - holder * half, rows, 2)
    block_rows = jnp.where(holder == col_index, own_rows, swap(own_rows, "col", 1))
    numer = jnp.sum(block_rows.astype(jnp.float32) * field, axis=(1, 2))
    sums = jnp.concatenate([numer, norms])
    return jnp.broadcast_to(sums[None], (copies_to_all(), *sums.shape))


def body(cross_spectra, replicas, tile_order):
    fnum = cross_spectra.shape[0]
    sources = replicas.shape[4]
    own = replicas[:, :, 0].astype(jnp.float32)
    norms = jnp.sum(own * own, axis=(1, 2))
    doubling = (
        lax.axis_size("row") == 8
        and fnum == 2
        and replicas.shape[3] % 128 == 0
        and cross_spectra.shape[2] == 2 * replicas.shape[3]
    )
    sums = (sums_by_swaps if doubling else sums_by_gather)(cross_spectra, replicas, norms)
    sums = sum_all(sums)
    numer, norms = sums[:fnum], sums[fnum:]
    beam = numer / (norms + 1e-06)
    width = sources // lax.axis_size("col")
    beam_half = lax.dynamic_slice_in_dim(beam, lax.axis_index("col") * width, width, 1)
    peak = jnp.max(jnp.abs(beam), axis=1) + 1e-06
    count = tile_order.shape[0]
    picker = (tile_order[:, None] == jnp.arange(count, dtype=jnp.int32)[None, :]).astype(jnp.float32)
    tiles = beam.reshape(fnum, count, sources // count)
    refined = (
        jnp.einsum("tu,fup->ftp", picker, tiles, precision=lax.Precision.HIGHEST)
        / peak[:, None, None]
    )
    return (beam_half, refined)


def solution(mesh):
    in_specs = (P("groups", None, "row", "col"), P("groups", None, "col", "row", None), P("groups"))
    out_specs = (P("groups", "col"), P("groups", None, None))
    return jax.shard_map(body, mesh=mesh, in_specs=in_specs, out_specs=out_specs, check_vma=False)
```
